32 devices in a mesh: tensor: 16 (over z, x, core), rep: 2 (over y).
Axes of the slice: x: 2, y: 2, z: 4, core: 2. Of those that a mesh axis runs over, the one named last changes fastest.
Arguments:
- amplitudes: float32 [8, 16384, 1024], P('rep', 'tensor'), may hold values from -6 to 6
- integrals: float32 [1024, 8, 16384], P(None, 'rep', 'tensor'), may hold values from -0.078125 to 0.078125
- row_count: int32 [8], replicated, may hold values from 1 to 1024, 6400 in all
- pair_count: int32 [8], replicated, may hold values from 1 to 16384, 80000 in all
- col_count: int32 [8], replicated, may hold values from 1 to 1024, 6400 in all
Outputs:
- cycle_term: float32 [1024, 8, 1024], P('tensor', None, 'rep')
The draws below stay inside these ranges and needn't reach their ends.
Inputs may be any that keep to these rules, and one draw needn't show every extreme that they name: row_count[h] is the number of (i, a) pairs with irrep product h for 8 occupied i; the counts sum to 6400 and one equals 1024. pair_count[h] is the number of (k, c) pairs with irrep product h; the counts sum to 80000 and one equals 16384. col_count[h] is the number of (j, b) pairs with irrep product h for 8 occupied j; the counts sum to 6400 and one equals 1024.
All inputs are finite; a program needn't handle non-finite values.
Results may differ from the reference program's by a relative error of at most 0.0003.
Values sent between devices are 32-bit elements; how exact they have to be, the bound alone decides.
No kernel may reach another device: no remote copies, remote signals or barrier semaphores. Data moves between devices by JAX's collectives and lax.ppermute only.
A program may use at most 128 MiB of HBM per device.

```python
import math
import jax
import jax.numpy as jnp
import numpy as np
from jax import lax

NH = 8
NO = 100
NV = 800
PAIR_CAP = 16384
I_WIN = 8
J_WIN = 8
ROW_CAP = 1024
COL_CAP = 1024


def raised(array, rng, source, target, parts, factor):
    owner, partner = [(jnp.arange(array.shape[axis_at]) // (array.shape[axis_at] // parts)).reshape([-1 if axis == axis_at else 1 for axis in range(array.ndim)]) for axis_at in (source, target)]
    chosen = jax.random.permutation(rng, parts)[partner]
    strong = (owner == chosen) | (owner == (partner + parts // 2) % parts)
    return jnp.where(strong, factor * array, array)


def steps_of(rng, dims, cuts, least, high):
    level, own = 1.0, jax.random.fold_in(rng, 6)
    for dim, parts in cuts:
        draws = jnp.exp(jax.random.uniform(jax.random.fold_in(own, dim), (parts,), jnp.float32, least / len(cuts), high / len(cuts)))
        level = level * jnp.repeat(draws, dims[dim] // parts).reshape([-1 if axis == dim else 1 for axis in range(len(dims))])
    return level


def length_profile(count, total, bound, skew):
    weights = [(1 << 20) // math.isqrt(standing ** skew) + 1 for standing in range(2, count + 1)]
    surplus, given = total - bound - (count - 1), [1] * (count - 1)
    while surplus > 0:
        movable = [i for i in range(count - 1) if given[i] < bound]
        mass, remaining = sum([weights[i] for i in movable]), surplus
        for i in movable:
            addition = min(bound - given[i], max(1, remaining * weights[i] // mass), surplus)
            given[i] = given[i] + addition
            surplus = surplus - addition
    return np.array([bound] + given)


def ragged(own_key, count, total, bound, slope):
    if count == 2:
        one = jax.random.randint(own_key, (), max(1, total - bound), min(bound, total - 1) + 1)
        return jnp.stack([one, total - one])
    lengths = jnp.asarray(length_profile(count, total, bound, slope), jnp.int32)
    couples = (count - 1) // 2
    donor, taker = lengths[1:1 + 2 * couples:2], lengths[2:2 + 2 * couples:2]
    slack = jnp.minimum(donor - 1, bound - taker)
    moved = jax.random.randint(jax.random.fold_in(own_key, 1), (couples,), 0, 1 << 20) % (slack + 1)
    lengths = lengths.at[1:1 + 2 * couples:2].set(donor - moved).at[2:2 + 2 * couples:2].set(taker + moved)
    return lengths[jax.random.permutation(jax.random.fold_in(own_key, 2), count)]


def bell_draw(key, dims, scale, limit, shards=(), kind=jnp.bfloat16):
    entries = jax.random.normal(key, dims, jnp.float32) * scale
    if len(shards) > 0:
        entries = steps_of(key, dims, shards, -0.22, 0.18) * entries
    return jnp.clip(entries, min=-limit, max=limit).astype(kind)


def heavy_noise(rng, extent, deviation, bound, pieces, heavy, kind=jnp.bfloat16):
    result = deviation * jax.random.normal(rng, extent, jnp.float32)
    if pieces:
        result = result * steps_of(rng, extent, pieces, -0.22, 0.18)
    return jnp.clip(raised(result, jax.random.fold_in(rng, 3), *heavy), -bound, bound).astype(kind)


def setup_inputs(seed: int = 0) -> dict:
    arg_keys = jax.random.split(jax.random.key(seed), 6)
    return {
        "amplitudes": bell_draw(arg_keys[0], (NH, PAIR_CAP, ROW_CAP), 1.0, 6.0, ((0, 2), (1, 16)), jnp.float32),
        "integrals": heavy_noise(arg_keys[1], (COL_CAP, NH, PAIR_CAP), (NO * NV // NH) ** -0.5, 0.078125, ((1, 2), (2, 16)), (2, 0, 16, 2.0), jnp.float32),
        "row_count": ragged(arg_keys[2], NH, I_WIN * NV, ROW_CAP, 1).astype(jnp.int32),
        "pair_count": ragged(arg_keys[3], NH, NO * NV, PAIR_CAP, 1).astype(jnp.int32),
        "col_count": ragged(arg_keys[4], NH, J_WIN * NV, COL_CAP, 1).astype(jnp.int32),
    }


def one_block(packed):
    slab, amps, rows_live, pairs_live, cols_live = packed
    pair_index = jnp.arange(PAIR_CAP, dtype=jnp.int32)
    masked = jnp.where((pair_index < pairs_live)[:, None], amps, jnp.float32(0.0))
    product = jnp.dot(slab, masked, precision=lax.Precision.HIGHEST, preferred_element_type=jnp.float32)
    col_index = jnp.arange(COL_CAP, dtype=jnp.int32)
    row_index = jnp.arange(ROW_CAP, dtype=jnp.int32)
    keep = (col_index < cols_live)[:, None] & (row_index < rows_live)[None, :]
    return jnp.where(keep, product, jnp.float32(0.0))


def reference(amplitudes, integrals, row_count, pair_count, col_count):
    slabs = jnp.moveaxis(integrals, 1, 0)
    blocks = lax.map(one_block, (slabs, amplitudes, row_count, pair_count, col_count))
    return jnp.moveaxis(blocks, 0, 1)
```

```python
import functools

import jax
import jax.numpy as jnp
from jax import lax
from jax.experimental import pallas as pl
from jax.experimental.pallas import tpu as pltpu
from jax.sharding import PartitionSpec as P

OUTER = 4
CORES = 2
VMEM_BYTES = 56 * 1024 * 1024
F32 = jnp.float32
BF16 = jnp.bfloat16


def split(value):
    high = value.astype(BF16)
    return high, (value - high.astype(F32)).astype(BF16)


def prep_kernel(place, limit, b_ref, high_ref, low_ref):
    blocks, depth = b_ref.shape[1], b_ref.shape[2]
    pair = lax.broadcasted_iota(jnp.int32, (1, depth), 1)
    for h in range(blocks):
        value = jnp.where(pair < limit[h], b_ref[:, h, :], F32(0.0))
        high, low = split(value)
        high_ref[h, 0, 0] = high
        low_ref[h, 0, 0] = low


def prepare(integrals, place, limit, inner, cols):
    _, blocks, depth = integrals.shape
    groups = inner * OUTER

    def source(c, g, place, limit):
        return (((g // inner) * inner + g % inner) * CORES + c, 0, 0)

    def target(c, g, place, limit):
        z = lax.rem(g // inner - place[0] + OUTER, OUTER)
        x = lax.rem(g % inner - place[1] + inner, inner)
        core = lax.rem(c - place[2] + CORES, CORES)
        return (0, core, x * OUTER + z, 0, 0)

    shape = jax.ShapeDtypeStruct((blocks, CORES, groups, cols, depth), BF16)
    spec = pl.BlockSpec((blocks, 1, 1, cols, depth), target)
    return pl.pallas_call(
        prep_kernel,
        grid_spec=pltpu.PrefetchScalarGridSpec(
            num_scalar_prefetch=2,
            grid=(CORES, groups),
            in_specs=[pl.BlockSpec((cols, blocks, depth), source)],
            out_specs=[spec, spec],
        ),
        out_shape=[shape, shape],
        compiler_params=pltpu.CompilerParams(vmem_limit_bytes=VMEM_BYTES),
        name="prepare",
    )(place, limit, integrals)


def product(b_high, b_low, a_high, a_low):
    dot = functools.partial(jnp.dot, preferred_element_type=F32)
    return dot(b_high, a_high) + (dot(b_high, a_low) + dot(b_low, a_high))


def first_kernel(rows_live, b_high, b_low, a_ref, out, a_high, a_low):
    tile = a_ref.shape[2]
    groups, cols, depth = b_high.shape[2:]
    high, low = split(a_ref[0])
    a_high[...] = high
    a_low[...] = low
    live = pl.program_id(0) * tile < rows_live[0]

    @pl.when(live)
    def _():
        left = (r[0, 0].reshape(groups * cols, depth) for r in (b_high, b_low))
        out[...] = product(*left, high, low)

    @pl.when(jnp.logical_not(live))
    def _():
        out[...] = jnp.zeros_like(out)


def second_kernel(rows_live, b_high, b_low, a_high, a_low, received, *outs):
    tile = a_high.shape[1]
    groups, cols, depth = b_high.shape[2:]
    size = outs[0].shape[0]
    live = pl.program_id(0) * tile < rows_live[0]

    @pl.when(live)
    def _():
        left = (r[0, 0].reshape(groups * cols, depth) for r in (b_high, b_low))
        total = received[...] + product(*left, a_high[...], a_low[...])
        for i, out in enumerate(outs):
            out[...] = total[i * size:(i + 1) * size]

    @pl.when(jnp.logical_not(live))
    def _():
        for i, out in enumerate(outs):
            out[...] = received[i * size:(i + 1) * size, :]


def cost(m, k, n):
    return pl.CostEstimate(
        flops=6 * m * k * n, bytes_accessed=4 * (m * k + k * n + m * n), transcendentals=0
    )


def first_half(h, rows_live, b_high, b_low, amplitudes):
    _, _, groups, cols, depth = b_high.shape
    rows = amplitudes.shape[2]
    tile = min(rows, 256)
    left = pl.BlockSpec((1, 1, groups, cols, depth), lambda n, s: (h, 1, 0, 0, 0))
    wide = pl.BlockSpec((depth, tile), lambda n, s: (0, n))
    return pl.pallas_call(
        first_kernel,
        grid_spec=pltpu.PrefetchScalarGridSpec(
            num_scalar_prefetch=1,
            grid=(rows // tile,),
            in_specs=[left, left, pl.BlockSpec((1, depth, tile), lambda n, s: (h, 0, n))],
            out_specs=[pl.BlockSpec((groups * cols, tile), lambda n, s: (0, n)), wide, wide],
        ),
        out_shape=[
            jax.ShapeDtypeStruct((groups * cols, rows), F32),
            jax.ShapeDtypeStruct((depth, rows), BF16),
            jax.ShapeDtypeStruct((depth, rows), BF16),
        ],
        cost_estimate=cost(groups * cols, depth, rows),
        compiler_params=pltpu.CompilerParams(vmem_limit_bytes=VMEM_BYTES),
        name="first_half",
    )(rows_live, b_high, b_low, amplitudes)


def second_half(h, rows_live, b_high, b_low, a_high, a_low, received, inner):
    _, _, groups, cols, depth = b_high.shape
    rows = a_high.shape[1]
    tile = min(rows, 256)
    size = groups * cols // inner
    left = pl.BlockSpec((1, 1, groups, cols, depth), lambda n, s: (h, 0, 0, 0, 0))
    wide = pl.BlockSpec((depth, tile), lambda n, s: (0, n))
    return pl.pallas_call(
        second_kernel,
        grid_spec=pltpu.PrefetchScalarGridSpec(
            num_scalar_prefetch=1,
            grid=(rows // tile,),
            in_specs=[left, left, wide, wide,
                      pl.BlockSpec((groups * cols, tile), lambda n, s: (0, n))],
            out_specs=[pl.BlockSpec((size, tile), lambda n, s: (0, n))] * inner,
        ),
        out_shape=[jax.ShapeDtypeStruct((size, rows), F32)] * inner,
        cost_estimate=cost(groups * cols, depth, rows),
        compiler_params=pltpu.CompilerParams(vmem_limit_bytes=VMEM_BYTES),
        name="second_half",
    )(rows_live, b_high, b_low, a_high, a_low, received)


def line_sum(shards, pairs_of):
    n = len(shards)
    if n == 2:
        return shards[0] + lax.ppermute(shards[1], "tensor", pairs_of([(0, 1), (1, 0)]))
    up = down = None
    for step in range(1, n):
        reach = n - step
        send_up, send_down = shards[reach], shards[step]
        if up is not None:
            send_up, send_down = send_up + up, send_down + down
        up = lax.ppermute(send_up, "tensor", pairs_of([(i, i + 1) for i in range(step)]))
        down = lax.ppermute(
            send_down, "tensor", pairs_of([(i, i - 1) for i in range(reach, n)])
        )
    return shards[0] + up + down


def local(inner, amplitudes, integrals, row_count, pair_count, col_count):
    blocks, depth, rows = amplitudes.shape
    all_cols = integrals.shape[0]
    tensor, rep = lax.axis_size("tensor"), lax.axis_size("rep")
    cols, row_local = all_cols // tensor, rows // rep
    me, side = lax.axis_index("tensor"), lax.axis_index("rep")
    z, x, core = me // (inner * CORES), me // CORES % inner, me % CORES
    place = jnp.stack([z, x, core]).astype(jnp.int32)

    pairs_here = lax.dynamic_slice_in_dim(pair_count, side * blocks, blocks) - me * depth
    rows_here = lax.dynamic_slice_in_dim(row_count, side * blocks, blocks)
    rows_here = jnp.where(pairs_here > 0, rows_here, 0)
    b_high, b_low = prepare(integrals, place, pairs_here, inner, cols)

    def index(z, x, core):
        return (z * inner + x) * CORES + core

    across = [(index(z, x, c), index(z, x, 1 - c))
              for z in range(OUTER) for x in range(inner) for c in range(CORES)]

    def along_inner(moves):
        return [(index(z, a, c), index(z, b, c))
                for z in range(OUTER) for c in range(CORES) for a, b in moves]

    def along_outer(moves):
        return [(index(a, x, c), index(b, x, c))
                for x in range(inner) for c in range(CORES) for a, b in moves]

    halves = []
    for h in range(blocks):
        live = rows_here[h:h + 1]
        sent, a_high, a_low = first_half(h, live, b_high, b_low, amplitudes)
        received = lax.ppermute(sent, "tensor", across)
        halves.append((live, a_high, a_low, received))
    mine, other = [], []
    for h in range(blocks):
        live, a_high, a_low, received = halves[h]
        shards = second_half(h, live, b_high, b_low, a_high, a_low, received, inner)
        summed = line_sum(shards, along_inner)
        total = line_sum([summed[j * cols:(j + 1) * cols] for j in range(OUTER)], along_outer)
        if rep == 2:
            mine.append(lax.dynamic_slice_in_dim(total, side * row_local, row_local, 1))
            away = lax.dynamic_slice_in_dim(total, (1 - side) * row_local, row_local, 1)
            other.append(lax.ppermute(away, "rep", [(0, 1), (1, 0)]))
        else:
            mine.append(total)
    if rep == 2:
        swap = side == 1
        low = [jnp.where(swap, b, a) for a, b in zip(mine, other)]
        high = [jnp.where(swap, a, b) for a, b in zip(mine, other)]
        arranged = jnp.stack(low + high, axis=1)
    else:
        arranged = lax.all_to_all(
            jnp.stack(mine, axis=1), "rep", split_axis=2, concat_axis=1, tiled=True
        )
    col_index = me * cols + lax.broadcasted_iota(jnp.int32, (cols, 1, 1), 0)
    row_index = side * row_local + lax.broadcasted_iota(jnp.int32, (1, 1, row_local), 2)
    keep = (col_index < col_count[None, :, None]) & (row_index < row_count[None, :, None])
    return jnp.where(keep, arranged, F32(0.0))


def solution(mesh):
    inner = mesh.shape["tensor"] // (OUTER * CORES)
    in_specs = (P("rep", "tensor", None), P(None, "rep", "tensor"), P(), P(), P())
    out_specs = P("tensor", None, "rep")
    return jax.shard_map(
        functools.partial(local, inner), mesh=mesh, in_specs=in_specs, out_specs=out_specs,
        check_vma=False,
    )
```

```python
import functools

import jax
import jax.numpy as jnp
from jax import lax
from jax.experimental import pallas as pl
from jax.experimental.pallas import tpu as pltpu
from jax.sharding import PartitionSpec as P

OUTER = 4
CORES = 2
LANES = 128
TILE = 256
VMEM_BYTES = 40 * 1024 * 1024
F32 = jnp.float32
BF16 = jnp.bfloat16


def params():
    return pltpu.CompilerParams(vmem_limit_bytes=VMEM_BYTES)


def cost():
    return pl.CostEstimate(flops=1024, bytes_accessed=1024, transcendentals=0)


def split(value):
    high = value.astype(BF16)
    return high, (value - high.astype(F32)).astype(BF16)


def reversed_bits(value, count):
    result, bit = 0, 1
    while bit < count:
        result = 2 * result + (value // bit) % 2
        bit *= 2
    return result


def prep_kernel(place, limit, b_ref, high_ref, low_ref):
    blocks, _, _, cols, depth = high_ref.shape
    tiles = depth // LANES
    lane = lax.broadcasted_iota(jnp.int32, (1, LANES), 1)
    for h in range(blocks):
        for t in range(tiles):
            value = b_ref[pl.ds(t * blocks + h, cols, stride=tiles * blocks), :]
            value = jnp.where(lane < limit[h] - t * LANES, value, F32(0.0))
            high, low = split(value)
            high_ref[h, 0, 0, :, t * LANES:(t + 1) * LANES] = high
            low_ref[h, 0, 0, :, t * LANES:(t + 1) * LANES] = low


def prepare(rows_of_b, place, limit, shift, blocks, cols, depth, inner):
    size = cols * depth * blocks // LANES

    def source(g, place, limit):
        return (g * CORES + lax.rem(place[2] + shift, CORES), 0)

    def target(g, place, limit):
        z = reversed_bits((g // inner) ^ place[0], OUTER)
        x = reversed_bits((g % inner) ^ place[1], inner)
        return (0, x, z, 0, 0)

    shape = jax.ShapeDtypeStruct((blocks, inner, OUTER, cols, depth), BF16)
    spec = pl.BlockSpec((blocks, 1, 1, cols, depth), target)
    return pl.pallas_call(
        prep_kernel,
        grid_spec=pltpu.PrefetchScalarGridSpec(
            num_scalar_prefetch=2,
            grid=(inner * OUTER,),
            in_specs=[pl.BlockSpec((size, LANES), source)],
            out_specs=[spec, spec],
        ),
        out_shape=[shape, shape],
        cost_estimate=cost(),
        compiler_params=params(),
        name="prepare",
    )(place, limit, rows_of_b)


def product(b_high, b_low, a_ref):
    inner, outer, cols, depth = b_high.shape[1:]
    high, low = split(a_ref[0])
    left_high, left_low = (r[0].reshape(inner * outer * cols, depth) for r in (b_high, b_low))
    dot = functools.partial(jnp.dot, preferred_element_type=F32)
    return dot(left_high, high) + (dot(left_high, low) + dot(left_low, high))


def first_kernel(start, rows_live, b_high, b_low, a_ref, out):
    live = start + pl.program_id(0) * out.shape[1] < rows_live[0]

    @pl.when(live)
    def _():
        out[...] = product(b_high, b_low, a_ref)

    @pl.when(jnp.logical_not(live))
    def _():
        out[...] = jnp.zeros_like(out)


def second_kernel(start, outer_first, rows_live, b_high, b_low, a_ref, received, *outs):
    inner, outer, cols = b_high.shape[1:4]
    live = start + pl.program_id(0) * received.shape[1] < rows_live[0]

    def put(total):
        half = inner * outer // 2
        for x in range(inner):
            for z in range(outer):
                part = total[(x * outer + z) * cols:(x * outer + z + 1) * cols]
                place = z * inner + x if outer_first else x * outer + z
                row = place % half * cols
                outs[place // half][row:row + cols, :] = part

    @pl.when(live)
    def _():
        put(received[...] + product(b_high, b_low, a_ref))

    @pl.when(jnp.logical_not(live))
    def _():
        put(received[...])


def specs(h, start, b_high, amplitudes):
    inner, outer, cols, depth = b_high.shape[1:]
    tile = min(amplitudes.shape[2], TILE)
    left = pl.BlockSpec((1, inner, outer, cols, depth), lambda n, s: (h, 0, 0, 0, 0))
    right = pl.BlockSpec((1, depth, tile), lambda n, s: (h, 0, start // tile + n))
    return tile, inner * outer * cols, [left, left, right]


def first_half(h, start, rows, rows_live, b_high, b_low, amplitudes):
    tile, total, in_specs = specs(h, start, b_high, amplitudes)
    depth = amplitudes.shape[1]
    return pl.pallas_call(
        functools.partial(first_kernel, start),
        grid_spec=pltpu.PrefetchScalarGridSpec(
            num_scalar_prefetch=1,
            grid=(rows // tile,),
            in_specs=in_specs,
            out_specs=pl.BlockSpec((total, tile), lambda n, s: (0, n)),
        ),
        out_shape=jax.ShapeDtypeStruct((total, rows), F32),
        cost_estimate=cost(),
        compiler_params=params(),
        name="first_half",
    )(rows_live, b_high, b_low, amplitudes)


def second_half(h, start, rows, outer_first, rows_live, b_high, b_low, amplitudes, received):
    tile, total, in_specs = specs(h, start, b_high, amplitudes)
    depth = amplitudes.shape[1]
    part = total // 2
    return pl.pallas_call(
        functools.partial(second_kernel, start, outer_first),
        grid_spec=pltpu.PrefetchScalarGridSpec(
            num_scalar_prefetch=1,
            grid=(rows // tile,),
            in_specs=in_specs + [pl.BlockSpec((total, tile), lambda n, s: (0, n))],
            out_specs=[pl.BlockSpec((part, tile), lambda n, s: (0, n))] * 2,
        ),
        out_shape=[jax.ShapeDtypeStruct((part, rows), F32)] * 2,
        cost_estimate=cost(),
        compiler_params=params(),
        name="second_half",
    )(rows_live, b_high, b_low, amplitudes, received)


class Chain:
    def __init__(self):
        self.last = None

    def run(self, step, *args):
        if self.last is not None:
            args, _ = lax.optimization_barrier((args, self.last))
        result = step(*args)
        self.last = jax.tree.leaves(result)[0]
        return result


def local(inner, amplitudes, integrals, row_count, pair_count, col_count):
    blocks, depth, rows = amplitudes.shape
    all_cols = integrals.shape[0]
    tensor, rep = lax.axis_size("tensor"), lax.axis_size("rep")
    cols, row_local = all_cols // tensor, rows // rep
    me, side = lax.axis_index("tensor"), lax.axis_index("rep")
    z, x, core = me // (inner * CORES), me // CORES % inner, me % CORES
    place = jnp.stack([z, x, core]).astype(jnp.int32)

    pairs_here = lax.dynamic_slice_in_dim(pair_count, side * blocks, blocks) - me * depth
    rows_here = lax.dynamic_slice_in_dim(row_count, side * blocks, blocks)
    rows_here = jnp.where(pairs_here > 0, rows_here, 0)
    live = [rows_here[h:h + 1] for h in range(blocks)]
    rows_of_b = integrals.reshape(all_cols, blocks, depth // LANES, LANES)
    rows_of_b = rows_of_b.transpose(0, 2, 1, 3).reshape(-1, LANES)

    def index(z, x, core):
        return (z * inner + x) * CORES + core

    across = [(index(z, x, c), index(z, x, 1 - c))
              for z in range(OUTER) for x in range(inner) for c in range(CORES)]

    def along_inner(bit):
        return [(index(z, x, c), index(z, x ^ bit, c))
                for z in range(OUTER) for x in range(inner) for c in range(CORES)]

    def along_outer(bit):
        return [(index(z, x, c), index(z ^ bit, x, c))
                for z in range(OUTER) for x in range(inner) for c in range(CORES)]

    chain = Chain()
    left, totals = {}, {}

    def prep(shift):
        left[shift] = chain.run(
            lambda b: prepare(b, place, pairs_here, shift, blocks, cols, depth, inner), rows_of_b
        )

    def work(h, start, count, outer_first):
        sent = chain.run(
            functools.partial(first_half, h, start, count), live[h], *left[1], amplitudes
        )
        yield
        got = lax.ppermute(sent, "tensor", across)
        keep, send = chain.run(
            functools.partial(second_half, h, start, count, outer_first),
            live[h], *left[0], amplitudes, got,
        )
        yield
        steps = [along_inner(1 << i) for i in range(inner.bit_length() - 1)]
        more = [along_outer(1 << i) for i in range(OUTER.bit_length() - 1)]
        for pairs in more + steps if outer_first else steps + more:
            got = lax.ppermute(send, "tensor", pairs)
            half = keep.shape[0] // 2
            if half < cols:
                total = chain.run(jnp.add, keep, got)
            else:
                keep, send = chain.run(
                    lambda a, b: (a[:half] + b[:half], a[half:] + b[half:]), keep, got
                )
            yield
        totals[h, start] = total

    mine, other = {}, {}

    def exchange(h):
        for chunk in owned[h]:
            for _ in chunk:
                pass
        if rep != 2:
            mine[h] = totals[h, 0]
            return
        if (h, row_local) in totals:
            first, second = totals[h, 0], totals[h, row_local]
        else:
            first, second = totals[h, 0][:, :row_local], totals[h, 0][:, row_local:]
        mine[h], away = chain.run(
            lambda a, b: (jnp.where(side == 0, a, b), jnp.where(side == 0, b, a)), first, second
        )
        other[h] = lax.ppermute(away, "rep", [(0, 1), (1, 0)])

    prep(1)
    if inner == 2 and rep == 2 and blocks == 4:
        chunks = [work(0, 0, rows, False), work(1, 0, rows, False), work(2, 0, rows, False),
                  work(3, row_local, row_local, False), work(3, 0, row_local, True)]
        owned = [chunks[:1], chunks[1:2], chunks[2:3], chunks[3:]]
        plan = "0p044112240" + "3341" + "0420" + "a" + "131" + "b2323cd"
    else:
        chunks = [work(h, 0, rows, False) for h in range(blocks)]
        owned = [[chunk] for chunk in chunks]
        steps = 2 + (inner * OUTER).bit_length() - 1
        plan = "".join("0p" + "0" * (steps - 1) + "a" if h == 0 else
                       str(h) * steps + "abcdefgh"[h] for h in range(blocks))
    for move in plan:
        if move == "p":
            prep(0)
        elif move in "abcdefgh":
            exchange("abcdefgh".index(move))
        else:
            next(chunks[int(move)], None)

    if rep == 2:
        low = [jnp.where(side == 1, other[h], mine[h]) for h in range(blocks)]
        high = [jnp.where(side == 1, mine[h], other[h]) for h in range(blocks)]
        arranged = jnp.stack(low + high, axis=1)
    else:
        arranged = lax.all_to_all(
            jnp.stack([mine[h] for h in range(blocks)], axis=1), "rep",
            split_axis=2, concat_axis=1, tiled=True,
        )
    col_index = me * cols + lax.broadcasted_iota(jnp.int32, (cols, 1, 1), 0)
    row_index = side * row_local + lax.broadcasted_iota(jnp.int32, (1, 1, row_local), 2)
    keep = (col_index < col_count[None, :, None]) & (row_index < row_count[None, :, None])
    return jnp.where(keep, arranged, F32(0.0))


def solution(mesh):
    inner = mesh.shape["tensor"] // (OUTER * CORES)
    in_specs = (P("rep", "tensor", None), P(None, "rep", "tensor"), P(), P(), P())
    out_specs = P("tensor", None, "rep")
    return jax.shard_map(
        functools.partial(local, inner), mesh=mesh, in_specs=in_specs, out_specs=out_specs,
        check_vma=False,
    )
```

```python
import functools

import jax
import jax.numpy as jnp
from jax import lax
from jax.experimental import pallas as pl
from jax.experimental.pallas import tpu as pltpu
from jax.sharding import PartitionSpec as P

OUTER = 4
CORES = 2
LANES = 128
TILE = 256
VMEM_BYTES = 40 * 1024 * 1024
F32 = jnp.float32
BF16 = jnp.bfloat16


def params():
    return pltpu.CompilerParams(vmem_limit_bytes=VMEM_BYTES)


def cost():
    return pl.CostEstimate(flops=1024, bytes_accessed=1024, transcendentals=0)


def split(value):
    high = value.astype(BF16)
    return high, (value - high.astype(F32)).astype(BF16)


def reversed_bits(value, count):
    result, bit = 0, 1
    while bit < count:
        result = 2 * result + (value // bit) % 2
        bit *= 2
    return result


def put_split(group, limit, first, b_ref, high_ref, low_ref, place):
    used = high_ref.shape[0]
    cols, depth = high_ref.shape[-2:]
    tiles = depth // LANES
    blocks = b_ref.shape[3] // tiles
    lane = lax.broadcasted_iota(jnp.int32, (1, LANES), 1)
    turned = jnp.swapaxes(b_ref[group, 0], 0, 1)
    for h in range(used):
        for t in range(tiles):
            value = turned[t * blocks + first + h]
            value = jnp.where(lane < limit[first + h] - t * LANES, value, F32(0.0))
            high, low = split(value)
            high_ref[(h, *place, slice(None), slice(t * LANES, (t + 1) * LANES))] = high
            low_ref[(h, *place, slice(None), slice(t * LANES, (t + 1) * LANES))] = low


def slot(group, place, inner):
    x = reversed_bits((group % inner) ^ place[1], inner)
    z = reversed_bits((group // inner) ^ place[0], OUTER)
    return x * OUTER + z


def prep_kernel(first, inner, place, limit, b_ref, high_ref, low_ref):
    put_split(0, limit, first, b_ref, high_ref, low_ref, (0,))


def prepare(parts_of_b, place, limit, first, shift, inner):
    groups, _, cols, rows, _ = parts_of_b.shape
    blocks = limit.shape[0]
    depth = rows * LANES // blocks

    def source(g, place, limit):
        return (g, lax.rem(place[2] + shift, CORES), 0, 0, 0)

    def target(g, place, limit):
        return (0, slot(g, place, inner), 0, 0)

    shape = jax.ShapeDtypeStruct((blocks - first, groups, cols, depth), BF16)
    spec = pl.BlockSpec((blocks - first, 1, cols, depth), target)
    return pl.pallas_call(
        functools.partial(prep_kernel, first, inner),
        grid_spec=pltpu.PrefetchScalarGridSpec(
            num_scalar_prefetch=2,
            grid=(groups,),
            in_specs=[pl.BlockSpec((1, 1, cols, rows, LANES), source)],
            out_specs=[spec, spec],
        ),
        out_shape=[shape, shape],
        cost_estimate=cost(),
        compiler_params=params(),
        name="prepare",
    )(place, limit, parts_of_b)


def halves_put(total, outs, inner, cols, outer_first):
    groups = total.shape[0] // cols
    for x in range(inner):
        for z in range(groups // inner):
            row = (x * OUTER + z) * cols
            place = z * inner + x if outer_first else x * OUTER + z
            at = place % (groups // 2) * cols
            outs[place // (groups // 2)][at:at + cols, :] = total[row:row + cols]


def both(refs):
    return jnp.concatenate([ref[...] for ref in refs], axis=0)


def dot3(left_high, left_low, a_ref):
    high, low = split(a_ref[0])
    dot = functools.partial(jnp.dot, preferred_element_type=F32)
    return dot(left_high, high) + (dot(left_high, low) + dot(left_low, high))


def whole_kernel(first, inner, step, chunks, adds, place, limit, rows_live, b_ref, a_ref, *refs):
    if adds:
        received, refs = refs[:2], refs[2:]
    *outs, high_ref, low_ref = refs
    tile = a_ref.shape[2]
    groups, cols, depth = high_ref.shape[1:]
    loads = groups // step
    now = pl.program_id(0)

    @pl.when(now < loads)
    def _():
        for i in range(step):
            group = now * step + i
            put_split(i, limit, first, b_ref, high_ref, low_ref, (slot(group, place, inner),))

    at = loads
    for i, (h, start, count) in enumerate(chunks):
        size = count // tile
        mine = (now >= at) & (now < at + size)
        live = start + (now - at) * tile < rows_live[h]

        @pl.when(mine & live)
        def _():
            total = dot3(*(r[h - first].reshape(groups * cols, depth) for r in (high_ref, low_ref)), a_ref)
            if adds:
                halves_put(total + both(received), outs, inner, cols, False)
            else:
                half = groups * cols // 2
                outs[2 * i][...] = total[:half]
                outs[2 * i + 1][...] = total[half:]

        @pl.when(mine & jnp.logical_not(live))
        def _():
            if adds:
                halves_put(both(received), outs, inner, cols, False)
            else:
                for out in outs[2 * i:2 * i + 2]:
                    out[...] = jnp.zeros_like(out)

        at += size


def whole_products(place, limit, rows_live, parts_of_b, amplitudes, chunks, shift, inner, received=None):
    groups, _, cols, rows_b, _ = parts_of_b.shape
    blocks, depth, rows = amplitudes.shape
    tile = min(rows, TILE)
    step = min(groups, 2)
    loads = groups // step
    first, last = chunks[0][0], chunks[-1][0]
    sizes = [count // tile for _, _, count in chunks]
    offset = chunks[0][1] // tile
    total = sum(sizes)
    per_block = rows // tile

    def b_map(n, place, *_):
        return (jnp.minimum(n, loads - 1), lax.rem(place[2] + shift, CORES), 0, 0, 0)

    def a_map(n, *_):
        t = jnp.maximum(n - loads, 0) + offset
        return (first + t // per_block, 0, t % per_block)

    def tile_map(at, size):
        return lambda n, *_: (0, jnp.clip(n - loads - at, 0, size - 1))

    in_specs = [pl.BlockSpec((step, 1, cols, rows_b, LANES), b_map),
                pl.BlockSpec((1, depth, tile), a_map)]
    operands = [parts_of_b, amplitudes]
    height = groups * cols
    if received is not None:
        in_specs += [pl.BlockSpec((height // 2, tile), tile_map(0, total))] * 2
        operands += received
        out_specs = [pl.BlockSpec((height // 2, tile), tile_map(0, total))] * 2
        shapes = [jax.ShapeDtypeStruct((height // 2, total * tile), F32)] * 2
    else:
        starts = [sum(sizes[:i]) for i in range(len(sizes))]
        out_specs = [pl.BlockSpec((height // 2, tile), tile_map(*x))
                     for x in zip(starts, sizes) for _ in range(2)]
        shapes = [jax.ShapeDtypeStruct((height // 2, size * tile), F32)
                  for size in sizes for _ in range(2)]
    part = pltpu.VMEM((last - first + 1, groups, cols, depth), BF16)
    return pl.pallas_call(
        functools.partial(whole_kernel, first, inner, step, chunks, received is not None),
        grid_spec=pltpu.PrefetchScalarGridSpec(
            num_scalar_prefetch=3,
            grid=(loads + total,),
            in_specs=in_specs,
            out_specs=out_specs,
            scratch_shapes=[part, part],
        ),
        out_shape=shapes,
        cost_estimate=cost(),
        compiler_params=params(),
        name="whole_products",
    )(place, limit, rows_live, *operands)


def second_kernel(h, start, inner, outer_first, rows_live, b_high, b_low, a_ref, *refs):
    received, outs = refs[:2], refs[2:]
    groups, cols, depth = b_high.shape[1:]
    live = start + pl.program_id(0) * a_ref.shape[2] < rows_live[h]

    @pl.when(live)
    def _():
        total = dot3(*(r[0].reshape(groups * cols, depth) for r in (b_high, b_low)), a_ref)
        halves_put(total + both(received), outs, inner, cols, outer_first)

    @pl.when(jnp.logical_not(live))
    def _():
        halves_put(both(received), outs, inner, cols, outer_first)


def second_half(h, start, count, first, inner, outer_first, rows_live, b_high, b_low, amplitudes, received):
    groups, cols, depth = b_high.shape[1:]
    tile = min(amplitudes.shape[2], TILE)
    height = groups * cols
    left = pl.BlockSpec((1, groups, cols, depth), lambda n, s: (h - first, 0, 0, 0))
    return pl.pallas_call(
        functools.partial(second_kernel, h, start, inner, outer_first),
        grid_spec=pltpu.PrefetchScalarGridSpec(
            num_scalar_prefetch=1,
            grid=(count // tile,),
            in_specs=[left, left,
                      pl.BlockSpec((1, depth, tile), lambda n, s: (h, 0, start // tile + n)),
                      *[pl.BlockSpec((height // 2, tile), lambda n, s: (0, n))] * 2],
            out_specs=[pl.BlockSpec((height // 2, tile), lambda n, s: (0, n))] * 2,
        ),
        out_shape=[jax.ShapeDtypeStruct((height // 2, count), F32)] * 2,
        cost_estimate=cost(),
        compiler_params=params(),
        name="second_half",
    )(rows_live, b_high, b_low, amplitudes, *received)


def place_kernel(side_ref, base, row_count, col_count, *refs):
    *parts, out_ref = refs
    side = side_ref[0]
    blocks = len(parts) // 2
    cols, rows = parts[0].shape
    col = base[0] + lax.broadcasted_iota(jnp.int32, (cols, rows), 0)
    row = base[1] + lax.broadcasted_iota(jnp.int32, (cols, rows), 1)
    for here in range(2):
        @pl.when(side == here)
        def _():
            order = parts[blocks:] + parts[:blocks] if here else parts
            kept = [
                jnp.where((col < col_count[h]) & (row < row_count[h]), part[...], F32(0.0))
                for h, part in enumerate(order)
            ]
            out_ref[...] = jnp.swapaxes(jnp.stack(kept), 0, 1)


def place_blocks(side, base, row_count, col_count, mine, other):
    cols, rows = mine[0].shape
    blocks = 2 * len(mine)
    vmem = pl.BlockSpec(memory_space=pltpu.VMEM)
    return pl.pallas_call(
        place_kernel,
        grid_spec=pltpu.PrefetchScalarGridSpec(
            num_scalar_prefetch=4, grid=(), in_specs=[vmem] * blocks, out_specs=vmem,
        ),
        out_shape=jax.ShapeDtypeStruct((cols, blocks, rows), F32),
        cost_estimate=cost(),
        compiler_params=params(),
        name="place_blocks",
    )(side, base, row_count, col_count, *mine, *other)


class Chain:
    def __init__(self):
        self.last = None

    def run(self, step, *args):
        if self.last is not None:
            args, _ = lax.optimization_barrier((args, self.last))
        result = step(*args)
        self.last = jax.tree.leaves(result)[0]
        return result


def local(inner, amplitudes, integrals, row_count, pair_count, col_count):
    blocks, depth, rows = amplitudes.shape
    all_cols = integrals.shape[0]
    tensor, rep = lax.axis_size("tensor"), lax.axis_size("rep")
    cols, row_local = all_cols // tensor, rows // rep
    me, side = lax.axis_index("tensor"), lax.axis_index("rep")
    z, x, core = me // (inner * CORES), me // CORES % inner, me % CORES
    place = jnp.stack([z, x, core]).astype(jnp.int32)

    pairs_here = lax.dynamic_slice_in_dim(pair_count, side * blocks, blocks) - me * depth
    rows_here = lax.dynamic_slice_in_dim(row_count, side * blocks, blocks)
    rows_here = jnp.where(pairs_here > 0, rows_here, 0)
    parts_of_b = integrals.reshape(all_cols, blocks, depth // LANES, LANES).transpose(0, 2, 1, 3)
    parts_of_b = parts_of_b.reshape(inner * OUTER, CORES, cols, blocks * depth // LANES, LANES)

    def index(z, x, core):
        return (z * inner + x) * CORES + core

    across = [(index(z, x, c), index(z, x, 1 - c))
              for z in range(OUTER) for x in range(inner) for c in range(CORES)]

    def along_inner(bit):
        return [(index(z, x, c), index(z, x ^ bit, c))
                for z in range(OUTER) for x in range(inner) for c in range(CORES)]

    def along_outer(bit):
        return [(index(z, x, c), index(z ^ bit, x, c))
                for z in range(OUTER) for x in range(inner) for c in range(CORES)]

    chain = Chain()
    received, totals = {}, {}

    def whole(chunks, shift, *got):
        return chain.run(
            lambda p, l, r, b, a, *g: whole_products(p, l, r, b, a, chunks, shift, inner, *g),
            place, pairs_here, rows_here, parts_of_b, amplitudes, *got,
        )

    def first_halves(chunks):
        sent = whole(chunks, 1)
        for i, (h, start, _) in enumerate(chunks):
            received[h, start] = [
                lax.ppermute(part, "tensor", across) for part in sent[2 * i:2 * i + 2]
            ]

    def work(h, start, count, outer_first=False):
        got = received[h, start]
        if h == 0:
            keep, send = whole([(h, start, count)], 0, got)
        else:
            keep, send = chain.run(
                functools.partial(second_half, h, start, count, 1, inner, outer_first),
                rows_here, *prepared, amplitudes, got,
            )
        yield
        steps = [along_inner(1 << i) for i in range(inner.bit_length() - 1)]
        more = [along_outer(1 << i) for i in range(OUTER.bit_length() - 1)]
        for pairs in more + steps if outer_first else steps + more:
            got = lax.ppermute(send, "tensor", pairs)
            half = keep.shape[0] // 2
            if half < cols:
                total = chain.run(jnp.add, keep, got)
            else:
                keep, send = chain.run(
                    lambda a, b: (a[:half] + b[:half], a[half:] + b[half:]), keep, got
                )
            yield
        totals[h, start] = total

    mine, other = {}, {}

    def exchange(h):
        for chunk in owned[h]:
            for _ in chunk:
                pass
        if rep != 2:
            mine[h] = totals[h, 0]
            return
        if (h, row_local) in totals:
            first, second = totals[h, 0], totals[h, row_local]
        else:
            first, second = totals[h, 0][:, :row_local], totals[h, 0][:, row_local:]
        mine[h], away = chain.run(
            lambda a, b: (jnp.where(side == 0, a, b), jnp.where(side == 0, b, a)), first, second
        )
        other[h] = lax.ppermute(away, "rep", [(0, 1), (1, 0)])

    first_halves([(0, 0, rows)])
    if inner == 2 and rep == 2 and blocks == 4:
        chunks = [work(0, 0, rows), work(1, 0, rows), work(2, 0, rows),
                  work(3, row_local, row_local), work(3, 0, row_local, True)]
        owned = [chunks[:1], chunks[1:2], chunks[2:3], chunks[3:]]
        later = [(1, 0, rows), (2, 0, rows), (3, 0, row_local), (3, row_local, row_local)]
        plan = "0p01024314a21A432bB3cCd"
    else:
        chunks = [work(h, 0, rows) for h in range(blocks)]
        owned = [[chunk] for chunk in chunks]
        later = [(h, 0, rows) for h in range(1, blocks)]
        plan = "0" + "p" * (blocks > 1) + "abcdefgh"[:blocks]
    for move in plan:
        if move == "p":
            first_halves(later)
            prepared = chain.run(
                lambda b: prepare(b, place, pairs_here, 1, 0, inner), parts_of_b
            )
        elif move in "ABCDEFGH":
            chain.last = chain.last, other["ABCDEFGH".index(move)]
        elif move in "abcdefgh":
            exchange("abcdefgh".index(move))
        else:
            next(chunks[int(move)], None)

    if rep == 2:
        base = jnp.stack([me * cols, side * row_local]).astype(jnp.int32)
        return place_blocks(
            jnp.reshape(side, (1,)).astype(jnp.int32), base, row_count, col_count,
            [mine[h] for h in range(blocks)], [other[h] for h in range(blocks)],
        )
    arranged = lax.all_to_all(
        jnp.stack([mine[h] for h in range(blocks)], axis=1), "rep",
        split_axis=2, concat_axis=1, tiled=True,
    )
    col_index = me * cols + lax.broadcasted_iota(jnp.int32, (cols, 1, 1), 0)
    row_index = side * row_local + lax.broadcasted_iota(jnp.int32, (1, 1, row_local), 2)
    keep = (col_index < col_count[None, :, None]) & (row_index < row_count[None, :, None])
    return jnp.where(keep, arranged, F32(0.0))


def solution(mesh):
    inner = mesh.shape["tensor"] // (OUTER * CORES)
    in_specs = (P("rep", "tensor", None), P(None, "rep", "tensor"), P(), P(), P())
    out_specs = P("tensor", None, "rep")
    return jax.shard_map(
        functools.partial(local, inner), mesh=mesh, in_specs=in_specs, out_specs=out_specs,
        check_vma=False,
    )
```

```python
import functools

import jax
import jax.numpy as jnp
from jax import lax
from jax.experimental import pallas as pl
from jax.experimental.pallas import tpu as pltpu
from jax.sharding import PartitionSpec as P

OUTER = 4
CORES = 2
LANES = 128
TILE = 256
VMEM_BYTES = 40 * 1024 * 1024
F32 = jnp.float32
BF16 = jnp.bfloat16


def params():
    return pltpu.CompilerParams(vmem_limit_bytes=VMEM_BYTES)


def cost():
    return pl.CostEstimate(flops=1024, bytes_accessed=1024, transcendentals=0)


def split(value):
    high = value.astype(BF16)
    return high, (value - high.astype(F32)).astype(BF16)


def reversed_bits(value, count):
    result, bit = 0, 1
    while bit < count:
        result = 2 * result + (value // bit) % 2
        bit *= 2
    return result


def put_split(group, limit, first, b_ref, high_ref, low_ref, place):
    used = high_ref.shape[0]
    cols, depth = high_ref.shape[-2:]
    tiles = depth // LANES
    blocks = b_ref.shape[3] // tiles
    lane = lax.broadcasted_iota(jnp.int32, (1, LANES), 1)
    for h in range(used):
        rows = pl.ds(first + h, tiles, stride=blocks) if blocks > 1 else slice(None)
        turned = jnp.swapaxes(b_ref[group, 0, :, rows, :], 0, 1)
        for t in range(tiles):
            value = jnp.where(lane < limit[first + h] - t * LANES, turned[t], F32(0.0))
            high, low = split(value)
            high_ref[(h, *place, slice(None), slice(t * LANES, (t + 1) * LANES))] = high
            low_ref[(h, *place, slice(None), slice(t * LANES, (t + 1) * LANES))] = low


def slot(group, place, inner):
    x = reversed_bits((group % inner) ^ place[1], inner)
    z = reversed_bits((group // inner) ^ place[0], OUTER)
    return x * OUTER + z


def halves_put(total, outs, inner, cols, outer_first):
    groups = total.shape[0] // cols
    for x in range(inner):
        for z in range(groups // inner):
            row = (x * OUTER + z) * cols
            place = z * inner + x if outer_first else x * OUTER + z
            at = place % (groups // 2) * cols
            outs[place // (groups // 2)][at:at + cols, :] = total[row:row + cols]


def both(refs):
    return jnp.concatenate([ref[...] for ref in refs], axis=0)


def dot3(left_high, left_low, a_ref):
    high, low = split(a_ref[0])
    dot = functools.partial(jnp.dot, preferred_element_type=F32)
    return dot(left_high, high) + (dot(left_high, low) + dot(left_low, high))


def products_kernel(first, inner, step, chunks, pieces, adds, place, limit, rows_live, b_ref, a_ref, *refs):
    taken = sum(pieces) if adds else 0
    received, outs, (high_ref, low_ref) = refs[:taken], refs[taken:-2], refs[-2:]
    tile = a_ref.shape[2]
    groups, cols, depth = high_ref.shape[1:]
    loads = groups // step
    now = pl.program_id(0)

    @pl.when(now < loads)
    def _():
        for i in range(step):
            group = now * step + i
            put_split(i, limit, first, b_ref, high_ref, low_ref, (slot(group, place, inner),))

    at = loads
    for (h, start, count, outer_first), parts in zip(chunks, pieces):
        size = count // tile
        mine = (now >= at) & (now < at + size)
        live = start + (now - at) * tile < rows_live[h]
        got, received = received[:parts], received[parts:]
        out, outs = outs[:2 if adds else parts], outs[2 if adds else parts:]

        def put(total):
            if adds:
                halves_put(total, out, inner, cols, outer_first)
                return
            part = total.shape[0] // parts
            for i, ref in enumerate(out):
                ref[...] = total[i * part:(i + 1) * part]

        @pl.when(mine & live)
        def _():
            left = (r[h - first].reshape(groups * cols, depth) for r in (high_ref, low_ref))
            total = dot3(*left, a_ref)
            put(total + both(got) if adds else total)

        @pl.when(mine & jnp.logical_not(live))
        def _():
            put(both(got) if adds else jnp.zeros((groups * cols, tile), F32))

        at += size


def products(place, limit, rows_live, parts_of_b, amplitudes, chunks, shift, inner, pieces, received):
    groups, _, cols, rows_b, _ = parts_of_b.shape
    blocks, depth, rows = amplitudes.shape
    tile = min(rows, TILE)
    step = min(groups, 2)
    loads = groups // step
    first, last = chunks[0][0], chunks[-1][0]
    sizes = [chunk[2] // tile for chunk in chunks]
    offset = chunks[0][1] // tile
    total = sum(sizes)
    per_block = rows // tile
    height = groups * cols
    adds = bool(received)

    def b_map(n, place, *_):
        return (jnp.minimum(n, loads - 1), lax.rem(place[2] + shift, CORES), 0, 0, 0)

    def a_map(n, *_):
        t = jnp.maximum(n - loads, 0) + offset
        return (first + t // per_block, 0, t % per_block)

    def tiles_of(counts):
        result, at = [], 0
        for size, count in zip(sizes, counts):
            result += [pl.BlockSpec(
                (height // count, tile),
                lambda n, *_, at=at, size=size: (0, jnp.clip(n - loads - at, 0, size - 1)),
            )] * count
            at += size
        return result

    counts = [2] * len(chunks) if adds else pieces
    part = pltpu.VMEM((last - first + 1, groups, cols, depth), BF16)
    return pl.pallas_call(
        functools.partial(products_kernel, first, inner, step, chunks, pieces, adds),
        grid_spec=pltpu.PrefetchScalarGridSpec(
            num_scalar_prefetch=3,
            grid=(loads + total,),
            in_specs=[pl.BlockSpec((step, 1, cols, rows_b, LANES), b_map),
                      pl.BlockSpec((1, depth, tile), a_map)] + (tiles_of(pieces) if adds else []),
            out_specs=tiles_of(counts),
            scratch_shapes=[part, part],
        ),
        out_shape=[jax.ShapeDtypeStruct((height // count, chunk[2]), F32)
                   for chunk, count in zip(chunks, counts) for _ in range(count)],
        cost_estimate=cost(),
        compiler_params=params(),
        name="second_halves" if adds else "first_halves",
    )(place, limit, rows_live, parts_of_b, amplitudes, *received)


def place_kernel(side_ref, base, row_count, col_count, *refs):
    *parts, out_ref = refs
    side = side_ref[0]
    blocks = len(parts) // 2
    cols, rows = parts[0].shape
    col = base[0] + lax.broadcasted_iota(jnp.int32, (cols, rows), 0)
    row = base[1] + lax.broadcasted_iota(jnp.int32, (cols, rows), 1)
    for here in range(2):
        @pl.when(side == here)
        def _():
            order = parts[blocks:] + parts[:blocks] if here else parts
            kept = [
                jnp.where((col < col_count[h]) & (row < row_count[h]), part[...], F32(0.0))
                for h, part in enumerate(order)
            ]
            out_ref[...] = jnp.swapaxes(jnp.stack(kept), 0, 1)


def place_blocks(side, base, row_count, col_count, mine, other):
    cols, rows = mine[0].shape
    blocks = 2 * len(mine)
    vmem = pl.BlockSpec(memory_space=pltpu.VMEM)
    return pl.pallas_call(
        place_kernel,
        grid_spec=pltpu.PrefetchScalarGridSpec(
            num_scalar_prefetch=4, grid=(), in_specs=[vmem] * blocks, out_specs=vmem,
        ),
        out_shape=jax.ShapeDtypeStruct((cols, blocks, rows), F32),
        cost_estimate=cost(),
        compiler_params=params(),
        name="place_blocks",
    )(side, base, row_count, col_count, *mine, *other)


class Chain:
    def __init__(self):
        self.last = None

    def run(self, step, *args):
        if self.last is not None:
            args, _ = lax.optimization_barrier((args, self.last))
        result = step(*args)
        self.last = jax.tree.leaves(result)[0]
        return result


def local(inner, amplitudes, integrals, row_count, pair_count, col_count):
    blocks, depth, rows = amplitudes.shape
    all_cols = integrals.shape[0]
    tensor, rep = lax.axis_size("tensor"), lax.axis_size("rep")
    cols, row_local = all_cols // tensor, rows // rep
    me, side = lax.axis_index("tensor"), lax.axis_index("rep")
    z, x, core = me // (inner * CORES), me // CORES % inner, me % CORES
    place = jnp.stack([z, x, core]).astype(jnp.int32)

    pairs_here = lax.dynamic_slice_in_dim(pair_count, side * blocks, blocks) - me * depth
    rows_here = lax.dynamic_slice_in_dim(row_count, side * blocks, blocks)
    rows_here = jnp.where(pairs_here > 0, rows_here, 0)
    parts_of_b = integrals.reshape(all_cols, blocks, depth // LANES, LANES).transpose(0, 2, 1, 3)
    parts_of_b = parts_of_b.reshape(inner * OUTER, CORES, cols, blocks * depth // LANES, LANES)

    def index(z, x, core):
        return (z * inner + x) * CORES + core

    across = [(index(z, x, c), index(z, x, 1 - c))
              for z in range(OUTER) for x in range(inner) for c in range(CORES)]

    def along_inner(bit):
        return [(index(z, x, c), index(z, x ^ bit, c))
                for z in range(OUTER) for x in range(inner) for c in range(CORES)]

    def along_outer(bit):
        return [(index(z, x, c), index(z ^ bit, x, c))
                for z in range(OUTER) for x in range(inner) for c in range(CORES)]

    chain = Chain()
    received, split_in, totals, gens = {}, {}, {}, {}

    def run_products(chunks, shift, pieces, *got):
        return chain.run(
            lambda p, l, r, b, a, *g: products(p, l, r, b, a, chunks, shift, inner, pieces, g),
            place, pairs_here, rows_here, parts_of_b, amplitudes, *got,
        )

    def first_halves(names, pieces):
        sent = run_products([chunks[i] for i in names], 1, pieces)
        for i, count in zip(names, pieces):
            received[i] = [lax.ppermute(part, "tensor", across) for part in sent[:count]]
            sent = sent[count:]

    def second_halves(names):
        got = [part for i in names for part in received[i]]
        outs = run_products([chunks[i] for i in names], 0, [len(received[i]) for i in names], *got)
        for at, i in enumerate(names):
            gens[i] = work(*chunks[i], *outs[2 * at:2 * at + 2])

    def work(h, start, count, outer_first, keep, send):
        steps = [along_inner(1 << i) for i in range(inner.bit_length() - 1)]
        more = [along_outer(1 << i) for i in range(OUTER.bit_length() - 1)]
        for pairs in more + steps if outer_first else steps + more:
            got = lax.ppermute(send, "tensor", pairs)
            half = keep.shape[0] // 2
            if half < cols:
                total = chain.run(jnp.add, keep, got)
            else:
                keep, send = chain.run(
                    lambda a, b: (a[:half] + b[:half], a[half:] + b[half:]), keep, got
                )
            yield
        totals[h, start] = total

    mine, other = {}, {}

    def exchange(h):
        for i, chunk in enumerate(chunks):
            if chunk[0] == h:
                for _ in gens[i]:
                    pass
        if rep != 2:
            mine[h] = totals[h, 0]
            return
        if (h, row_local) in totals:
            first, second = totals[h, 0], totals[h, row_local]
        else:
            first, second = totals[h, 0][:, :row_local], totals[h, 0][:, row_local:]
        mine[h], away = chain.run(
            lambda a, b: (jnp.where(side == 0, a, b), jnp.where(side == 0, b, a)), first, second
        )
        other[h] = lax.ppermute(away, "rep", [(0, 1), (1, 0)])

    if inner == 2 and rep == 2 and blocks == 4:
        half = rows // 2
        chunks = [(0, 0, rows, False), (1, 0, half, True), (1, half, half, False),
                  (2, 0, rows, False), (3, 0, half, False), (3, half, half, False)]
        firsts = {"p": ([0, 1, 2], [2, 2, 2]), "q": ([3, 4, 5], [4, 2, 2])}
        seconds = {"w": [0], "x": [1, 2], "y": [3], "z": [4, 5]}
        plan = "pwxq01y21z020a3A21b4353cB45Cd"
    else:
        chunks = [(h, 0, rows, False) for h in range(blocks)]
        firsts = {"p": (list(range(blocks)), [2] * blocks)}
        seconds = {"w": list(range(blocks))}
        plan = "pw" + "abcdefgh"[:blocks]
    for move in plan:
        if move in firsts:
            first_halves(*firsts[move])
        elif move in seconds:
            second_halves(seconds[move])
        elif move in "ABCDEFGH":
            chain.last = chain.last, other["ABCDEFGH".index(move)]
        elif move in "abcdefgh":
            exchange("abcdefgh".index(move))
        else:
            next(gens[int(move)])

    if rep == 2:
        base = jnp.stack([me * cols, side * row_local]).astype(jnp.int32)
        return place_blocks(
            jnp.reshape(side, (1,)).astype(jnp.int32), base, row_count, col_count,
            [mine[h] for h in range(blocks)], [other[h] for h in range(blocks)],
        )
    arranged = lax.all_to_all(
        jnp.stack([mine[h] for h in range(blocks)], axis=1), "rep",
        split_axis=2, concat_axis=1, tiled=True,
    )
    col_index = me * cols + lax.broadcasted_iota(jnp.int32, (cols, 1, 1), 0)
    row_index = side * row_local + lax.broadcasted_iota(jnp.int32, (1, 1, row_local), 2)
    keep = (col_index < col_count[None, :, None]) & (row_index < row_count[None, :, None])
    return jnp.where(keep, arranged, F32(0.0))


def solution(mesh):
    inner = mesh.shape["tensor"] // (OUTER * CORES)
    in_specs = (P("rep", "tensor", None), P(None, "rep", "tensor"), P(), P(), P())
    out_specs = P("tensor", None, "rep")
    return jax.shard_map(
        functools.partial(local, inner), mesh=mesh, in_specs=in_specs, out_specs=out_specs,
        check_vma=False,
    )
```

```python
import functools

import jax
import jax.numpy as jnp
from jax import lax
from jax.experimental import pallas as pl
from jax.experimental.pallas import tpu as pltpu
from jax.sharding import PartitionSpec as P

OUTER = 4
CORES = 2
LANES = 128
TILE = 256
PIECES = 2
VMEM_BYTES = 40 * 1024 * 1024
F32 = jnp.float32
BF16 = jnp.bfloat16


def params():
    return pltpu.CompilerParams(vmem_limit_bytes=VMEM_BYTES)


def cost():
    return pl.CostEstimate(flops=1024, bytes_accessed=1024, transcendentals=0)


def split(value):
    high = value.astype(BF16)
    return high, (value - high.astype(F32)).astype(BF16)


def reversed_bits(value, count):
    result, bit = 0, 1
    while bit < count:
        result = 2 * result + (value // bit) % 2
        bit *= 2
    return result


def put_split(group, limit, first, b_ref, high_ref, low_ref, place):
    used = high_ref.shape[0]
    cols, depth = high_ref.shape[-2:]
    tiles = depth // LANES
    blocks = b_ref.shape[3] // tiles
    lane = lax.broadcasted_iota(jnp.int32, (1, LANES), 1)
    for h in range(used):
        rows = pl.ds(first + h, tiles, stride=blocks) if blocks > 1 else slice(None)
        turned = jnp.swapaxes(b_ref[group, 0, :, rows, :], 0, 1)
        for t in range(tiles):
            value = jnp.where(lane < limit[first + h] - t * LANES, turned[t], F32(0.0))
            high, low = split(value)
            high_ref[(h, *place, slice(None), slice(t * LANES, (t + 1) * LANES))] = high
            low_ref[(h, *place, slice(None), slice(t * LANES, (t + 1) * LANES))] = low


def slot(group, place, inner):
    x = reversed_bits((group % inner) ^ place[1], inner)
    z = reversed_bits((group // inner) ^ place[0], OUTER)
    return x * OUTER + z


def halves_put(total, outs, inner, cols, outer_first):
    groups = total.shape[0] // cols
    for x in range(inner):
        for z in range(groups // inner):
            row = (x * OUTER + z) * cols
            place = z * inner + x if outer_first else x * OUTER + z
            at = place % (groups // 2) * cols
            outs[place // (groups // 2)][at:at + cols, :] = total[row:row + cols]


def joined(refs):
    return jnp.concatenate([ref[...] for ref in refs], axis=0)


def dot3(left_high, left_low, a_ref):
    high, low = split(a_ref[0])
    dot = functools.partial(jnp.dot, preferred_element_type=F32)
    return dot(left_high, high) + (dot(left_high, low) + dot(left_low, high))


def products_kernel(first, inner, step, chunks, pieces, adds, place, limit, rows_live, b_ref, a_ref, *refs):
    received, outs, (high_ref, low_ref) = refs[:adds], refs[adds:-2], refs[-2:]
    tile = a_ref.shape[2]
    groups, cols, depth = high_ref.shape[1:]
    loads = groups // step
    now = pl.program_id(0)

    @pl.when(now < loads)
    def _():
        for i in range(step):
            group = now * step + i
            put_split(i, limit, first, b_ref, high_ref, low_ref, (slot(group, place, inner),))

    at = loads
    for h, start, count, outer_first in chunks:
        size = count // tile
        mine = (now >= at) & (now < at + size)
        live = start + (now - at) * tile < rows_live[h]
        got = received[(h - first) * pieces:(h - first + 1) * pieces]
        out, outs = outs[:2 if adds else pieces], outs[2 if adds else pieces:]

        def put(total):
            if adds:
                halves_put(total, out, inner, cols, outer_first)
                return
            part = total.shape[0] // pieces
            for i, ref in enumerate(out):
                ref[...] = total[i * part:(i + 1) * part]

        @pl.when(mine & live)
        def _():
            left = (r[h - first].reshape(groups * cols, depth) for r in (high_ref, low_ref))
            total = dot3(*left, a_ref)
            put(total + joined(got) if adds else total)

        @pl.when(mine & jnp.logical_not(live))
        def _():
            put(joined(got) if adds else jnp.zeros((groups * cols, tile), F32))

        at += size


def products(place, limit, rows_live, parts_of_b, amplitudes, chunks, shift, inner, received):
    groups, _, cols, rows_b, _ = parts_of_b.shape
    blocks, depth, rows = amplitudes.shape
    tile = min(rows, TILE)
    step = min(groups, 2)
    loads = groups // step
    first, last = chunks[0][0], chunks[-1][0]
    sizes = [chunk[2] // tile for chunk in chunks]
    offset = chunks[0][1] // tile
    total = sum(sizes)
    per_block = rows // tile
    height = groups * cols
    adds = bool(received)

    def b_map(n, place, *_):
        return (jnp.minimum(n, loads - 1), lax.rem(place[2] + shift, CORES), 0, 0, 0)

    def a_map(n, *_):
        t = jnp.maximum(n - loads, 0) + offset
        return (first + t // per_block, 0, t % per_block)

    def tiles_of(counts):
        result, at = [], 0
        for size, count in zip(sizes, counts):
            result += [pl.BlockSpec(
                (height // count, tile),
                lambda n, *_, at=at, size=size: (0, jnp.clip(n - loads - at, 0, size - 1)),
            )] * count
            at += size
        return result

    counts = [2 if adds else PIECES] * len(chunks)
    got_specs = []
    for h in range(first, last + 1) if adds else []:
        mine = [i for i, chunk in enumerate(chunks) if chunk[0] == h]
        at, size = sum(sizes[:mine[0]]), sum(sizes[i] for i in mine)
        begin = chunks[mine[0]][1] // tile
        got_specs += [pl.BlockSpec(
            (height // PIECES, tile),
            lambda n, *_, at=at, size=size, begin=begin: (0, begin + jnp.clip(n - loads - at, 0, size - 1)),
        )] * PIECES
    part = pltpu.VMEM((last - first + 1, groups, cols, depth), BF16)
    return pl.pallas_call(
        functools.partial(products_kernel, first, inner, step, chunks, PIECES, len(received)),
        grid_spec=pltpu.PrefetchScalarGridSpec(
            num_scalar_prefetch=3,
            grid=(loads + total,),
            in_specs=[pl.BlockSpec((step, 1, cols, rows_b, LANES), b_map),
                      pl.BlockSpec((1, depth, tile), a_map)] + got_specs,
            out_specs=tiles_of(counts),
            scratch_shapes=[part, part],
        ),
        out_shape=[jax.ShapeDtypeStruct((height // count, chunk[2]), F32)
                   for chunk, count in zip(chunks, counts) for _ in range(count)],
        cost_estimate=cost(),
        compiler_params=params(),
        name="second_halves" if adds else "first_halves",
    )(place, limit, rows_live, parts_of_b, amplitudes, *received)


def place_kernel(side_ref, base, row_count, col_count, *refs):
    *parts, out_ref = refs
    side = side_ref[0]
    blocks = len(parts) // 2
    cols, rows = parts[0].shape
    col = base[0] + lax.broadcasted_iota(jnp.int32, (cols, rows), 0)
    row = base[1] + lax.broadcasted_iota(jnp.int32, (cols, rows), 1)
    for here in range(2):
        @pl.when(side == here)
        def _():
            order = parts[blocks:] + parts[:blocks] if here else parts
            kept = [
                jnp.where((col < col_count[h]) & (row < row_count[h]), part[...], F32(0.0))
                for h, part in enumerate(order)
            ]
            out_ref[...] = jnp.swapaxes(jnp.stack(kept), 0, 1)


def place_blocks(side, base, row_count, col_count, mine, other):
    cols, rows = mine[0].shape
    blocks = 2 * len(mine)
    vmem = pl.BlockSpec(memory_space=pltpu.VMEM)
    return pl.pallas_call(
        place_kernel,
        grid_spec=pltpu.PrefetchScalarGridSpec(
            num_scalar_prefetch=4, grid=(), in_specs=[vmem] * blocks, out_specs=vmem,
        ),
        out_shape=jax.ShapeDtypeStruct((cols, blocks, rows), F32),
        cost_estimate=cost(),
        compiler_params=params(),
        name="place_blocks",
    )(side, base, row_count, col_count, *mine, *other)


class Chain:
    def __init__(self):
        self.last = None

    def run(self, step, *args):
        if self.last is not None:
            args, _ = lax.optimization_barrier((args, self.last))
        result = step(*args)
        self.last = jax.tree.leaves(result)[0]
        return result


def local(inner, amplitudes, integrals, row_count, pair_count, col_count):
    blocks, depth, rows = amplitudes.shape
    all_cols = integrals.shape[0]
    tensor, rep = lax.axis_size("tensor"), lax.axis_size("rep")
    cols, row_local = all_cols // tensor, rows // rep
    me, side = lax.axis_index("tensor"), lax.axis_index("rep")
    z, x, core = me // (inner * CORES), me // CORES % inner, me % CORES
    place = jnp.stack([z, x, core]).astype(jnp.int32)

    pairs_here = lax.dynamic_slice_in_dim(pair_count, side * blocks, blocks) - me * depth
    rows_here = lax.dynamic_slice_in_dim(row_count, side * blocks, blocks)
    rows_here = jnp.where(pairs_here > 0, rows_here, 0)
    parts_of_b = integrals.reshape(all_cols, blocks, depth // LANES, LANES).transpose(0, 2, 1, 3)
    parts_of_b = parts_of_b.reshape(inner * OUTER, CORES, cols, blocks * depth // LANES, LANES)

    def index(z, x, core):
        return (z * inner + x) * CORES + core

    across = [(index(z, x, c), index(z, x, 1 - c))
              for z in range(OUTER) for x in range(inner) for c in range(CORES)]

    def along_inner(bit):
        return [(index(z, x, c), index(z, x ^ bit, c))
                for z in range(OUTER) for x in range(inner) for c in range(CORES)]

    def along_outer(bit):
        return [(index(z, x, c), index(z ^ bit, x, c))
                for z in range(OUTER) for x in range(inner) for c in range(CORES)]

    chain = Chain()
    received, split_in, totals, gens = {}, {}, {}, {}

    def run_products(chunks, shift, *got):
        return chain.run(
            lambda p, l, r, b, a, *g: products(p, l, r, b, a, chunks, shift, inner, g),
            place, pairs_here, rows_here, parts_of_b, amplitudes, *got,
        )

    def first_halves(names):
        sent = run_products([(h, 0, rows, False) for h in names], 1)
        for i, h in enumerate(names):
            received[h] = [lax.ppermute(part, "tensor", across)
                           for part in sent[i * PIECES:(i + 1) * PIECES]]

    def second_halves(names):
        got = [part for h in sorted({chunks[i][0] for i in names}) for part in received[h]]
        outs = run_products([chunks[i] for i in names], 0, *got)
        for at, i in enumerate(names):
            gens[i] = work(*chunks[i], *outs[2 * at:2 * at + 2])

    def work(h, start, count, outer_first, keep, send):
        steps = [along_inner(1 << i) for i in range(inner.bit_length() - 1)]
        more = [along_outer(1 << i) for i in range(OUTER.bit_length() - 1)]
        for pairs in more + steps if outer_first else steps + more:
            got = lax.ppermute(send, "tensor", pairs)
            half = keep.shape[0] // 2
            if half < cols:
                total = chain.run(jnp.add, keep, got)
            else:
                keep, send = chain.run(
                    lambda a, b: (a[:half] + b[:half], a[half:] + b[half:]), keep, got
                )
            yield
        totals[h, start] = total

    mine, other = {}, {}

    def exchange(h):
        for i, chunk in enumerate(chunks):
            if chunk[0] == h:
                for _ in gens[i]:
                    pass
        if rep != 2:
            mine[h] = totals[h, 0]
            return
        if (h, row_local) in totals:
            first, second = totals[h, 0], totals[h, row_local]
        else:
            first, second = totals[h, 0][:, :row_local], totals[h, 0][:, row_local:]
        mine[h], away = chain.run(
            lambda a, b: (jnp.where(side == 0, a, b), jnp.where(side == 0, b, a)), first, second
        )
        other[h] = lax.ppermute(away, "rep", [(0, 1), (1, 0)])

    if inner == 2 and rep == 2 and blocks == 4:
        half = rows // 2
        chunks = [(0, 0, rows, False), (1, 0, rows, False), (2, 0, rows, False),
                  (3, 0, half, False), (3, half, half, False)]
        firsts = {"p": [0, 1], "q": [2, 3]}
        seconds = {"w": [0, 1], "z": [2, 3, 4]}
        plan = "pwq0z01a213Ab24B3c4Cd"
    else:
        chunks = [(h, 0, rows, False) for h in range(blocks)]
        firsts = {"p": list(range(blocks))}
        seconds = {"w": list(range(blocks))}
        plan = "pw" + "abcdefgh"[:blocks]
    for move in plan:
        if move in firsts:
            first_halves(firsts[move])
        elif move in seconds:
            second_halves(seconds[move])
        elif move in "ABCDEFGH":
            chain.last = chain.last, other["ABCDEFGH".index(move)]
        elif move in "abcdefgh":
            exchange("abcdefgh".index(move))
        else:
            next(gens[int(move)])

    if rep == 2:
        base = jnp.stack([me * cols, side * row_local]).astype(jnp.int32)
        return place_blocks(
            jnp.reshape(side, (1,)).astype(jnp.int32), base, row_count, col_count,
            [mine[h] for h in range(blocks)], [other[h] for h in range(blocks)],
        )
    arranged = lax.all_to_all(
        jnp.stack([mine[h] for h in range(blocks)], axis=1), "rep",
        split_axis=2, concat_axis=1, tiled=True,
    )
    col_index = me * cols + lax.broadcasted_iota(jnp.int32, (cols, 1, 1), 0)
    row_index = side * row_local + lax.broadcasted_iota(jnp.int32, (1, 1, row_local), 2)
    keep = (col_index < col_count[None, :, None]) & (row_index < row_count[None, :, None])
    return jnp.where(keep, arranged, F32(0.0))


def solution(mesh):
    inner = mesh.shape["tensor"] // (OUTER * CORES)
    in_specs = (P("rep", "tensor", None), P(None, "rep", "tensor"), P(), P(), P())
    out_specs = P("tensor", None, "rep")
    return jax.shard_map(
        functools.partial(local, inner), mesh=mesh, in_specs=in_specs, out_specs=out_specs,
        check_vma=False,
    )
```

```python
import functools

import jax
import jax.numpy as jnp
from jax import lax
from jax.experimental import pallas as pl
from jax.experimental.pallas import tpu as pltpu
from jax.sharding import PartitionSpec as P

OUTER = 4
CORES = 2
LANES = 128
TILE = 256
PIECES = 2
VMEM_BYTES = 44 * 1024 * 1024
F32 = jnp.float32
BF16 = jnp.bfloat16


def params():
    return pltpu.CompilerParams(vmem_limit_bytes=VMEM_BYTES)


def cost():
    return pl.CostEstimate(flops=1024, bytes_accessed=1024, transcendentals=0)


def split(value):
    high = value.astype(BF16)
    return high, (value - high.astype(F32)).astype(BF16)


def reversed_bits(value, count):
    result, bit = 0, 1
    while bit < count:
        result = 2 * result + (value // bit) % 2
        bit *= 2
    return result


def put_split(group, limit, first, b_ref, high_ref, low_ref, place):
    used = high_ref.shape[0]
    cols, depth = high_ref.shape[-2:]
    tiles = depth // LANES
    blocks = b_ref.shape[2] // tiles
    lane = lax.broadcasted_iota(jnp.int32, (1, LANES), 1)
    for h in range(used):
        rows = pl.ds(first + h, tiles, stride=blocks) if blocks > 1 else slice(None)
        turned = jnp.swapaxes(b_ref[group, :, rows, :], 0, 1)
        for t in range(tiles):
            value = jnp.where(lane < limit[first + h] - t * LANES, turned[t], F32(0.0))
            high, low = split(value)
            high_ref[(h, *place, slice(None), slice(t * LANES, (t + 1) * LANES))] = high
            low_ref[(h, *place, slice(None), slice(t * LANES, (t + 1) * LANES))] = low


def slot(group, place, inner):
    x = reversed_bits((group % inner) ^ place[1], inner)
    z = reversed_bits((group // inner) ^ place[0], OUTER)
    return x * OUTER + z


def dot3(left_high, left_low, a_ref):
    high, low = split(a_ref[...])
    dot = functools.partial(jnp.dot, preferred_element_type=F32)
    return dot(left_high, high) + (dot(left_high, low) + dot(left_low, high))


def products_kernel(first, inner, chunks, adds, place, limit, rows_live, b_hbm, a_hbm, *refs):
    received, (*outs, b_buf, a_buf, sums, high_ref, low_ref, b_sem, a_sem, in_sem, out_sem) = (
        refs[:adds], refs[adds:]
    )
    groups, cols, depth = high_ref.shape[1:]
    tile = a_buf.shape[2]
    height = groups * cols
    per_chunk = 2 if adds else PIECES
    side = lax.rem(place[2] + (0 if adds else 1), CORES)
    tiles = []
    at = 0
    for i, (h, start, count, outer_first) in enumerate(chunks):
        tiles.append((at, count // tile, h, start, outer_first, outs[i * per_chunk:(i + 1) * per_chunk]))
        at += count // tile

    def columns(n, start=0):
        return pl.ds(pl.multiple_of(start + n * tile, tile), tile)

    def load_b(g):
        return pltpu.make_async_copy(b_hbm.at[g, side], b_buf.at[g], b_sem.at[g])

    def load_a(at, n, h, start):
        return pltpu.make_async_copy(
            a_hbm.at[h, :, columns(n, start)], a_buf.at[at + n], a_sem.at[at + n]
        )

    def loads(at, n, h, start):
        part = height // PIECES
        return [pltpu.make_async_copy(
            received[(h - first) * PIECES + i].at[:, columns(n, start)],
            sums.at[at + n, pl.ds(i * part, part)], in_sem.at[at + n, i],
        ) for i in range(PIECES if adds else 0)]

    def stores(at, n, outer_first, out):
        copies = []
        part = height // len(out)
        pieces = groups if outer_first else len(out)
        for i in range(pieces):
            if outer_first:
                x, z = i // OUTER, i % OUTER
                to, row = divmod((z * inner + x) * cols, part)
            else:
                to, row = i, 0
            size = height // pieces
            copies.append(pltpu.make_async_copy(
                sums.at[at + n, pl.ds(i * size, size)],
                out[to].at[pl.ds(row, size), columns(n)], out_sem.at[at + n, i],
            ))
        return copies

    def live(n, h, start):
        return start + n * tile < rows_live[h]

    for g in range(groups):
        load_b(g).start()
    for at, count, h, start, _, _ in tiles:
        @pl.loop(0, count)
        def _(n):
            @pl.when(live(n, h, start))
            def _():
                load_a(at, n, h, start).start()
            for copy in loads(at, n, h, start):
                copy.start()

    @pl.loop(0, groups)
    def _(g):
        load_b(g).wait()
        put_split(g, limit, first, b_buf, high_ref, low_ref, (slot(g, place, inner),))

    for at, count, h, start, outer_first, out in tiles:
        @pl.loop(0, count)
        def _(n):
            for copy in loads(at, n, h, start):
                copy.wait()

            @pl.when(live(n, h, start))
            def _():
                load_a(at, n, h, start).wait()
                left = (r[h - first].reshape(height, depth) for r in (high_ref, low_ref))
                total = dot3(*left, a_buf.at[at + n])
                sums[at + n] = sums[at + n] + total if adds else total

            if not adds:
                @pl.when(jnp.logical_not(live(n, h, start)))
                def _():
                    sums[at + n] = jnp.zeros((height, tile), F32)

            for copy in stores(at, n, outer_first, out):
                copy.start()

    for at, count, _, _, outer_first, out in tiles:
        @pl.loop(0, count)
        def _(n):
            for copy in stores(at, n, outer_first, out):
                copy.wait()


def products(place, limit, rows_live, parts_of_b, amplitudes, chunks, inner, received):
    groups, _, cols, rows_b, _ = parts_of_b.shape
    blocks, depth, rows = amplitudes.shape
    tile = min(rows, TILE)
    first, last = chunks[0][0], chunks[-1][0]
    total = sum(chunk[2] for chunk in chunks) // tile
    height = groups * cols
    count = 2 if received else PIECES
    anywhere = pl.BlockSpec(memory_space=pl.ANY)
    part = pltpu.VMEM((last - first + 1, groups, cols, depth), BF16)
    return pl.pallas_call(
        functools.partial(products_kernel, first, inner, chunks, len(received)),
        grid_spec=pltpu.PrefetchScalarGridSpec(
            num_scalar_prefetch=3,
            grid=(),
            in_specs=[anywhere] * (2 + len(received)),
            out_specs=[anywhere] * (count * len(chunks)),
            scratch_shapes=[
                pltpu.VMEM((groups, cols, rows_b, LANES), F32),
                pltpu.VMEM((total, depth, tile), F32),
                pltpu.VMEM((total, height, tile), F32),
                part,
                part,
                pltpu.SemaphoreType.DMA((groups,)),
                pltpu.SemaphoreType.DMA((total,)),
                pltpu.SemaphoreType.DMA((total, PIECES)),
                pltpu.SemaphoreType.DMA((total, groups)),
            ],
        ),
        out_shape=[jax.ShapeDtypeStruct((height // count, chunk[2]), F32)
                   for chunk in chunks for _ in range(count)],
        cost_estimate=cost(),
        compiler_params=params(),
        name="second_halves" if received else "first_halves",
    )(place, limit, rows_live, parts_of_b, amplitudes, *received)


def place_kernel(side_ref, base, row_count, col_count, *refs):
    *parts, out_ref = refs
    side = side_ref[0]
    blocks = len(parts) // 2
    cols, rows = parts[0].shape
    col = base[0] + lax.broadcasted_iota(jnp.int32, (cols, rows), 0)
    row = base[1] + lax.broadcasted_iota(jnp.int32, (cols, rows), 1)
    for here in range(2):
        @pl.when(side == here)
        def _():
            order = parts[blocks:] + parts[:blocks] if here else parts
            kept = [
                jnp.where((col < col_count[h]) & (row < row_count[h]), part[...], F32(0.0))
                for h, part in enumerate(order)
            ]
            out_ref[...] = jnp.swapaxes(jnp.stack(kept), 0, 1)


def place_blocks(side, base, row_count, col_count, mine, other):
    cols, rows = mine[0].shape
    blocks = 2 * len(mine)
    vmem = pl.BlockSpec(memory_space=pltpu.VMEM)
    return pl.pallas_call(
        place_kernel,
        grid_spec=pltpu.PrefetchScalarGridSpec(
            num_scalar_prefetch=4, grid=(), in_specs=[vmem] * blocks, out_specs=vmem,
        ),
        out_shape=jax.ShapeDtypeStruct((cols, blocks, rows), F32),
        cost_estimate=cost(),
        compiler_params=params(),
        name="place_blocks",
    )(side, base, row_count, col_count, *mine, *other)


class Chain:
    def __init__(self):
        self.last = None

    def run(self, step, *args):
        if self.last is not None:
            args, _ = lax.optimization_barrier((args, self.last))
        result = step(*args)
        self.last = jax.tree.leaves(result)[0]
        return result


def local(inner, amplitudes, integrals, row_count, pair_count, col_count):
    blocks, depth, rows = amplitudes.shape
    all_cols = integrals.shape[0]
    tensor, rep = lax.axis_size("tensor"), lax.axis_size("rep")
    cols, row_local = all_cols // tensor, rows // rep
    me, side = lax.axis_index("tensor"), lax.axis_index("rep")
    z, x, core = me // (inner * CORES), me // CORES % inner, me % CORES
    place = jnp.stack([z, x, core]).astype(jnp.int32)

    pairs_here = lax.dynamic_slice_in_dim(pair_count, side * blocks, blocks) - me * depth
    rows_here = lax.dynamic_slice_in_dim(row_count, side * blocks, blocks)
    rows_here = jnp.where(pairs_here > 0, rows_here, 0)
    parts_of_b = integrals.reshape(all_cols, blocks, depth // LANES, LANES).transpose(0, 2, 1, 3)
    parts_of_b = parts_of_b.reshape(inner * OUTER, CORES, cols, blocks * depth // LANES, LANES)

    def index(z, x, core):
        return (z * inner + x) * CORES + core

    across = [(index(z, x, c), index(z, x, 1 - c))
              for z in range(OUTER) for x in range(inner) for c in range(CORES)]

    def along_inner(bit):
        return [(index(z, x, c), index(z, x ^ bit, c))
                for z in range(OUTER) for x in range(inner) for c in range(CORES)]

    def along_outer(bit):
        return [(index(z, x, c), index(z ^ bit, x, c))
                for z in range(OUTER) for x in range(inner) for c in range(CORES)]

    chain = Chain()
    received, split_in, totals, gens = {}, {}, {}, {}

    def run_products(chunks, *got):
        return chain.run(
            lambda p, l, r, b, a, *g: products(p, l, r, b, a, chunks, inner, g),
            place, pairs_here, rows_here, parts_of_b, amplitudes, *got,
        )

    def first_halves(names):
        sent = run_products([(h, 0, rows, False) for h in names])
        for i, h in enumerate(names):
            received[h] = [lax.ppermute(part, "tensor", across)
                           for part in sent[i * PIECES:(i + 1) * PIECES]]

    def second_halves(names):
        got = [part for h in sorted({chunks[i][0] for i in names}) for part in received[h]]
        outs = run_products([chunks[i] for i in names], *got)
        for at, i in enumerate(names):
            gens[i] = work(*chunks[i], *outs[2 * at:2 * at + 2])

    def work(h, start, count, outer_first, keep, send):
        steps = [along_inner(1 << i) for i in range(inner.bit_length() - 1)]
        more = [along_outer(1 << i) for i in range(OUTER.bit_length() - 1)]
        for pairs in more + steps if outer_first else steps + more:
            got = lax.ppermute(send, "tensor", pairs)
            half = keep.shape[0] // 2
            if half < cols:
                total = chain.run(jnp.add, keep, got)
            else:
                keep, send = chain.run(
                    lambda a, b: (a[:half] + b[:half], a[half:] + b[half:]), keep, got
                )
            yield
        totals[h, start] = total

    mine, other = {}, {}

    def exchange(h):
        for i, chunk in enumerate(chunks):
            if chunk[0] == h:
                for _ in gens[i]:
                    pass
        if rep != 2:
            mine[h] = totals[h, 0]
            return
        if (h, row_local) in totals:
            first, second = totals[h, 0], totals[h, row_local]
        else:
            first, second = totals[h, 0][:, :row_local], totals[h, 0][:, row_local:]
        mine[h], away = chain.run(
            lambda a, b: (jnp.where(side == 0, a, b), jnp.where(side == 0, b, a)), first, second
        )
        other[h] = lax.ppermute(away, "rep", [(0, 1), (1, 0)])

    if inner == 2 and rep == 2 and blocks == 4:
        half = rows // 2
        chunks = [(0, 0, rows, False), (1, 0, rows, False), (2, 0, rows, False),
                  (3, 0, half, True), (3, half, half, False)]
        firsts = {"p": [0, 1], "q": [2, 3]}
        seconds = {"w": [0], "x": [1], "z": [2, 3, 4]}
        plan = "pwxq0z013a132A42bB4cCd"
    else:
        chunks = [(h, 0, rows, False) for h in range(blocks)]
        firsts = {"p": list(range(blocks))}
        seconds = {"w": list(range(blocks))}
        plan = "pw" + "abcdefgh"[:blocks]
    for move in plan:
        if move in firsts:
            first_halves(firsts[move])
        elif move in seconds:
            second_halves(seconds[move])
        elif move in "ABCDEFGH":
            chain.last = chain.last, other["ABCDEFGH".index(move)]
        elif move in "abcdefgh":
            exchange("abcdefgh".index(move))
        else:
            next(gens[int(move)])

    if rep == 2:
        base = jnp.stack([me * cols, side * row_local]).astype(jnp.int32)
        return place_blocks(
            jnp.reshape(side, (1,)).astype(jnp.int32), base, row_count, col_count,
            [mine[h] for h in range(blocks)], [other[h] for h in range(blocks)],
        )
    arranged = lax.all_to_all(
        jnp.stack([mine[h] for h in range(blocks)], axis=1), "rep",
        split_axis=2, concat_axis=1, tiled=True,
    )
    col_index = me * cols + lax.broadcasted_iota(jnp.int32, (cols, 1, 1), 0)
    row_index = side * row_local + lax.broadcasted_iota(jnp.int32, (1, 1, row_local), 2)
    keep = (col_index < col_count[None, :, None]) & (row_index < row_count[None, :, None])
    return jnp.where(keep, arranged, F32(0.0))


def solution(mesh):
    inner = mesh.shape["tensor"] // (OUTER * CORES)
    in_specs = (P("rep", "tensor", None), P(None, "rep", "tensor"), P(), P(), P())
    out_specs = P("tensor", None, "rep")
    return jax.shard_map(
        functools.partial(local, inner), mesh=mesh, in_specs=in_specs, out_specs=out_specs,
        check_vma=False,
    )
```

```python
import functools

import jax
import jax.numpy as jnp
from jax import lax
from jax.experimental import pallas as pl
from jax.experimental.pallas import tpu as pltpu
from jax.sharding import PartitionSpec as P

OUTER = 4
CORES = 2
LANES = 128
TILE = 256
PIECES = 2
VMEM_BYTES = 44 * 1024 * 1024
F32 = jnp.float32
BF16 = jnp.bfloat16


def params():
    return pltpu.CompilerParams(vmem_limit_bytes=VMEM_BYTES)


def cost():
    return pl.CostEstimate(flops=1024, bytes_accessed=1024, transcendentals=0)


def split(value):
    high = value.astype(BF16)
    return high, (value - high.astype(F32)).astype(BF16)


def reversed_bits(value, count):
    result, bit = 0, 1
    while bit < count:
        result = 2 * result + (value // bit) % 2
        bit *= 2
    return result


def put_split(group, limit, first, b_ref, high_ref, low_ref, place):
    used = high_ref.shape[0]
    cols, depth = high_ref.shape[-2:]
    tiles = depth // LANES
    blocks = b_ref.shape[2] // tiles
    lane = lax.broadcasted_iota(jnp.int32, (1, LANES), 1)
    for h in range(used):
        rows = pl.ds(first + h, tiles, stride=blocks) if blocks > 1 else slice(None)
        turned = jnp.swapaxes(b_ref[group, :, rows, :], 0, 1)
        for t in range(tiles):
            value = jnp.where(lane < limit[first + h] - t * LANES, turned[t], F32(0.0))
            high, low = split(value)
            high_ref[(h, *place, slice(None), slice(t * LANES, (t + 1) * LANES))] = high
            low_ref[(h, *place, slice(None), slice(t * LANES, (t + 1) * LANES))] = low


def slot(group, place, inner):
    x = reversed_bits((group % inner) ^ place[1], inner)
    z = reversed_bits((group // inner) ^ place[0], OUTER)
    return x * OUTER + z


def dot3(left_high, left_low, a_ref):
    high, low = split(a_ref[...])
    dot = functools.partial(jnp.dot, preferred_element_type=F32)
    return dot(left_high, high) + (dot(left_high, low) + dot(left_low, high))


def products_kernel(first, inner, chunks, adds, place, limit, rows_live, b_hbm, a_hbm, *refs):
    received, (*outs, b_buf, a_buf, sums, high_ref, low_ref, b_sem, a_sem, in_sem, out_sem) = (
        refs[:adds], refs[adds:]
    )
    groups, cols, depth = high_ref.shape[1:]
    tile = a_buf.shape[2]
    height = groups * cols
    per_chunk = 2 if adds else PIECES
    side = lax.rem(place[2] + (0 if adds else 1), CORES)
    tiles = []
    at = 0
    for i, (h, start, count, outer_first) in enumerate(chunks):
        tiles.append((at, count // tile, h, start, outer_first, outs[i * per_chunk:(i + 1) * per_chunk]))
        at += count // tile

    def columns(n, start=0):
        return pl.ds(pl.multiple_of(start + n * tile, tile), tile)

    def load_b(g):
        return pltpu.make_async_copy(b_hbm.at[g, side], b_buf.at[g], b_sem.at[g])

    def load_a(at, n, h, start):
        return pltpu.make_async_copy(
            a_hbm.at[h, :, columns(n, start)], a_buf.at[at + n], a_sem.at[at + n]
        )

    def loads(at, n, h, start):
        part = height // PIECES
        return [pltpu.make_async_copy(
            received[(h - first) * PIECES + i].at[:, columns(n, start)],
            sums.at[at + n, pl.ds(i * part, part)], in_sem.at[at + n, i],
        ) for i in range(PIECES if adds else 0)]

    def stores(at, n, outer_first, out):
        copies = []
        part = height // len(out)
        pieces = groups if outer_first else len(out)
        for i in range(pieces):
            if outer_first:
                x, z = i // OUTER, i % OUTER
                to, row = divmod((z * inner + x) * cols, part)
            else:
                to, row = i, 0
            size = height // pieces
            copies.append(pltpu.make_async_copy(
                sums.at[at + n, pl.ds(i * size, size)],
                out[to].at[pl.ds(row, size), columns(n)], out_sem.at[at + n, i],
            ))
        return copies

    def live(n, h, start):
        return start + n * tile < rows_live[h]

    for g in range(groups):
        load_b(g).start()
    for at, count, h, start, _, _ in tiles:
        @pl.loop(0, count)
        def _(n):
            @pl.when(live(n, h, start))
            def _():
                load_a(at, n, h, start).start()
            for copy in loads(at, n, h, start):
                copy.start()

    @pl.loop(0, groups)
    def _(g):
        load_b(g).wait()
        put_split(g, limit, first, b_buf, high_ref, low_ref, (slot(g, place, inner),))

    for at, count, h, start, outer_first, out in tiles:
        @pl.loop(0, count)
        def _(n):
            for copy in loads(at, n, h, start):
                copy.wait()

            @pl.when(live(n, h, start))
            def _():
                load_a(at, n, h, start).wait()
                left = (r[h - first].reshape(height, depth) for r in (high_ref, low_ref))
                total = dot3(*left, a_buf.at[at + n])
                sums[at + n] = sums[at + n] + total if adds else total

            if not adds:
                @pl.when(jnp.logical_not(live(n, h, start)))
                def _():
                    sums[at + n] = jnp.zeros((height, tile), F32)

            for copy in stores(at, n, outer_first, out):
                copy.start()

    for at, count, _, _, outer_first, out in tiles:
        @pl.loop(0, count)
        def _(n):
            for copy in stores(at, n, outer_first, out):
                copy.wait()


def products(place, limit, rows_live, parts_of_b, amplitudes, chunks, inner, received):
    groups, _, cols, rows_b, _ = parts_of_b.shape
    blocks, depth, rows = amplitudes.shape
    tile = min(rows, TILE)
    first, last = chunks[0][0], chunks[-1][0]
    total = sum(chunk[2] for chunk in chunks) // tile
    height = groups * cols
    count = 2 if received else PIECES
    anywhere = pl.BlockSpec(memory_space=pl.ANY)
    part = pltpu.VMEM((last - first + 1, groups, cols, depth), BF16)
    return pl.pallas_call(
        functools.partial(products_kernel, first, inner, chunks, len(received)),
        grid_spec=pltpu.PrefetchScalarGridSpec(
            num_scalar_prefetch=3,
            grid=(),
            in_specs=[anywhere] * (2 + len(received)),
            out_specs=[anywhere] * (count * len(chunks)),
            scratch_shapes=[
                pltpu.VMEM((groups, cols, rows_b, LANES), F32),
                pltpu.VMEM((total, depth, tile), F32),
                pltpu.VMEM((total, height, tile), F32),
                part,
                part,
                pltpu.SemaphoreType.DMA((groups,)),
                pltpu.SemaphoreType.DMA((total,)),
                pltpu.SemaphoreType.DMA((total, PIECES)),
                pltpu.SemaphoreType.DMA((total, groups)),
            ],
        ),
        out_shape=[jax.ShapeDtypeStruct((height // count, chunk[2]), F32)
                   for chunk in chunks for _ in range(count)],
        cost_estimate=cost(),
        compiler_params=params(),
        name="second_halves" if received else "first_halves",
    )(place, limit, rows_live, parts_of_b, amplitudes, *received)


def place_kernel(side_ref, base, row_count, col_count, *refs):
    *parts, out_ref = refs
    side = side_ref[0]
    blocks = len(parts) // 2
    cols, rows = parts[0].shape
    col = base[0] + lax.broadcasted_iota(jnp.int32, (cols, rows), 0)
    row = base[1] + lax.broadcasted_iota(jnp.int32, (cols, rows), 1)
    for here in range(2):
        @pl.when(side == here)
        def _():
            order = parts[blocks:] + parts[:blocks] if here else parts
            kept = [
                jnp.where((col < col_count[h]) & (row < row_count[h]), part[...], F32(0.0))
                for h, part in enumerate(order)
            ]
            out_ref[...] = jnp.swapaxes(jnp.stack(kept), 0, 1)


def place_blocks(side, base, row_count, col_count, mine, other):
    cols, rows = mine[0].shape
    blocks = 2 * len(mine)
    vmem = pl.BlockSpec(memory_space=pltpu.VMEM)
    return pl.pallas_call(
        place_kernel,
        grid_spec=pltpu.PrefetchScalarGridSpec(
            num_scalar_prefetch=4, grid=(), in_specs=[vmem] * blocks, out_specs=vmem,
        ),
        out_shape=jax.ShapeDtypeStruct((cols, blocks, rows), F32),
        cost_estimate=cost(),
        compiler_params=params(),
        name="place_blocks",
    )(side, base, row_count, col_count, *mine, *other)


class Chain:
    def __init__(self):
        self.last = None

    def run(self, step, *args):
        if self.last is not None:
            args, _ = lax.optimization_barrier((args, self.last))
        result = step(*args)
        self.last = jax.tree.leaves(result)[0]
        return result


def local(inner, amplitudes, integrals, row_count, pair_count, col_count):
    blocks, depth, rows = amplitudes.shape
    all_cols = integrals.shape[0]
    tensor, rep = lax.axis_size("tensor"), lax.axis_size("rep")
    cols, row_local = all_cols // tensor, rows // rep
    me, side = lax.axis_index("tensor"), lax.axis_index("rep")
    z, x, core = me // (inner * CORES), me // CORES % inner, me % CORES
    place = jnp.stack([z, x, core]).astype(jnp.int32)

    pairs_here = lax.dynamic_slice_in_dim(pair_count, side * blocks, blocks) - me * depth
    rows_here = lax.dynamic_slice_in_dim(row_count, side * blocks, blocks)
    rows_here = jnp.where(pairs_here > 0, rows_here, 0)
    parts_of_b = integrals.reshape(all_cols, blocks, depth // LANES, LANES).transpose(0, 2, 1, 3)
    parts_of_b = parts_of_b.reshape(inner * OUTER, CORES, cols, blocks * depth // LANES, LANES)

    def index(z, x, core):
        return (z * inner + x) * CORES + core

    across = [(index(z, x, c), index(z, x, 1 - c))
              for z in range(OUTER) for x in range(inner) for c in range(CORES)]

    def along_inner(bit):
        return [(index(z, x, c), index(z, x ^ bit, c))
                for z in range(OUTER) for x in range(inner) for c in range(CORES)]

    def along_outer(bit):
        return [(index(z, x, c), index(z ^ bit, x, c))
                for z in range(OUTER) for x in range(inner) for c in range(CORES)]

    chain = Chain()
    received, totals, gens = {}, {}, {}

    def run_products(chunks, *got):
        return chain.run(
            lambda p, l, r, b, a, *g: products(p, l, r, b, a, chunks, inner, g),
            place, pairs_here, rows_here, parts_of_b, amplitudes, *got,
        )

    def first_halves(names):
        sent = run_products([(h, 0, rows, False) for h in names])
        for i, h in enumerate(names):
            received[h] = [lax.ppermute(part, "tensor", across)
                           for part in sent[i * PIECES:(i + 1) * PIECES]]

    def second_halves(names):
        got = [part for h in sorted({chunks[i][0] for i in names}) for part in received[h]]
        outs = run_products([chunks[i] for i in names], *got)
        for at, i in enumerate(names):
            gens[i] = work(*chunks[i], *outs[2 * at:2 * at + 2])

    def work(h, start, count, outer_first, keep, send):
        steps = [along_inner(1 << i) for i in range(inner.bit_length() - 1)]
        more = [along_outer(1 << i) for i in range(OUTER.bit_length() - 1)]
        for pairs in more + steps if outer_first else steps + more:
            got = lax.ppermute(send, "tensor", pairs)
            half = keep.shape[0] // 2
            if half < cols:
                totals[h, start] = chain.run(jnp.add, keep, got)
            else:
                keep, send = chain.run(
                    lambda a, b: (a[:half] + b[:half], a[half:] + b[half:]), keep, got
                )
            yield

    mine, other, arriving = {}, {}, []

    def exchange(group):
        if rep != 2:
            for h in group:
                mine[h] = totals[h, 0]
            return
        pairs = []
        for h in group:
            if (h, row_local) in totals:
                pairs.append((totals[h, 0], totals[h, row_local]))
            else:
                pairs.append((totals[h, 0][:, :row_local], totals[h, 0][:, row_local:]))

        def choose(pairs):
            kept = [jnp.where(side == 0, a, b) for a, b in pairs]
            return kept, jnp.concatenate([jnp.where(side == 0, b, a) for a, b in pairs])

        kept, away = chain.run(choose, pairs)
        got = lax.ppermute(away, "rep", [(0, 1), (1, 0)])
        for i, h in enumerate(group):
            mine[h], other[h] = kept[i], got[i * cols:(i + 1) * cols]
        arriving.append(got)

    if inner == 2 and rep == 2 and blocks == 4:
        half = rows // 2
        chunks = [(0, 0, rows, False), (1, 0, rows, False), (2, 0, rows, False),
                  (3, 0, half, False), (3, half, half, False)]
        firsts = {"p": [0, 1], "q": [2, 3]}
        seconds = {"w": [0], "x": [1], "y": [2], "z": [3, 4]}
        groups = {"a": [0, 1, 2], "d": [3]}
        plan = "pwxq0y0z1012132432a434Ad"
    else:
        chunks = [(h, 0, rows, False) for h in range(blocks)]
        firsts = {"p": list(range(blocks))}
        seconds = {"w": list(range(blocks))}
        groups = {"a": list(range(blocks))}
        steps = (inner * OUTER).bit_length() - 1
        plan = "pw" + "".join(str(h) * steps for h in range(blocks)) + "a"
    for move in plan:
        if move in firsts:
            first_halves(firsts[move])
        elif move in seconds:
            second_halves(seconds[move])
        elif move == "A":
            chain.last = chain.last, arriving[-1]
        elif move in groups:
            exchange(groups[move])
        else:
            next(gens[int(move)])

    if rep == 2:
        base = jnp.stack([me * cols, side * row_local]).astype(jnp.int32)
        return place_blocks(
            jnp.reshape(side, (1,)).astype(jnp.int32), base, row_count, col_count,
            [mine[h] for h in range(blocks)], [other[h] for h in range(blocks)],
        )
    arranged = lax.all_to_all(
        jnp.stack([mine[h] for h in range(blocks)], axis=1), "rep",
        split_axis=2, concat_axis=1, tiled=True,
    )
    col_index = me * cols + lax.broadcasted_iota(jnp.int32, (cols, 1, 1), 0)
    row_index = side * row_local + lax.broadcasted_iota(jnp.int32, (1, 1, row_local), 2)
    keep = (col_index < col_count[None, :, None]) & (row_index < row_count[None, :, None])
    return jnp.where(keep, arranged, F32(0.0))


def solution(mesh):
    inner = mesh.shape["tensor"] // (OUTER * CORES)
    in_specs = (P("rep", "tensor", None), P(None, "rep", "tensor"), P(), P(), P())
    out_specs = P("tensor", None, "rep")
    return jax.shard_map(
        functools.partial(local, inner), mesh=mesh, in_specs=in_specs, out_specs=out_specs,
        check_vma=False,
    )
```

```python
import functools

import jax
import jax.numpy as jnp
from jax import lax
from jax.experimental import pallas as pl
from jax.experimental.pallas import tpu as pltpu
from jax.sharding import PartitionSpec as P

OUTER = 4
CORES = 2
LANES = 128
TILE = 256
PIECES = 2
VMEM_BYTES = 44 * 1024 * 1024
F32 = jnp.float32
BF16 = jnp.bfloat16


def params():
    return pltpu.CompilerParams(vmem_limit_bytes=VMEM_BYTES)


def cost():
    return pl.CostEstimate(flops=1024, bytes_accessed=1024, transcendentals=0)


def split(value):
    high = value.astype(BF16)
    return high, (value - high.astype(F32)).astype(BF16)


def reversed_bits(value, count):
    result, bit = 0, 1
    while bit < count:
        result = 2 * result + (value // bit) % 2
        bit *= 2
    return result


def put_split(group, limit, first, b_ref, high_ref, low_ref, place):
    used = high_ref.shape[0]
    cols, depth = high_ref.shape[-2:]
    tiles = depth // LANES
    blocks = b_ref.shape[2] // tiles
    lane = lax.broadcasted_iota(jnp.int32, (1, LANES), 1)
    for h in range(used):
        rows = pl.ds(first + h, tiles, stride=blocks) if blocks > 1 else slice(None)
        turned = jnp.swapaxes(b_ref[group, :, rows, :], 0, 1)
        for t in range(tiles):
            value = jnp.where(lane < limit[first + h] - t * LANES, turned[t], F32(0.0))
            high, low = split(value)
            high_ref[(h, *place, slice(None), slice(t * LANES, (t + 1) * LANES))] = high
            low_ref[(h, *place, slice(None), slice(t * LANES, (t + 1) * LANES))] = low


def slot(group, place, inner):
    x = reversed_bits((group % inner) ^ place[1], inner)
    z = reversed_bits((group // inner) ^ place[0], OUTER)
    return x * OUTER + z


def dot3(left_high, left_low, a_ref):
    high, low = split(a_ref[...])
    dot = functools.partial(jnp.dot, preferred_element_type=F32)
    return dot(left_high, high) + (dot(left_high, low) + dot(left_low, high))


def products_kernel(first, inner, chunks, adds, place, limit, rows_live, b_hbm, a_hbm, *refs):
    received, (*outs, b_buf, a_buf, sums, high_ref, low_ref, b_sem, a_sem, in_sem, out_sem) = (
        refs[:adds], refs[adds:]
    )
    groups, cols, depth = high_ref.shape[1:]
    tile = a_buf.shape[2]
    height = groups * cols
    per_chunk = 2 if adds else PIECES
    side = lax.rem(place[2] + (0 if adds else 1), CORES)
    tiles = []
    at = 0
    for i, (h, start, count, outer_first) in enumerate(chunks):
        tiles.append((at, count // tile, h, start, outer_first, outs[i * per_chunk:(i + 1) * per_chunk]))
        at += count // tile

    def columns(n, start=0):
        return pl.ds(pl.multiple_of(start + n * tile, tile), tile)

    def load_b(g):
        return pltpu.make_async_copy(b_hbm.at[g, side], b_buf.at[g], b_sem.at[g])

    def load_a(at, n, h, start):
        return pltpu.make_async_copy(
            a_hbm.at[h, :, columns(n, start)], a_buf.at[at + n], a_sem.at[at + n]
        )

    def loads(at, n, h, start):
        part = height // PIECES
        return [pltpu.make_async_copy(
            received[(h - first) * PIECES + i].at[:, columns(n, start)],
            sums.at[at + n, pl.ds(i * part, part)], in_sem.at[at + n, i],
        ) for i in range(PIECES if adds else 0)]

    def stores(at, n, outer_first, out):
        copies = []
        part = height // len(out)
        pieces = groups if outer_first else len(out)
        for i in range(pieces):
            if outer_first:
                x, z = i // OUTER, i % OUTER
                to, row = divmod((z * inner + x) * cols, part)
            else:
                to, row = i, 0
            size = height // pieces
            copies.append(pltpu.make_async_copy(
                sums.at[at + n, pl.ds(i * size, size)],
                out[to].at[pl.ds(row, size), columns(n)], out_sem.at[at + n, i],
            ))
        return copies

    def live(n, h, start):
        return start + n * tile < rows_live[h]

    for g in range(groups):
        load_b(g).start()
    for at, count, h, start, _, _ in tiles:
        @pl.loop(0, count)
        def _(n):
            @pl.when(live(n, h, start))
            def _():
                load_a(at, n, h, start).start()
            for copy in loads(at, n, h, start):
                copy.start()

    @pl.loop(0, groups)
    def _(g):
        load_b(g).wait()
        put_split(g, limit, first, b_buf, high_ref, low_ref, (slot(g, place, inner),))

    for at, count, h, start, outer_first, out in tiles:
        @pl.loop(0, count)
        def _(n):
            for copy in loads(at, n, h, start):
                copy.wait()

            @pl.when(live(n, h, start))
            def _():
                load_a(at, n, h, start).wait()
                left = (r[h - first].reshape(height, depth) for r in (high_ref, low_ref))
                total = dot3(*left, a_buf.at[at + n])
                sums[at + n] = sums[at + n] + total if adds else total

            if not adds:
                @pl.when(jnp.logical_not(live(n, h, start)))
                def _():
                    sums[at + n] = jnp.zeros((height, tile), F32)

            for copy in stores(at, n, outer_first, out):
                copy.start()

    for at, count, _, _, outer_first, out in tiles:
        @pl.loop(0, count)
        def _(n):
            for copy in stores(at, n, outer_first, out):
                copy.wait()


def products(place, limit, rows_live, parts_of_b, amplitudes, chunks, inner, received):
    groups, _, cols, rows_b, _ = parts_of_b.shape
    blocks, depth, rows = amplitudes.shape
    tile = min(rows, TILE)
    first, last = chunks[0][0], chunks[-1][0]
    total = sum(chunk[2] for chunk in chunks) // tile
    height = groups * cols
    count = 2 if received else PIECES
    anywhere = pl.BlockSpec(memory_space=pl.ANY)
    part = pltpu.VMEM((last - first + 1, groups, cols, depth), BF16)
    return pl.pallas_call(
        functools.partial(products_kernel, first, inner, chunks, len(received)),
        grid_spec=pltpu.PrefetchScalarGridSpec(
            num_scalar_prefetch=3,
            grid=(),
            in_specs=[anywhere] * (2 + len(received)),
            out_specs=[anywhere] * (count * len(chunks)),
            scratch_shapes=[
                pltpu.VMEM((groups, cols, rows_b, LANES), F32),
                pltpu.VMEM((total, depth, tile), F32),
                pltpu.VMEM((total, height, tile), F32),
                part,
                part,
                pltpu.SemaphoreType.DMA((groups,)),
                pltpu.SemaphoreType.DMA((total,)),
                pltpu.SemaphoreType.DMA((total, PIECES)),
                pltpu.SemaphoreType.DMA((total, groups)),
            ],
        ),
        out_shape=[jax.ShapeDtypeStruct((height // count, chunk[2]), F32)
                   for chunk in chunks for _ in range(count)],
        cost_estimate=cost(),
        compiler_params=params(),
        name="second_halves" if received else "first_halves",
    )(place, limit, rows_live, parts_of_b, amplitudes, *received)


def place_kernel(side_ref, base, row_count, col_count, *refs):
    *parts, out_ref = refs
    side = side_ref[0]
    blocks = len(parts) // 2
    cols, rows = parts[0].shape
    col = base[0] + lax.broadcasted_iota(jnp.int32, (cols, rows), 0)
    row = base[1] + lax.broadcasted_iota(jnp.int32, (cols, rows), 1)
    for here in range(2):
        @pl.when(side == here)
        def _():
            order = parts[blocks:] + parts[:blocks] if here else parts
            kept = [
                jnp.where((col < col_count[h]) & (row < row_count[h]), part[...], F32(0.0))
                for h, part in enumerate(order)
            ]
            out_ref[...] = jnp.swapaxes(jnp.stack(kept), 0, 1)


def place_blocks(side, base, row_count, col_count, mine, other):
    cols, rows = mine[0].shape
    blocks = 2 * len(mine)
    vmem = pl.BlockSpec(memory_space=pltpu.VMEM)
    return pl.pallas_call(
        place_kernel,
        grid_spec=pltpu.PrefetchScalarGridSpec(
            num_scalar_prefetch=4, grid=(), in_specs=[vmem] * blocks, out_specs=vmem,
        ),
        out_shape=jax.ShapeDtypeStruct((cols, blocks, rows), F32),
        cost_estimate=cost(),
        compiler_params=params(),
        name="place_blocks",
    )(side, base, row_count, col_count, *mine, *other)


class Chain:
    def __init__(self):
        self.last = None

    def run(self, step, *args):
        if self.last is not None:
            args, _ = lax.optimization_barrier((args, self.last))
        result = step(*args)
        self.last = jax.tree.leaves(result)[0]
        return result


def local(inner, amplitudes, integrals, row_count, pair_count, col_count):
    blocks, depth, rows = amplitudes.shape
    all_cols = integrals.shape[0]
    tensor, rep = lax.axis_size("tensor"), lax.axis_size("rep")
    cols, row_local = all_cols // tensor, rows // rep
    me, side = lax.axis_index("tensor"), lax.axis_index("rep")
    z, x, core = me // (inner * CORES), me // CORES % inner, me % CORES
    place = jnp.stack([z, x, core]).astype(jnp.int32)

    pairs_here = lax.dynamic_slice_in_dim(pair_count, side * blocks, blocks) - me * depth
    rows_here = lax.dynamic_slice_in_dim(row_count, side * blocks, blocks)
    rows_here = jnp.where(pairs_here > 0, rows_here, 0)
    parts_of_b = integrals.reshape(all_cols, blocks, depth // LANES, LANES).transpose(0, 2, 1, 3)
    parts_of_b = parts_of_b.reshape(inner * OUTER, CORES, cols, blocks * depth // LANES, LANES)

    def index(z, x, core):
        return (z * inner + x) * CORES + core

    across = [(index(z, x, c), index(z, x, 1 - c))
              for z in range(OUTER) for x in range(inner) for c in range(CORES)]

    def along_inner(bit):
        return [(index(z, x, c), index(z, x ^ bit, c))
                for z in range(OUTER) for x in range(inner) for c in range(CORES)]

    def along_outer(bit):
        return [(index(z, x, c), index(z ^ bit, x, c))
                for z in range(OUTER) for x in range(inner) for c in range(CORES)]

    chain = Chain()
    received, totals, gens = {}, {}, {}

    def run_products(chunks, *got):
        return chain.run(
            lambda p, l, r, b, a, *g: products(p, l, r, b, a, chunks, inner, g),
            place, pairs_here, rows_here, parts_of_b, amplitudes, *got,
        )

    def first_halves(names):
        sent = run_products([(h, 0, rows, False) for h in names])
        for i, h in enumerate(names):
            received[h] = [lax.ppermute(part, "tensor", across)
                           for part in sent[i * PIECES:(i + 1) * PIECES]]

    def second_halves(names):
        got = [part for h in sorted({chunks[i][0] for i in names}) for part in received[h]]
        outs = run_products([chunks[i] for i in names], *got)
        for at, i in enumerate(names):
            gens[i] = work(*chunks[i], *outs[2 * at:2 * at + 2])

    def work(h, start, count, outer_first, keep, send):
        steps = [along_inner(1 << i) for i in range(inner.bit_length() - 1)]
        more = [along_outer(1 << i) for i in range(OUTER.bit_length() - 1)]
        for pairs in more + steps if outer_first else steps + more:
            got = lax.ppermute(send, "tensor", pairs)
            half = keep.shape[0] // 2
            if half < cols:
                totals[h, start] = chain.run(jnp.add, keep, got)
            else:
                keep, send = chain.run(
                    lambda a, b: (a[:half] + b[:half], a[half:] + b[half:]), keep, got
                )
            yield

    mine, other, arriving = {}, {}, []

    def exchange(group):
        if rep != 2:
            for h in group:
                mine[h] = totals[h, 0]
            return
        pairs = []
        for h in group:
            if (h, row_local) in totals:
                pairs.append((totals[h, 0], totals[h, row_local]))
            else:
                pairs.append((totals[h, 0][:, :row_local], totals[h, 0][:, row_local:]))

        def choose(pairs):
            kept = [jnp.where(side == 0, a, b) for a, b in pairs]
            return kept, jnp.concatenate([jnp.where(side == 0, b, a) for a, b in pairs])

        kept, away = chain.run(choose, pairs)
        got = lax.ppermute(away, "rep", [(0, 1), (1, 0)])
        for i, h in enumerate(group):
            mine[h], other[h] = kept[i], got[i * cols:(i + 1) * cols]
        arriving.append(got)

    if inner == 2 and rep == 2 and blocks == 4:
        half = rows // 2
        chunks = [(0, 0, rows, False), (1, 0, rows, False), (2, 0, half, True),
                  (2, half, half, False), (3, 0, half, False), (3, half, half, False)]
        firsts = {"p": [0, 1], "q": [2, 3]}
        seconds = {"w": [0], "x": [1], "y": [2, 3], "z": [4, 5]}
        groups = {"a": [0, 1, 2], "d": [3]}
        plan = "pwxq0yz01203214135243a545Ad"
    else:
        chunks = [(h, 0, rows, False) for h in range(blocks)]
        firsts = {"p": list(range(blocks))}
        seconds = {"w": list(range(blocks))}
        groups = {"a": list(range(blocks))}
        steps = (inner * OUTER).bit_length() - 1
        plan = "pw" + "".join(str(h) * steps for h in range(blocks)) + "a"
    for move in plan:
        if move in firsts:
            first_halves(firsts[move])
        elif move in seconds:
            second_halves(seconds[move])
        elif move == "A":
            chain.last = chain.last, arriving[-1]
        elif move in groups:
            exchange(groups[move])
        else:
            next(gens[int(move)])

    if rep == 2:
        base = jnp.stack([me * cols, side * row_local]).astype(jnp.int32)
        return place_blocks(
            jnp.reshape(side, (1,)).astype(jnp.int32), base, row_count, col_count,
            [mine[h] for h in range(blocks)], [other[h] for h in range(blocks)],
        )
    arranged = lax.all_to_all(
        jnp.stack([mine[h] for h in range(blocks)], axis=1), "rep",
        split_axis=2, concat_axis=1, tiled=True,
    )
    col_index = me * cols + lax.broadcasted_iota(jnp.int32, (cols, 1, 1), 0)
    row_index = side * row_local + lax.broadcasted_iota(jnp.int32, (1, 1, row_local), 2)
    keep = (col_index < col_count[None, :, None]) & (row_index < row_count[None, :, None])
    return jnp.where(keep, arranged, F32(0.0))


def solution(mesh):
    inner = mesh.shape["tensor"] // (OUTER * CORES)
    in_specs = (P("rep", "tensor", None), P(None, "rep", "tensor"), P(), P(), P())
    out_specs = P("tensor", None, "rep")
    return jax.shard_map(
        functools.partial(local, inner), mesh=mesh, in_specs=in_specs, out_specs=out_specs,
        check_vma=False,
    )
```

```python
import functools

import jax
import jax.numpy as jnp
from jax import lax
from jax.experimental import pallas as pl
from jax.experimental.pallas import tpu as pltpu
from jax.sharding import PartitionSpec as P

OUTER = 4
CORES = 2
LANES = 128
TILE = 256
PIECES = 2
VMEM_BYTES = 44 * 1024 * 1024
F32 = jnp.float32
BF16 = jnp.bfloat16


def params():
    return pltpu.CompilerParams(vmem_limit_bytes=VMEM_BYTES)


def cost():
    return pl.CostEstimate(flops=1024, bytes_accessed=1024, transcendentals=0)


def split(value):
    high = value.astype(BF16)
    return high, (value - high.astype(F32)).astype(BF16)


def reversed_bits(value, count):
    result, bit = 0, 1
    while bit < count:
        result = 2 * result + (value // bit) % 2
        bit *= 2
    return result


def put_split(group, limit, first, b_ref, high_ref, low_ref, place):
    used = high_ref.shape[0]
    cols, depth = high_ref.shape[-2:]
    tiles = depth // LANES
    blocks = b_ref.shape[2] // tiles
    lane = lax.broadcasted_iota(jnp.int32, (1, LANES), 1)
    for h in range(used):
        rows = pl.ds(first + h, tiles, stride=blocks) if blocks > 1 else slice(None)
        turned = jnp.swapaxes(b_ref[group, :, rows, :], 0, 1)
        for t in range(tiles):
            value = jnp.where(lane < limit[first + h] - t * LANES, turned[t], F32(0.0))
            high, low = split(value)
            high_ref[(h, *place, slice(None), slice(t * LANES, (t + 1) * LANES))] = high
            low_ref[(h, *place, slice(None), slice(t * LANES, (t + 1) * LANES))] = low


def slot(group, place, inner):
    x = reversed_bits((group % inner) ^ place[1], inner)
    z = reversed_bits((group // inner) ^ place[0], OUTER)
    return x * OUTER + z


def dot3(left_high, left_low, a_ref):
    high, low = split(a_ref[...])
    dot = functools.partial(jnp.dot, preferred_element_type=F32)
    return dot(left_high, high) + (dot(left_high, low) + dot(left_low, high))


def products_kernel(first, inner, chunks, adds, place, limit, rows_live, b_hbm, a_hbm, *refs):
    received, (*outs, b_buf, a_buf, sums, high_ref, low_ref, b_sem, a_sem, in_sem, out_sem) = (
        refs[:adds], refs[adds:]
    )
    groups, cols, depth = high_ref.shape[1:]
    tile = a_buf.shape[2]
    height = groups * cols
    per_chunk = 2 if adds else PIECES
    side = lax.rem(place[2] + (0 if adds else 1), CORES)
    tiles = []
    at = 0
    for i, (h, start, count, outer_first) in enumerate(chunks):
        tiles.append((at, count // tile, h, start, outer_first, outs[i * per_chunk:(i + 1) * per_chunk]))
        at += count // tile

    def columns(n, start=0):
        return pl.ds(pl.multiple_of(start + n * tile, tile), tile)

    def load_b(g):
        return pltpu.make_async_copy(b_hbm.at[g, side], b_buf.at[g], b_sem.at[g])

    def load_a(at, n, h, start):
        return pltpu.make_async_copy(
            a_hbm.at[h, :, columns(n, start)], a_buf.at[at + n], a_sem.at[at + n]
        )

    def loads(at, n, h, start):
        part = height // PIECES
        return [pltpu.make_async_copy(
            received[(h - first) * PIECES + i].at[:, columns(n, start)],
            sums.at[at + n, pl.ds(i * part, part)], in_sem.at[at + n, i],
        ) for i in range(PIECES if adds else 0)]

    def stores(at, n, outer_first, out):
        copies = []
        part = height // len(out)
        pieces = groups if outer_first else len(out)
        for i in range(pieces):
            if outer_first:
                x, z = i // OUTER, i % OUTER
                to, row = divmod((z * inner + x) * cols, part)
            else:
                to, row = i, 0
            size = height // pieces
            copies.append(pltpu.make_async_copy(
                sums.at[at + n, pl.ds(i * size, size)],
                out[to].at[pl.ds(row, size), columns(n)], out_sem.at[at + n, i],
            ))
        return copies

    def live(n, h, start):
        return start + n * tile < rows_live[h]

    for g in range(groups):
        load_b(g).start()
    for at, count, h, start, _, _ in tiles:
        @pl.loop(0, count)
        def _(n):
            @pl.when(live(n, h, start))
            def _():
                load_a(at, n, h, start).start()
            for copy in loads(at, n, h, start):
                copy.start()

    @pl.loop(0, groups)
    def _(g):
        load_b(g).wait()
        put_split(g, limit, first, b_buf, high_ref, low_ref, (slot(g, place, inner),))

    for at, count, h, start, outer_first, out in tiles:
        @pl.loop(0, count)
        def _(n):
            for copy in loads(at, n, h, start):
                copy.wait()

            @pl.when(live(n, h, start))
            def _():
                load_a(at, n, h, start).wait()
                left = (r[h - first].reshape(height, depth) for r in (high_ref, low_ref))
                total = dot3(*left, a_buf.at[at + n])
                sums[at + n] = sums[at + n] + total if adds else total

            if not adds:
                @pl.when(jnp.logical_not(live(n, h, start)))
                def _():
                    sums[at + n] = jnp.zeros((height, tile), F32)

            for copy in stores(at, n, outer_first, out):
                copy.start()

    for at, count, _, _, outer_first, out in tiles:
        @pl.loop(0, count)
        def _(n):
            for copy in stores(at, n, outer_first, out):
                copy.wait()


def products(place, limit, rows_live, parts_of_b, amplitudes, chunks, inner, received):
    groups, _, cols, rows_b, _ = parts_of_b.shape
    blocks, depth, rows = amplitudes.shape
    tile = min(rows, TILE)
    first, last = chunks[0][0], chunks[-1][0]
    total = sum(chunk[2] for chunk in chunks) // tile
    height = groups * cols
    count = 2 if received else PIECES
    anywhere = pl.BlockSpec(memory_space=pl.ANY)
    part = pltpu.VMEM((last - first + 1, groups, cols, depth), BF16)
    return pl.pallas_call(
        functools.partial(products_kernel, first, inner, chunks, len(received)),
        grid_spec=pltpu.PrefetchScalarGridSpec(
            num_scalar_prefetch=3,
            grid=(),
            in_specs=[anywhere] * (2 + len(received)),
            out_specs=[anywhere] * (count * len(chunks)),
            scratch_shapes=[
                pltpu.VMEM((groups, cols, rows_b, LANES), F32),
                pltpu.VMEM((total, depth, tile), F32),
                pltpu.VMEM((total, height, tile), F32),
                part,
                part,
                pltpu.SemaphoreType.DMA((groups,)),
                pltpu.SemaphoreType.DMA((total,)),
                pltpu.SemaphoreType.DMA((total, PIECES)),
                pltpu.SemaphoreType.DMA((total, groups)),
            ],
        ),
        out_shape=[jax.ShapeDtypeStruct((height // count, chunk[2]), F32)
                   for chunk in chunks for _ in range(count)],
        cost_estimate=cost(),
        compiler_params=params(),
        name="second_halves" if received else "first_halves",
    )(place, limit, rows_live, parts_of_b, amplitudes, *received)


def place_kernel(side_ref, base, row_count, col_count, *refs):
    *parts, out_ref = refs
    side = side_ref[0]
    blocks = len(parts) // 2
    cols, rows = parts[0].shape
    col = base[0] + lax.broadcasted_iota(jnp.int32, (cols, rows), 0)
    row = base[1] + lax.broadcasted_iota(jnp.int32, (cols, rows), 1)
    for here in range(2):
        @pl.when(side == here)
        def _():
            order = parts[blocks:] + parts[:blocks] if here else parts
            kept = [
                jnp.where((col < col_count[h]) & (row < row_count[h]), part[...], F32(0.0))
                for h, part in enumerate(order)
            ]
            out_ref[...] = jnp.swapaxes(jnp.stack(kept), 0, 1)


def place_blocks(side, base, row_count, col_count, mine, other):
    cols, rows = mine[0].shape
    blocks = 2 * len(mine)
    vmem = pl.BlockSpec(memory_space=pltpu.VMEM)
    return pl.pallas_call(
        place_kernel,
        grid_spec=pltpu.PrefetchScalarGridSpec(
            num_scalar_prefetch=4, grid=(), in_specs=[vmem] * blocks, out_specs=vmem,
        ),
        out_shape=jax.ShapeDtypeStruct((cols, blocks, rows), F32),
        cost_estimate=cost(),
        compiler_params=params(),
        name="place_blocks",
    )(side, base, row_count, col_count, *mine, *other)


class Chain:
    def __init__(self):
        self.last = None

    def run(self, step, *args):
        if self.last is not None:
            args, _ = lax.optimization_barrier((args, self.last))
        result = step(*args)
        self.last = jax.tree.leaves(result)[0]
        return result


def local(inner, amplitudes, integrals, row_count, pair_count, col_count):
    blocks, depth, rows = amplitudes.shape
    all_cols = integrals.shape[0]
    tensor, rep = lax.axis_size("tensor"), lax.axis_size("rep")
    cols, row_local = all_cols // tensor, rows // rep
    me, side = lax.axis_index("tensor"), lax.axis_index("rep")
    z, x, core = me // (inner * CORES), me // CORES % inner, me % CORES
    place = jnp.stack([z, x, core]).astype(jnp.int32)

    pairs_here = lax.dynamic_slice_in_dim(pair_count, side * blocks, blocks) - me * depth
    rows_here = lax.dynamic_slice_in_dim(row_count, side * blocks, blocks)
    rows_here = jnp.where(pairs_here > 0, rows_here, 0)
    parts_of_b = integrals.reshape(all_cols, blocks, depth // LANES, LANES).transpose(0, 2, 1, 3)
    parts_of_b = parts_of_b.reshape(inner * OUTER, CORES, cols, blocks * depth // LANES, LANES)

    def index(z, x, core):
        return (z * inner + x) * CORES + core

    across = [(index(z, x, c), index(z, x, 1 - c))
              for z in range(OUTER) for x in range(inner) for c in range(CORES)]

    def along_inner(bit):
        return [(index(z, x, c), index(z, x ^ bit, c))
                for z in range(OUTER) for x in range(inner) for c in range(CORES)]

    def along_outer(bit):
        return [(index(z, x, c), index(z ^ bit, x, c))
                for z in range(OUTER) for x in range(inner) for c in range(CORES)]

    chain = Chain()
    received, totals, gens = {}, {}, {}

    def run_products(chunks, *got):
        return chain.run(
            lambda p, l, r, b, a, *g: products(p, l, r, b, a, chunks, inner, g),
            place, pairs_here, rows_here, parts_of_b, amplitudes, *got,
        )

    def first_halves(names):
        sent = run_products([(h, 0, rows, False) for h in names])
        for i, h in enumerate(names):
            received[h] = [lax.ppermute(part, "tensor", across)
                           for part in sent[i * PIECES:(i + 1) * PIECES]]

    def second_halves(names):
        got = [part for h in sorted({chunks[i][0] for i in names}) for part in received[h]]
        outs = run_products([chunks[i] for i in names], *got)
        for at, i in enumerate(names):
            gens[i] = work(*chunks[i], *outs[2 * at:2 * at + 2])

    def work(h, start, count, outer_first, keep, send):
        steps = [along_inner(1 << i) for i in range(inner.bit_length() - 1)]
        more = [along_outer(1 << i) for i in range(OUTER.bit_length() - 1)]
        for pairs in more + steps if outer_first else steps + more:
            got = lax.ppermute(send, "tensor", pairs)
            half = keep.shape[0] // 2
            if half < cols:
                totals[h, start] = chain.run(jnp.add, keep, got)
            else:
                keep, send = chain.run(
                    lambda a, b: (a[:half] + b[:half], a[half:] + b[half:]), keep, got
                )
            yield

    mine, other, arriving = {}, {}, []

    def exchange(group):
        if rep != 2:
            for h in group:
                mine[h] = totals[h, 0]
            return
        pairs = []
        for h in group:
            if (h, row_local) in totals:
                pairs.append((totals[h, 0], totals[h, row_local]))
            else:
                pairs.append((totals[h, 0][:, :row_local], totals[h, 0][:, row_local:]))

        def choose(pairs):
            kept = [jnp.where(side == 0, a, b) for a, b in pairs]
            return kept, jnp.concatenate([jnp.where(side == 0, b, a) for a, b in pairs])

        kept, away = chain.run(choose, pairs)
        got = lax.ppermute(away, "rep", [(0, 1), (1, 0)])
        for i, h in enumerate(group):
            mine[h], other[h] = kept[i], got[i * cols:(i + 1) * cols]
        arriving.append(got)

    if inner == 2 and rep == 2 and blocks == 4:
        half = rows // 2
        chunks = [(0, 0, rows, False), (1, 0, half, True), (1, half, half, False),
                  (2, 0, rows, False), (3, 0, half, False), (3, half, half, False)]
        firsts = {"p": [0, 1], "q": [2, 3]}
        seconds = {"w": [0], "x": [1, 2], "y": [3], "z": [4, 5]}
        groups = {"a": [0, 1, 2], "d": [3]}
        plan = "pwxq0y12z012032143543a545Ad"
    else:
        chunks = [(h, 0, rows, False) for h in range(blocks)]
        firsts = {"p": list(range(blocks))}
        seconds = {"w": list(range(blocks))}
        groups = {"a": list(range(blocks))}
        steps = (inner * OUTER).bit_length() - 1
        plan = "pw" + "".join(str(h) * steps for h in range(blocks)) + "a"
    for move in plan:
        if move in firsts:
            first_halves(firsts[move])
        elif move in seconds:
            second_halves(seconds[move])
        elif move == "A":
            chain.last = chain.last, arriving[-1]
        elif move in groups:
            exchange(groups[move])
        else:
            next(gens[int(move)])

    if rep == 2:
        base = jnp.stack([me * cols, side * row_local]).astype(jnp.int32)
        return place_blocks(
            jnp.reshape(side, (1,)).astype(jnp.int32), base, row_count, col_count,
            [mine[h] for h in range(blocks)], [other[h] for h in range(blocks)],
        )
    arranged = lax.all_to_all(
        jnp.stack([mine[h] for h in range(blocks)], axis=1), "rep",
        split_axis=2, concat_axis=1, tiled=True,
    )
    col_index = me * cols + lax.broadcasted_iota(jnp.int32, (cols, 1, 1), 0)
    row_index = side * row_local + lax.broadcasted_iota(jnp.int32, (1, 1, row_local), 2)
    keep = (col_index < col_count[None, :, None]) & (row_index < row_count[None, :, None])
    return jnp.where(keep, arranged, F32(0.0))


def solution(mesh):
    inner = mesh.shape["tensor"] // (OUTER * CORES)
    in_specs = (P("rep", "tensor", None), P(None, "rep", "tensor"), P(), P(), P())
    out_specs = P("tensor", None, "rep")
    return jax.shard_map(
        functools.partial(local, inner), mesh=mesh, in_specs=in_specs, out_specs=out_specs,
        check_vma=False,
    )
```

```python
import functools

import jax
import jax.numpy as jnp
from jax import lax
from jax.experimental import pallas as pl
from jax.experimental.pallas import tpu as pltpu
from jax.sharding import PartitionSpec as P

OUTER = 4
CORES = 2
LANES = 128
TILE = 256
PIECES = 2
VMEM_BYTES = 44 * 1024 * 1024
F32 = jnp.float32
BF16 = jnp.bfloat16


def params():
    return pltpu.CompilerParams(vmem_limit_bytes=VMEM_BYTES)


def cost():
    return pl.CostEstimate(flops=1024, bytes_accessed=1024, transcendentals=0)


def split(value):
    high = value.astype(BF16)
    return high, (value - high.astype(F32)).astype(BF16)


def reversed_bits(value, count):
    result, bit = 0, 1
    while bit < count:
        result = 2 * result + (value // bit) % 2
        bit *= 2
    return result


def put_split(group, limit, first, b_ref, high_ref, low_ref, place):
    used = high_ref.shape[0]
    cols, depth = high_ref.shape[-2:]
    tiles = depth // LANES
    blocks = b_ref.shape[2] // tiles
    lane = lax.broadcasted_iota(jnp.int32, (1, LANES), 1)
    for h in range(used):
        rows = pl.ds(first + h, tiles, stride=blocks) if blocks > 1 else slice(None)
        turned = jnp.swapaxes(b_ref[group, :, rows, :], 0, 1)
        for t in range(tiles):
            value = jnp.where(lane < limit[first + h] - t * LANES, turned[t], F32(0.0))
            high, low = split(value)
            high_ref[(h, *place, slice(None), slice(t * LANES, (t + 1) * LANES))] = high
            low_ref[(h, *place, slice(None), slice(t * LANES, (t + 1) * LANES))] = low


def slot(group, place, inner):
    x = reversed_bits((group % inner) ^ place[1], inner)
    z = reversed_bits((group // inner) ^ place[0], OUTER)
    return x * OUTER + z


def dot3(left_high, left_low, a_ref):
    high, low = split(a_ref[...])
    dot = functools.partial(jnp.dot, preferred_element_type=F32)
    return dot(left_high, high) + (dot(left_high, low) + dot(left_low, high))


def products_kernel(first, inner, chunks, adds, place, limit, rows_live, b_hbm, a_hbm, *refs):
    received, (*outs, b_buf, a_buf, sums, high_ref, low_ref, b_sem, a_sem, in_sem, out_sem) = (
        refs[:adds], refs[adds:]
    )
    groups, cols, depth = high_ref.shape[1:]
    tile = a_buf.shape[2]
    height = groups * cols
    per_chunk = 2 if adds else PIECES
    side = lax.rem(place[2] + (0 if adds else 1), CORES)
    tiles = []
    at = 0
    for i, (h, start, count, outer_first) in enumerate(chunks):
        tiles.append((at, count // tile, h, start, outer_first, outs[i * per_chunk:(i + 1) * per_chunk]))
        at += count // tile

    def columns(n, start=0):
        return pl.ds(pl.multiple_of(start + n * tile, tile), tile)

    def load_b(g):
        return pltpu.make_async_copy(b_hbm.at[g, side], b_buf.at[g], b_sem.at[g])

    def load_a(at, n, h, start):
        return pltpu.make_async_copy(
            a_hbm.at[h, :, columns(n, start)], a_buf.at[at + n], a_sem.at[at + n]
        )

    def loads(at, n, h, start):
        part = height // PIECES
        return [pltpu.make_async_copy(
            received[(h - first) * PIECES + i].at[:, columns(n, start)],
            sums.at[at + n, pl.ds(i * part, part)], in_sem.at[at + n, i],
        ) for i in range(PIECES if adds else 0)]

    def stores(at, n, outer_first, out):
        copies = []
        part = height // len(out)
        pieces = groups if outer_first else len(out)
        for i in range(pieces):
            if outer_first:
                x, z = i // OUTER, i % OUTER
                to, row = divmod((z * inner + x) * cols, part)
            else:
                to, row = i, 0
            size = height // pieces
            copies.append(pltpu.make_async_copy(
                sums.at[at + n, pl.ds(i * size, size)],
                out[to].at[pl.ds(row, size), columns(n)], out_sem.at[at + n, i],
            ))
        return copies

    def live(n, h, start):
        return start + n * tile < rows_live[h]

    for g in range(groups):
        load_b(g).start()
    for at, count, h, start, _, _ in tiles:
        @pl.loop(0, count)
        def _(n):
            @pl.when(live(n, h, start))
            def _():
                load_a(at, n, h, start).start()
            for copy in loads(at, n, h, start):
                copy.start()

    @pl.loop(0, groups)
    def _(g):
        load_b(g).wait()
        put_split(g, limit, first, b_buf, high_ref, low_ref, (slot(g, place, inner),))

    for at, count, h, start, outer_first, out in tiles:
        @pl.loop(0, count)
        def _(n):
            for copy in loads(at, n, h, start):
                copy.wait()

            @pl.when(live(n, h, start))
            def _():
                load_a(at, n, h, start).wait()
                left = (r[h - first].reshape(height, depth) for r in (high_ref, low_ref))
                total = dot3(*left, a_buf.at[at + n])
                sums[at + n] = sums[at + n] + total if adds else total

            if not adds:
                @pl.when(jnp.logical_not(live(n, h, start)))
                def _():
                    sums[at + n] = jnp.zeros((height, tile), F32)

            for copy in stores(at, n, outer_first, out):
                copy.start()

    for at, count, _, _, outer_first, out in tiles:
        @pl.loop(0, count)
        def _(n):
            for copy in stores(at, n, outer_first, out):
                copy.wait()


def products(place, limit, rows_live, parts_of_b, amplitudes, chunks, inner, received):
    groups, _, cols, rows_b, _ = parts_of_b.shape
    blocks, depth, rows = amplitudes.shape
    tile = min(rows, TILE)
    first, last = chunks[0][0], chunks[-1][0]
    total = sum(chunk[2] for chunk in chunks) // tile
    height = groups * cols
    count = 2 if received else PIECES
    anywhere = pl.BlockSpec(memory_space=pl.ANY)
    part = pltpu.VMEM((last - first + 1, groups, cols, depth), BF16)
    return pl.pallas_call(
        functools.partial(products_kernel, first, inner, chunks, len(received)),
        grid_spec=pltpu.PrefetchScalarGridSpec(
            num_scalar_prefetch=3,
            grid=(),
            in_specs=[anywhere] * (2 + len(received)),
            out_specs=[anywhere] * (count * len(chunks)),
            scratch_shapes=[
                pltpu.VMEM((groups, cols, rows_b, LANES), F32),
                pltpu.VMEM((total, depth, tile), F32),
                pltpu.VMEM((total, height, tile), F32),
                part,
                part,
                pltpu.SemaphoreType.DMA((groups,)),
                pltpu.SemaphoreType.DMA((total,)),
                pltpu.SemaphoreType.DMA((total, PIECES)),
                pltpu.SemaphoreType.DMA((total, groups)),
            ],
        ),
        out_shape=[jax.ShapeDtypeStruct((height // count, chunk[2]), F32)
                   for chunk in chunks for _ in range(count)],
        cost_estimate=cost(),
        compiler_params=params(),
        name="second_halves" if received else "first_halves",
    )(place, limit, rows_live, parts_of_b, amplitudes, *received)


def place_kernel(side_ref, base, row_count, col_count, *refs):
    *parts, out_ref = refs
    side = side_ref[0]
    blocks = len(parts) // 2
    cols, rows = parts[0].shape
    col = base[0] + lax.broadcasted_iota(jnp.int32, (cols, rows), 0)
    row = base[1] + lax.broadcasted_iota(jnp.int32, (cols, rows), 1)
    for here in range(2):
        @pl.when(side == here)
        def _():
            order = parts[blocks:] + parts[:blocks] if here else parts
            kept = [
                jnp.where((col < col_count[h]) & (row < row_count[h]), part[...], F32(0.0))
                for h, part in enumerate(order)
            ]
            out_ref[...] = jnp.swapaxes(jnp.stack(kept), 0, 1)


def place_blocks(side, base, row_count, col_count, mine, other):
    cols, rows = mine[0].shape
    blocks = 2 * len(mine)
    vmem = pl.BlockSpec(memory_space=pltpu.VMEM)
    return pl.pallas_call(
        place_kernel,
        grid_spec=pltpu.PrefetchScalarGridSpec(
            num_scalar_prefetch=4, grid=(), in_specs=[vmem] * blocks, out_specs=vmem,
        ),
        out_shape=jax.ShapeDtypeStruct((cols, blocks, rows), F32),
        cost_estimate=cost(),
        compiler_params=params(),
        name="place_blocks",
    )(side, base, row_count, col_count, *mine, *other)


class Chain:
    def __init__(self):
        self.last = None

    def run(self, step, *args):
        if self.last is not None:
            args, _ = lax.optimization_barrier((args, self.last))
        result = step(*args)
        self.last = jax.tree.leaves(result)[0]
        return result


def local(inner, amplitudes, integrals, row_count, pair_count, col_count):
    blocks, depth, rows = amplitudes.shape
    all_cols = integrals.shape[0]
    tensor, rep = lax.axis_size("tensor"), lax.axis_size("rep")
    cols, row_local = all_cols // tensor, rows // rep
    me, side = lax.axis_index("tensor"), lax.axis_index("rep")
    z, x, core = me // (inner * CORES), me // CORES % inner, me % CORES
    place = jnp.stack([z, x, core]).astype(jnp.int32)

    pairs_here = lax.dynamic_slice_in_dim(pair_count, side * blocks, blocks) - me * depth
    rows_here = lax.dynamic_slice_in_dim(row_count, side * blocks, blocks)
    rows_here = jnp.where(pairs_here > 0, rows_here, 0)
    parts_of_b = integrals.reshape(all_cols, blocks, depth // LANES, LANES).transpose(0, 2, 1, 3)
    parts_of_b = parts_of_b.reshape(inner * OUTER, CORES, cols, blocks * depth // LANES, LANES)

    def index(z, x, core):
        return (z * inner + x) * CORES + core

    across = [(index(z, x, c), index(z, x, 1 - c))
              for z in range(OUTER) for x in range(inner) for c in range(CORES)]

    def along_inner(bit):
        return [(index(z, x, c), index(z, x ^ bit, c))
                for z in range(OUTER) for x in range(inner) for c in range(CORES)]

    def along_outer(bit):
        return [(index(z, x, c), index(z ^ bit, x, c))
                for z in range(OUTER) for x in range(inner) for c in range(CORES)]

    chain = Chain()
    received, totals, gens = {}, {}, {}

    def run_products(chunks, *got):
        return chain.run(
            lambda p, l, r, b, a, *g: products(p, l, r, b, a, chunks, inner, g),
            place, pairs_here, rows_here, parts_of_b, amplitudes, *got,
        )

    def first_halves(names):
        sent = run_products([(h, 0, rows, False) for h in names])
        for i, h in enumerate(names):
            received[h] = [lax.ppermute(part, "tensor", across)
                           for part in sent[i * PIECES:(i + 1) * PIECES]]

    def second_halves(names):
        got = [part for h in sorted({chunks[i][0] for i in names}) for part in received[h]]
        outs = run_products([chunks[i] for i in names], *got)
        for at, i in enumerate(names):
            gens[i] = work(*chunks[i], *outs[2 * at:2 * at + 2])

    def work(h, start, count, outer_first, keep, send):
        steps = [along_inner(1 << i) for i in range(inner.bit_length() - 1)]
        more = [along_outer(1 << i) for i in range(OUTER.bit_length() - 1)]
        for pairs in more + steps if outer_first else steps + more:
            got = lax.ppermute(send, "tensor", pairs)
            half = keep.shape[0] // 2
            if half < cols:
                totals[h, start] = chain.run(jnp.add, keep, got)
            else:
                keep, send = chain.run(
                    lambda a, b: (a[:half] + b[:half], a[half:] + b[half:]), keep, got
                )
            yield

    mine, other, arriving = {}, {}, []

    def exchange(group):
        if rep != 2:
            for h in group:
                mine[h] = totals[h, 0]
            return
        pairs = []
        for h in group:
            if (h, row_local) in totals:
                pairs.append((totals[h, 0], totals[h, row_local]))
            else:
                pairs.append((totals[h, 0][:, :row_local], totals[h, 0][:, row_local:]))

        def choose(pairs):
            kept = [jnp.where(side == 0, a, b) for a, b in pairs]
            return kept, jnp.concatenate([jnp.where(side == 0, b, a) for a, b in pairs])

        kept, away = chain.run(choose, pairs)
        got = lax.ppermute(away, "rep", [(0, 1), (1, 0)])
        for i, h in enumerate(group):
            mine[h], other[h] = kept[i], got[i * cols:(i + 1) * cols]
        arriving.append(got)

    if inner == 2 and rep == 2 and blocks == 4:
        half = rows // 2
        chunks = [(0, 0, rows, False), (1, 0, rows, False), (2, 0, half, True),
                  (2, half, half, False), (3, 0, half, False), (3, half, half, False)]
        firsts = {"p": [0, 1], "q": [2, 3]}
        seconds = {"w": [0], "x": [1], "y": [2, 3], "z": [4, 5]}
        groups = {"a": [0, 1], "d": [2, 3]}
        plan = "pwxq0yz012032141352a45345Ad"
    else:
        chunks = [(h, 0, rows, False) for h in range(blocks)]
        firsts = {"p": list(range(blocks))}
        seconds = {"w": list(range(blocks))}
        groups = {"a": list(range(blocks))}
        steps = (inner * OUTER).bit_length() - 1
        plan = "pw" + "".join(str(h) * steps for h in range(blocks)) + "a"
    for move in plan:
        if move in firsts:
            first_halves(firsts[move])
        elif move in seconds:
            second_halves(seconds[move])
        elif move == "A":
            chain.last = chain.last, arriving[-1]
        elif move in groups:
            exchange(groups[move])
        else:
            next(gens[int(move)])

    if rep == 2:
        base = jnp.stack([me * cols, side * row_local]).astype(jnp.int32)
        return place_blocks(
            jnp.reshape(side, (1,)).astype(jnp.int32), base, row_count, col_count,
            [mine[h] for h in range(blocks)], [other[h] for h in range(blocks)],
        )
    arranged = lax.all_to_all(
        jnp.stack([mine[h] for h in range(blocks)], axis=1), "rep",
        split_axis=2, concat_axis=1, tiled=True,
    )
    col_index = me * cols + lax.broadcasted_iota(jnp.int32, (cols, 1, 1), 0)
    row_index = side * row_local + lax.broadcasted_iota(jnp.int32, (1, 1, row_local), 2)
    keep = (col_index < col_count[None, :, None]) & (row_index < row_count[None, :, None])
    return jnp.where(keep, arranged, F32(0.0))


def solution(mesh):
    inner = mesh.shape["tensor"] // (OUTER * CORES)
    in_specs = (P("rep", "tensor", None), P(None, "rep", "tensor"), P(), P(), P())
    out_specs = P("tensor", None, "rep")
    return jax.shard_map(
        functools.partial(local, inner), mesh=mesh, in_specs=in_specs, out_specs=out_specs,
        check_vma=False,
    )
```

```python
import functools

import jax
import jax.numpy as jnp
from jax import lax
from jax.experimental import pallas as pl
from jax.experimental.pallas import tpu as pltpu
from jax.sharding import PartitionSpec as P

OUTER = 4
CORES = 2
LANES = 128
TILE = 256
VMEM_BYTES = 44 * 1024 * 1024
F32 = jnp.float32
BF16 = jnp.bfloat16


def params():
    return pltpu.CompilerParams(vmem_limit_bytes=VMEM_BYTES)


def cost():
    return pl.CostEstimate(flops=1024, bytes_accessed=1024, transcendentals=0)


def split(value):
    high = value.astype(BF16)
    return high, (value - high.astype(F32)).astype(BF16)


def reversed_bits(value, count):
    result, bit = 0, 1
    while bit < count:
        result = 2 * result + (value // bit) % 2
        bit *= 2
    return result


def put_split(group, limit, first, b_ref, high_ref, low_ref, place):
    used = high_ref.shape[0]
    cols, depth = high_ref.shape[-2:]
    tiles = depth // LANES
    blocks = b_ref.shape[2] // tiles
    lane = lax.broadcasted_iota(jnp.int32, (1, LANES), 1)
    for h in range(used):
        rows = pl.ds(first + h, tiles, stride=blocks) if blocks > 1 else slice(None)
        turned = jnp.swapaxes(b_ref[group, :, rows, :], 0, 1)
        for t in range(tiles):
            value = jnp.where(lane < limit[first + h] - t * LANES, turned[t], F32(0.0))
            high, low = split(value)
            high_ref[(h, *place, slice(None), slice(t * LANES, (t + 1) * LANES))] = high
            low_ref[(h, *place, slice(None), slice(t * LANES, (t + 1) * LANES))] = low


def slot(group, place, inner):
    x = reversed_bits((group % inner) ^ place[1], inner)
    z = reversed_bits((group // inner) ^ place[0], OUTER)
    return x * OUTER + z


def dot3(left_high, left_low, a_ref):
    high, low = split(a_ref[...])
    dot = functools.partial(jnp.dot, preferred_element_type=F32)
    return dot(left_high, high) + (dot(left_high, low) + dot(left_low, high))


def products_kernel(first, inner, chunks, pieces, adds, place, limit, rows_live, b_hbm, a_hbm, *refs):
    received, (*outs, b_buf, a_buf, sums, high_ref, low_ref, b_sem, a_sem, in_sem, out_sem) = (
        refs[:adds], refs[adds:]
    )
    groups, cols, depth = high_ref.shape[1:]
    tile = a_buf.shape[2]
    height = groups * cols
    per_chunk = 2 if adds else pieces
    side = lax.rem(place[2] + (0 if adds else 1), CORES)
    tiles = []
    at = 0
    for i, (h, start, count, outer_first) in enumerate(chunks):
        tiles.append((at, count // tile, h, start, outer_first, outs[i * per_chunk:(i + 1) * per_chunk]))
        at += count // tile

    def columns(n, start=0):
        return pl.ds(pl.multiple_of(start + n * tile, tile), tile)

    def load_b(g):
        return pltpu.make_async_copy(b_hbm.at[g, side], b_buf.at[g], b_sem.at[g])

    def load_a(at, n, h, start):
        return pltpu.make_async_copy(
            a_hbm.at[h, :, columns(n, start)], a_buf.at[at + n], a_sem.at[at + n]
        )

    def loads(at, n, h, start):
        part = height // pieces
        return [pltpu.make_async_copy(
            received[(h - first) * pieces + i].at[:, columns(n, start)],
            sums.at[at + n, pl.ds(i * part, part)], in_sem.at[at + n, i],
        ) for i in range(pieces if adds else 0)]

    def stores(at, n, outer_first, out):
        copies = []
        part = height // len(out)
        moves = groups if outer_first else len(out)
        for i in range(moves):
            if outer_first:
                x, z = i // OUTER, i % OUTER
                to, row = divmod((z * inner + x) * cols, part)
            else:
                to, row = i, 0
            size = height // moves
            copies.append(pltpu.make_async_copy(
                sums.at[at + n, pl.ds(i * size, size)],
                out[to].at[pl.ds(row, size), columns(n)], out_sem.at[at + n, i],
            ))
        return copies

    def live(n, h, start):
        return start + n * tile < rows_live[h]

    for g in range(groups):
        load_b(g).start()
    for at, count, h, start, _, _ in tiles:
        @pl.loop(0, count)
        def _(n):
            @pl.when(live(n, h, start))
            def _():
                load_a(at, n, h, start).start()
            for copy in loads(at, n, h, start):
                copy.start()

    @pl.loop(0, groups)
    def _(g):
        load_b(g).wait()
        put_split(g, limit, first, b_buf, high_ref, low_ref, (slot(g, place, inner),))

    for at, count, h, start, outer_first, out in tiles:
        @pl.loop(0, count)
        def _(n):
            for copy in loads(at, n, h, start):
                copy.wait()

            @pl.when(live(n, h, start))
            def _():
                load_a(at, n, h, start).wait()
                left = (r[h - first].reshape(height, depth) for r in (high_ref, low_ref))
                total = dot3(*left, a_buf.at[at + n])
                sums[at + n] = sums[at + n] + total if adds else total

            if not adds:
                @pl.when(jnp.logical_not(live(n, h, start)))
                def _():
                    sums[at + n] = jnp.zeros((height, tile), F32)

            for copy in stores(at, n, outer_first, out):
                copy.start()

    for at, count, _, _, outer_first, out in tiles:
        @pl.loop(0, count)
        def _(n):
            for copy in stores(at, n, outer_first, out):
                copy.wait()


def products(place, limit, rows_live, parts_of_b, amplitudes, chunks, pieces, inner, received):
    groups, _, cols, rows_b, _ = parts_of_b.shape
    blocks, depth, rows = amplitudes.shape
    tile = min(rows, TILE)
    first, last = chunks[0][0], chunks[-1][0]
    total = sum(chunk[2] for chunk in chunks) // tile
    height = groups * cols
    count = 2 if received else pieces
    anywhere = pl.BlockSpec(memory_space=pl.ANY)
    part = pltpu.VMEM((last - first + 1, groups, cols, depth), BF16)
    return pl.pallas_call(
        functools.partial(products_kernel, first, inner, chunks, pieces, len(received)),
        grid_spec=pltpu.PrefetchScalarGridSpec(
            num_scalar_prefetch=3,
            grid=(),
            in_specs=[anywhere] * (2 + len(received)),
            out_specs=[anywhere] * (count * len(chunks)),
            scratch_shapes=[
                pltpu.VMEM((groups, cols, rows_b, LANES), F32),
                pltpu.VMEM((total, depth, tile), F32),
                pltpu.VMEM((total, height, tile), F32),
                part,
                part,
                pltpu.SemaphoreType.DMA((groups,)),
                pltpu.SemaphoreType.DMA((total,)),
                pltpu.SemaphoreType.DMA((total, pieces)),
                pltpu.SemaphoreType.DMA((total, groups)),
            ],
        ),
        out_shape=[jax.ShapeDtypeStruct((height // count, chunk[2]), F32)
                   for chunk in chunks for _ in range(count)],
        cost_estimate=cost(),
        compiler_params=params(),
        name="second_halves" if received else "first_halves",
    )(place, limit, rows_live, parts_of_b, amplitudes, *received)


def place_kernel(side_ref, base, row_count, col_count, *refs):
    *parts, out_ref = refs
    side = side_ref[0]
    blocks = len(parts) // 2
    cols, rows = parts[0].shape
    col = base[0] + lax.broadcasted_iota(jnp.int32, (cols, rows), 0)
    row = base[1] + lax.broadcasted_iota(jnp.int32, (cols, rows), 1)
    for here in range(2):
        @pl.when(side == here)
        def _():
            order = parts[blocks:] + parts[:blocks] if here else parts
            kept = [
                jnp.where((col < col_count[h]) & (row < row_count[h]), part[...], F32(0.0))
                for h, part in enumerate(order)
            ]
            out_ref[...] = jnp.swapaxes(jnp.stack(kept), 0, 1)


def place_blocks(side, base, row_count, col_count, mine, other):
    cols, rows = mine[0].shape
    blocks = 2 * len(mine)
    vmem = pl.BlockSpec(memory_space=pltpu.VMEM)
    return pl.pallas_call(
        place_kernel,
        grid_spec=pltpu.PrefetchScalarGridSpec(
            num_scalar_prefetch=4, grid=(), in_specs=[vmem] * blocks, out_specs=vmem,
        ),
        out_shape=jax.ShapeDtypeStruct((cols, blocks, rows), F32),
        cost_estimate=cost(),
        compiler_params=params(),
        name="place_blocks",
    )(side, base, row_count, col_count, *mine, *other)


class Chain:
    def __init__(self):
        self.last = None

    def run(self, step, *args):
        if self.last is not None:
            args, _ = lax.optimization_barrier((args, self.last))
        result = step(*args)
        self.last = jax.tree.leaves(result)[0]
        return result


def local(inner, amplitudes, integrals, row_count, pair_count, col_count):
    blocks, depth, rows = amplitudes.shape
    all_cols = integrals.shape[0]
    tensor, rep = lax.axis_size("tensor"), lax.axis_size("rep")
    cols, row_local = all_cols // tensor, rows // rep
    me, side = lax.axis_index("tensor"), lax.axis_index("rep")
    z, x, core = me // (inner * CORES), me // CORES % inner, me % CORES
    place = jnp.stack([z, x, core]).astype(jnp.int32)

    pairs_here = lax.dynamic_slice_in_dim(pair_count, side * blocks, blocks) - me * depth
    rows_here = lax.dynamic_slice_in_dim(row_count, side * blocks, blocks)
    rows_here = jnp.where(pairs_here > 0, rows_here, 0)
    parts_of_b = integrals.reshape(all_cols, blocks, depth // LANES, LANES).transpose(0, 2, 1, 3)
    parts_of_b = parts_of_b.reshape(inner * OUTER, CORES, cols, blocks * depth // LANES, LANES)

    def index(z, x, core):
        return (z * inner + x) * CORES + core

    across = [(index(z, x, c), index(z, x, 1 - c))
              for z in range(OUTER) for x in range(inner) for c in range(CORES)]

    def along_inner(bit):
        return [(index(z, x, c), index(z, x ^ bit, c))
                for z in range(OUTER) for x in range(inner) for c in range(CORES)]

    def along_outer(bit):
        return [(index(z, x, c), index(z ^ bit, x, c))
                for z in range(OUTER) for x in range(inner) for c in range(CORES)]

    chain = Chain()
    received, totals, gens = {}, {}, {}

    def run_products(chunks, pieces, *got):
        return chain.run(
            lambda p, l, r, b, a, *g: products(p, l, r, b, a, chunks, pieces, inner, g),
            place, pairs_here, rows_here, parts_of_b, amplitudes, *got,
        )

    def first_halves(names, pieces):
        sent = run_products([(h, 0, rows, False) for h in names], pieces)
        for i, h in enumerate(names):
            received[h] = [lax.ppermute(part, "tensor", across)
                           for part in sent[i * pieces:(i + 1) * pieces]]

    def second_halves(names):
        got = [received[h] for h in sorted({chunks[i][0] for i in names})]
        outs = run_products([chunks[i] for i in names], len(got[0]), *sum(got, []))
        for at, i in enumerate(names):
            gens[i] = work(*chunks[i], *outs[2 * at:2 * at + 2])

    def work(h, start, count, outer_first, keep, send):
        steps = [along_inner(1 << i) for i in range(inner.bit_length() - 1)]
        more = [along_outer(1 << i) for i in range(OUTER.bit_length() - 1)]
        for pairs in more + steps if outer_first else steps + more:
            got = lax.ppermute(send, "tensor", pairs)
            half = keep.shape[0] // 2
            if half < cols:
                totals[h, start] = chain.run(jnp.add, keep, got)
            else:
                keep, send = chain.run(
                    lambda a, b: (a[:half] + b[:half], a[half:] + b[half:]), keep, got
                )
            yield

    mine, other, arriving = {}, {}, []

    def exchange(group):
        if rep != 2:
            for h in group:
                mine[h] = totals[h, 0]
            return
        pairs = []
        for h in group:
            if (h, row_local) in totals:
                pairs.append((totals[h, 0], totals[h, row_local]))
            else:
                pairs.append((totals[h, 0][:, :row_local], totals[h, 0][:, row_local:]))

        def choose(pairs):
            kept = [jnp.where(side == 0, a, b) for a, b in pairs]
            return kept, jnp.concatenate([jnp.where(side == 0, b, a) for a, b in pairs])

        kept, away = chain.run(choose, pairs)
        got = lax.ppermute(away, "rep", [(0, 1), (1, 0)])
        for i, h in enumerate(group):
            mine[h], other[h] = kept[i], got[i * cols:(i + 1) * cols]
        arriving.append(got)

    if inner == 2 and rep == 2 and blocks == 4:
        half = rows // 2
        chunks = [(0, 0, half, True), (0, half, half, False), (1, 0, rows, False),
                  (2, 0, rows, False), (3, 0, half, False), (3, half, half, False)]
        firsts = {"p": ([0, 1], 2), "q": ([2], 4), "r": ([3], 2)}
        seconds = {"w": [0, 1], "x": [2], "y": [3], "z": [4, 5]}
        groups = {"a": [0, 1], "b": [2], "d": [3]}
        plan = "pwxq10y10r2z12342350a453b45Ad"
    else:
        chunks = [(h, 0, rows, False) for h in range(blocks)]
        firsts = {"p": (list(range(blocks)), 2)}
        seconds = {"w": list(range(blocks))}
        groups = {"a": list(range(blocks))}
        steps = (inner * OUTER).bit_length() - 1
        plan = "pw" + "".join(str(h) * steps for h in range(blocks)) + "a"
    for move in plan:
        if move in firsts:
            first_halves(*firsts[move])
        elif move in seconds:
            second_halves(seconds[move])
        elif move == "A":
            chain.last = chain.last, arriving[-1]
        elif move in groups:
            exchange(groups[move])
        else:
            next(gens[int(move)])

    if rep == 2:
        base = jnp.stack([me * cols, side * row_local]).astype(jnp.int32)
        return place_blocks(
            jnp.reshape(side, (1,)).astype(jnp.int32), base, row_count, col_count,
            [mine[h] for h in range(blocks)], [other[h] for h in range(blocks)],
        )
    arranged = lax.all_to_all(
        jnp.stack([mine[h] for h in range(blocks)], axis=1), "rep",
        split_axis=2, concat_axis=1, tiled=True,
    )
    col_index = me * cols + lax.broadcasted_iota(jnp.int32, (cols, 1, 1), 0)
    row_index = side * row_local + lax.broadcasted_iota(jnp.int32, (1, 1, row_local), 2)
    keep = (col_index < col_count[None, :, None]) & (row_index < row_count[None, :, None])
    return jnp.where(keep, arranged, F32(0.0))


def solution(mesh):
    inner = mesh.shape["tensor"] // (OUTER * CORES)
    in_specs = (P("rep", "tensor", None), P(None, "rep", "tensor"), P(), P(), P())
    out_specs = P("tensor", None, "rep")
    return jax.shard_map(
        functools.partial(local, inner), mesh=mesh, in_specs=in_specs, out_specs=out_specs,
        check_vma=False,
    )
```

```python
import functools

import jax
import jax.numpy as jnp
from jax import lax
from jax.experimental import pallas as pl
from jax.experimental.pallas import tpu as pltpu
from jax.sharding import PartitionSpec as P

OUTER = 4
CORES = 2
LANES = 128
TILE = 256
PIECES = 2
VMEM_BYTES = 44 * 1024 * 1024
F32 = jnp.float32
BF16 = jnp.bfloat16


def params():
    return pltpu.CompilerParams(vmem_limit_bytes=VMEM_BYTES)


def cost():
    return pl.CostEstimate(flops=1024, bytes_accessed=1024, transcendentals=0)


def split(value):
    high = value.astype(BF16)
    return high, (value - high.astype(F32)).astype(BF16)


def reversed_bits(value, count):
    result, bit = 0, 1
    while bit < count:
        result = 2 * result + (value // bit) % 2
        bit *= 2
    return result


def put_split(group, limit, first, b_ref, high_ref, low_ref, place):
    used = high_ref.shape[0]
    cols, depth = high_ref.shape[-2:]
    tiles = depth // LANES
    blocks = b_ref.shape[2] // tiles
    lane = lax.broadcasted_iota(jnp.int32, (1, LANES), 1)
    for h in range(used):
        rows = pl.ds(first + h, tiles, stride=blocks) if blocks > 1 else slice(None)
        turned = jnp.swapaxes(b_ref[group, :, rows, :], 0, 1)
        for t in range(tiles):
            value = jnp.where(lane < limit[first + h] - t * LANES, turned[t], F32(0.0))
            high, low = split(value)
            high_ref[(h, *place, slice(None), slice(t * LANES, (t + 1) * LANES))] = high
            low_ref[(h, *place, slice(None), slice(t * LANES, (t + 1) * LANES))] = low


def slot(group, place, inner):
    x = reversed_bits((group % inner) ^ place[1], inner)
    z = reversed_bits((group // inner) ^ place[0], OUTER)
    return x * OUTER + z


def dot3(left_high, left_low, a_ref):
    high, low = split(a_ref[...])
    dot = functools.partial(jnp.dot, preferred_element_type=F32)
    return dot(left_high, high) + (dot(left_high, low) + dot(left_low, high))


def products_kernel(first, inner, chunks, adds, place, limit, rows_live, b_hbm, a_hbm, *refs):
    received, (*outs, b_buf, a_buf, sums, high_ref, low_ref, b_sem, a_sem, in_sem, out_sem) = (
        refs[:adds], refs[adds:]
    )
    groups, cols, depth = high_ref.shape[1:]
    tile = a_buf.shape[2]
    height = groups * cols
    per_chunk = 2 if adds else PIECES
    side = lax.rem(place[2] + (0 if adds else 1), CORES)
    tiles = []
    at = 0
    for i, (h, start, count, outer_first) in enumerate(chunks):
        tiles.append((at, count // tile, h, start, outer_first, outs[i * per_chunk:(i + 1) * per_chunk]))
        at += count // tile

    def columns(n, start=0):
        return pl.ds(pl.multiple_of(start + n * tile, tile), tile)

    def load_b(g):
        return pltpu.make_async_copy(b_hbm.at[g, side], b_buf.at[g], b_sem.at[g])

    def load_a(at, n, h, start):
        return pltpu.make_async_copy(
            a_hbm.at[h, :, columns(n, start)], a_buf.at[at + n], a_sem.at[at + n]
        )

    def loads(at, n, h, start):
        part = height // PIECES
        return [pltpu.make_async_copy(
            received[(h - first) * PIECES + i].at[:, columns(n, start)],
            sums.at[at + n, pl.ds(i * part, part)], in_sem.at[at + n, i],
        ) for i in range(PIECES if adds else 0)]

    def stores(at, n, outer_first, out):
        copies = []
        part = height // len(out)
        pieces = groups if outer_first else len(out)
        for i in range(pieces):
            if outer_first:
                x, z = i // OUTER, i % OUTER
                to, row = divmod((z * inner + x) * cols, part)
            else:
                to, row = i, 0
            size = height // pieces
            copies.append(pltpu.make_async_copy(
                sums.at[at + n, pl.ds(i * size, size)],
                out[to].at[pl.ds(row, size), columns(n)], out_sem.at[at + n, i],
            ))
        return copies

    def live(n, h, start):
        return start + n * tile < rows_live[h]

    for g in range(groups):
        load_b(g).start()
    for at, count, h, start, _, _ in tiles:
        @pl.loop(0, count)
        def _(n):
            @pl.when(live(n, h, start))
            def _():
                load_a(at, n, h, start).start()
            for copy in loads(at, n, h, start):
                copy.start()

    @pl.loop(0, groups)
    def _(g):
        load_b(g).wait()
        put_split(g, limit, first, b_buf, high_ref, low_ref, (slot(g, place, inner),))

    for at, count, h, start, outer_first, out in tiles:
        @pl.loop(0, count)
        def _(n):
            for copy in loads(at, n, h, start):
                copy.wait()

            @pl.when(live(n, h, start))
            def _():
                load_a(at, n, h, start).wait()
                left = (r[h - first].reshape(height, depth) for r in (high_ref, low_ref))
                total = dot3(*left, a_buf.at[at + n])
                sums[at + n] = sums[at + n] + total if adds else total

            if not adds:
                @pl.when(jnp.logical_not(live(n, h, start)))
                def _():
                    sums[at + n] = jnp.zeros((height, tile), F32)

            for copy in stores(at, n, outer_first, out):
                copy.start()

    for at, count, _, _, outer_first, out in tiles:
        @pl.loop(0, count)
        def _(n):
            for copy in stores(at, n, outer_first, out):
                copy.wait()


def products(place, limit, rows_live, parts_of_b, amplitudes, chunks, inner, received):
    groups, _, cols, rows_b, _ = parts_of_b.shape
    blocks, depth, rows = amplitudes.shape
    tile = min(rows, TILE)
    first, last = chunks[0][0], chunks[-1][0]
    total = sum(chunk[2] for chunk in chunks) // tile
    height = groups * cols
    count = 2 if received else PIECES
    anywhere = pl.BlockSpec(memory_space=pl.ANY)
    part = pltpu.VMEM((last - first + 1, groups, cols, depth), BF16)
    return pl.pallas_call(
        functools.partial(products_kernel, first, inner, chunks, len(received)),
        grid_spec=pltpu.PrefetchScalarGridSpec(
            num_scalar_prefetch=3,
            grid=(),
            in_specs=[anywhere] * (2 + len(received)),
            out_specs=[anywhere] * (count * len(chunks)),
            scratch_shapes=[
                pltpu.VMEM((groups, cols, rows_b, LANES), F32),
                pltpu.VMEM((total, depth, tile), F32),
                pltpu.VMEM((total, height, tile), F32),
                part,
                part,
                pltpu.SemaphoreType.DMA((groups,)),
                pltpu.SemaphoreType.DMA((total,)),
                pltpu.SemaphoreType.DMA((total, PIECES)),
                pltpu.SemaphoreType.DMA((total, groups)),
            ],
        ),
        out_shape=[jax.ShapeDtypeStruct((height // count, chunk[2]), F32)
                   for chunk in chunks for _ in range(count)],
        cost_estimate=cost(),
        compiler_params=params(),
        name="second_halves" if received else "first_halves",
    )(place, limit, rows_live, parts_of_b, amplitudes, *received)


def place_kernel(side_ref, base, row_count, col_count, *refs):
    *parts, out_ref = refs
    side = side_ref[0]
    blocks = len(parts) // 2
    cols, rows = parts[0].shape
    col = base[0] + lax.broadcasted_iota(jnp.int32, (cols, rows), 0)
    row = base[1] + lax.broadcasted_iota(jnp.int32, (cols, rows), 1)
    for here in range(2):
        @pl.when(side == here)
        def _():
            order = parts[blocks:] + parts[:blocks] if here else parts
            kept = [
                jnp.where((col < col_count[h]) & (row < row_count[h]), part[...], F32(0.0))
                for h, part in enumerate(order)
            ]
            out_ref[...] = jnp.swapaxes(jnp.stack(kept), 0, 1)


def place_blocks(side, base, row_count, col_count, mine, other):
    cols, rows = mine[0].shape
    blocks = 2 * len(mine)
    vmem = pl.BlockSpec(memory_space=pltpu.VMEM)
    return pl.pallas_call(
        place_kernel,
        grid_spec=pltpu.PrefetchScalarGridSpec(
            num_scalar_prefetch=4, grid=(), in_specs=[vmem] * blocks, out_specs=vmem,
        ),
        out_shape=jax.ShapeDtypeStruct((cols, blocks, rows), F32),
        cost_estimate=cost(),
        compiler_params=params(),
        name="place_blocks",
    )(side, base, row_count, col_count, *mine, *other)


class Chain:
    def __init__(self):
        self.last = None

    def run(self, step, *args):
        if self.last is not None:
            args, _ = lax.optimization_barrier((args, self.last))
        result = step(*args)
        self.last = jax.tree.leaves(result)[0]
        return result


def local(inner, amplitudes, integrals, row_count, pair_count, col_count):
    blocks, depth, rows = amplitudes.shape
    all_cols = integrals.shape[0]
    tensor, rep = lax.axis_size("tensor"), lax.axis_size("rep")
    cols, row_local = all_cols // tensor, rows // rep
    me, side = lax.axis_index("tensor"), lax.axis_index("rep")
    z, x, core = me // (inner * CORES), me // CORES % inner, me % CORES
    place = jnp.stack([z, x, core]).astype(jnp.int32)

    pairs_here = lax.dynamic_slice_in_dim(pair_count, side * blocks, blocks) - me * depth
    rows_here = lax.dynamic_slice_in_dim(row_count, side * blocks, blocks)
    rows_here = jnp.where(pairs_here > 0, rows_here, 0)
    parts_of_b = integrals.reshape(all_cols, blocks, depth // LANES, LANES).transpose(0, 2, 1, 3)
    parts_of_b = parts_of_b.reshape(inner * OUTER, CORES, cols, blocks * depth // LANES, LANES)

    def index(z, x, core):
        return (z * inner + x) * CORES + core

    across = [(index(z, x, c), index(z, x, 1 - c))
              for z in range(OUTER) for x in range(inner) for c in range(CORES)]

    def along_inner(bit):
        return [(index(z, x, c), index(z, x ^ bit, c))
                for z in range(OUTER) for x in range(inner) for c in range(CORES)]

    def along_outer(bit):
        return [(index(z, x, c), index(z ^ bit, x, c))
                for z in range(OUTER) for x in range(inner) for c in range(CORES)]

    chain = Chain()
    received, totals, gens = {}, {}, {}

    def run_products(chunks, *got):
        return chain.run(
            lambda p, l, r, b, a, *g: products(p, l, r, b, a, chunks, inner, g),
            place, pairs_here, rows_here, parts_of_b, amplitudes, *got,
        )

    def first_halves(names):
        sent = run_products([(h, 0, rows, False) for h in names])
        for i, h in enumerate(names):
            received[h] = [lax.ppermute(part, "tensor", across)
                           for part in sent[i * PIECES:(i + 1) * PIECES]]

    def second_halves(names):
        got = [part for h in sorted({chunks[i][0] for i in names}) for part in received[h]]
        outs = run_products([chunks[i] for i in names], *got)
        for at, i in enumerate(names):
            gens[i] = work(*chunks[i], *outs[2 * at:2 * at + 2])

    def work(h, start, count, outer_first, keep, send):
        steps = [along_inner(1 << i) for i in range(inner.bit_length() - 1)]
        more = [along_outer(1 << i) for i in range(OUTER.bit_length() - 1)]
        for pairs in more + steps if outer_first else steps + more:
            got = lax.ppermute(send, "tensor", pairs)
            half = keep.shape[0] // 2
            if half < cols:
                totals[h, start] = chain.run(jnp.add, keep, got)
            else:
                keep, send = chain.run(
                    lambda a, b: (a[:half] + b[:half], a[half:] + b[half:]), keep, got
                )
            yield

    mine, other, arriving = {}, {}, []

    def exchange(group):
        if rep != 2:
            for h in group:
                mine[h] = totals[h, 0]
            return
        pairs = []
        for h in group:
            if (h, row_local) in totals:
                pairs.append((totals[h, 0], totals[h, row_local]))
            else:
                pairs.append((totals[h, 0][:, :row_local], totals[h, 0][:, row_local:]))

        def choose(pairs):
            kept = [jnp.where(side == 0, a, b) for a, b in pairs]
            return kept, jnp.concatenate([jnp.where(side == 0, b, a) for a, b in pairs])

        kept, away = chain.run(choose, pairs)
        chain.last = away
        got = lax.ppermute(away, "rep", [(0, 1), (1, 0)])
        for i, h in enumerate(group):
            mine[h], other[h] = kept[i], got[i * cols:(i + 1) * cols]
        arriving.append(got)

    if inner == 2 and rep == 2 and blocks == 4:
        half = rows // 2
        chunks = [(0, 0, rows, False), (1, 0, rows, False), (2, 0, half, True),
                  (2, half, half, False), (3, 0, half, False), (3, half, half, False)]
        firsts = {"p": [0, 1], "q": [2, 3]}
        seconds = {"w": [0], "x": [1], "y": [2, 3], "z": [4, 5]}
        groups = {"a": [0, 1], "b": [2], "d": [3]}
        plan = "pwxq0yz012032141352a453Ab45Ad"
    else:
        chunks = [(h, 0, rows, False) for h in range(blocks)]
        firsts = {"p": list(range(blocks))}
        seconds = {"w": list(range(blocks))}
        groups = {"a": list(range(blocks))}
        steps = (inner * OUTER).bit_length() - 1
        plan = "pw" + "".join(str(h) * steps for h in range(blocks)) + "a"
    for move in plan:
        if move in firsts:
            first_halves(firsts[move])
        elif move in seconds:
            second_halves(seconds[move])
        elif move == "A":
            chain.last = chain.last, arriving[-1]
        elif move in groups:
            exchange(groups[move])
        else:
            next(gens[int(move)])

    if rep == 2:
        base = jnp.stack([me * cols, side * row_local]).astype(jnp.int32)
        return place_blocks(
            jnp.reshape(side, (1,)).astype(jnp.int32), base, row_count, col_count,
            [mine[h] for h in range(blocks)], [other[h] for h in range(blocks)],
        )
    arranged = lax.all_to_all(
        jnp.stack([mine[h] for h in range(blocks)], axis=1), "rep",
        split_axis=2, concat_axis=1, tiled=True,
    )
    col_index = me * cols + lax.broadcasted_iota(jnp.int32, (cols, 1, 1), 0)
    row_index = side * row_local + lax.broadcasted_iota(jnp.int32, (1, 1, row_local), 2)
    keep = (col_index < col_count[None, :, None]) & (row_index < row_count[None, :, None])
    return jnp.where(keep, arranged, F32(0.0))


def solution(mesh):
    inner = mesh.shape["tensor"] // (OUTER * CORES)
    in_specs = (P("rep", "tensor", None), P(None, "rep", "tensor"), P(), P(), P())
    out_specs = P("tensor", None, "rep")
    return jax.shard_map(
        functools.partial(local, inner), mesh=mesh, in_specs=in_specs, out_specs=out_specs,
        check_vma=False,
    )
```

```python
import functools

import jax
import jax.numpy as jnp
from jax import lax
from jax.experimental import pallas as pl
from jax.experimental.pallas import tpu as pltpu
from jax.sharding import PartitionSpec as P

OUTER = 4
CORES = 2
LANES = 128
TILE = 256
PIECES = 2
VMEM_BYTES = 44 * 1024 * 1024
F32 = jnp.float32
BF16 = jnp.bfloat16


def params():
    return pltpu.CompilerParams(vmem_limit_bytes=VMEM_BYTES)


def cost():
    return pl.CostEstimate(flops=1024, bytes_accessed=1024, transcendentals=0)


def split(value):
    high = value.astype(BF16)
    return high, (value - high.astype(F32)).astype(BF16)


def reversed_bits(value, count):
    result, bit = 0, 1
    while bit < count:
        result = 2 * result + (value // bit) % 2
        bit *= 2
    return result


def put_split(group, limit, first, b_ref, high_ref, low_ref, place):
    used = high_ref.shape[0]
    cols, depth = high_ref.shape[-2:]
    tiles = depth // LANES
    blocks = b_ref.shape[2] // tiles
    lane = lax.broadcasted_iota(jnp.int32, (1, LANES), 1)
    for h in range(used):
        rows = pl.ds(first + h, tiles, stride=blocks) if blocks > 1 else slice(None)
        turned = jnp.swapaxes(b_ref[group, :, rows, :], 0, 1)
        for t in range(tiles):
            value = jnp.where(lane < limit[first + h] - t * LANES, turned[t], F32(0.0))
            high, low = split(value)
            high_ref[(h, *place, slice(None), slice(t * LANES, (t + 1) * LANES))] = high
            low_ref[(h, *place, slice(None), slice(t * LANES, (t + 1) * LANES))] = low


def slot(group, place, inner):
    x = reversed_bits((group % inner) ^ place[1], inner)
    z = reversed_bits((group // inner) ^ place[0], OUTER)
    return x * OUTER + z


def dot3(left_high, left_low, a_ref):
    high, low = split(a_ref[...])
    dot = functools.partial(jnp.dot, preferred_element_type=F32)
    return dot(left_high, high) + (dot(left_high, low) + dot(left_low, high))


def products_kernel(first, inner, chunks, adds, place, limit, rows_live, b_hbm, a_hbm, *refs):
    received, (*outs, b_buf, a_buf, sums, high_ref, low_ref, b_sem, a_sem, in_sem, out_sem) = (
        refs[:adds], refs[adds:]
    )
    groups, cols, depth = high_ref.shape[1:]
    tile = a_buf.shape[2]
    height = groups * cols
    per_chunk = 2 if adds else PIECES
    side = lax.rem(place[2] + (0 if adds else 1), CORES)
    tiles = []
    at = 0
    for i, (h, start, count, outer_first) in enumerate(chunks):
        tiles.append((at, count // tile, h, start, outer_first, outs[i * per_chunk:(i + 1) * per_chunk]))
        at += count // tile

    def columns(n, start=0):
        return pl.ds(pl.multiple_of(start + n * tile, tile), tile)

    def load_b(g):
        return pltpu.make_async_copy(b_hbm.at[g, side], b_buf.at[g], b_sem.at[g])

    def load_a(at, n, h, start):
        return pltpu.make_async_copy(
            a_hbm.at[h, :, columns(n, start)], a_buf.at[at + n], a_sem.at[at + n]
        )

    def loads(at, n, h, start):
        part = height // PIECES
        return [pltpu.make_async_copy(
            received[(h - first) * PIECES + i].at[:, columns(n, start)],
            sums.at[at + n, pl.ds(i * part, part)], in_sem.at[at + n, i],
        ) for i in range(PIECES if adds else 0)]

    def stores(at, n, outer_first, out):
        copies = []
        part = height // len(out)
        pieces = groups if outer_first else len(out)
        for i in range(pieces):
            if outer_first:
                x, z = i // OUTER, i % OUTER
                to, row = divmod((z * inner + x) * cols, part)
            else:
                to, row = i, 0
            size = height // pieces
            copies.append(pltpu.make_async_copy(
                sums.at[at + n, pl.ds(i * size, size)],
                out[to].at[pl.ds(row, size), columns(n)], out_sem.at[at + n, i],
            ))
        return copies

    def live(n, h, start):
        return start + n * tile < rows_live[h]

    for g in range(groups):
        load_b(g).start()
    for at, count, h, start, _, _ in tiles:
        @pl.loop(0, count)
        def _(n):
            @pl.when(live(n, h, start))
            def _():
                load_a(at, n, h, start).start()
            for copy in loads(at, n, h, start):
                copy.start()

    @pl.loop(0, groups)
    def _(g):
        load_b(g).wait()
        put_split(g, limit, first, b_buf, high_ref, low_ref, (slot(g, place, inner),))

    for at, count, h, start, outer_first, out in tiles:
        @pl.loop(0, count)
        def _(n):
            for copy in loads(at, n, h, start):
                copy.wait()

            @pl.when(live(n, h, start))
            def _():
                load_a(at, n, h, start).wait()
                left = (r[h - first].reshape(height, depth) for r in (high_ref, low_ref))
                total = dot3(*left, a_buf.at[at + n])
                sums[at + n] = sums[at + n] + total if adds else total

            if not adds:
                @pl.when(jnp.logical_not(live(n, h, start)))
                def _():
                    sums[at + n] = jnp.zeros((height, tile), F32)

            for copy in stores(at, n, outer_first, out):
                copy.start()

    for at, count, _, _, outer_first, out in tiles:
        @pl.loop(0, count)
        def _(n):
            for copy in stores(at, n, outer_first, out):
                copy.wait()


def products(place, limit, rows_live, parts_of_b, amplitudes, chunks, inner, received):
    groups, _, cols, rows_b, _ = parts_of_b.shape
    blocks, depth, rows = amplitudes.shape
    tile = min(rows, TILE)
    first, last = chunks[0][0], chunks[-1][0]
    total = sum(chunk[2] for chunk in chunks) // tile
    height = groups * cols
    count = 2 if received else PIECES
    anywhere = pl.BlockSpec(memory_space=pl.ANY)
    part = pltpu.VMEM((last - first + 1, groups, cols, depth), BF16)
    return pl.pallas_call(
        functools.partial(products_kernel, first, inner, chunks, len(received)),
        grid_spec=pltpu.PrefetchScalarGridSpec(
            num_scalar_prefetch=3,
            grid=(),
            in_specs=[anywhere] * (2 + len(received)),
            out_specs=[anywhere] * (count * len(chunks)),
            scratch_shapes=[
                pltpu.VMEM((groups, cols, rows_b, LANES), F32),
                pltpu.VMEM((total, depth, tile), F32),
                pltpu.VMEM((total, height, tile), F32),
                part,
                part,
                pltpu.SemaphoreType.DMA((groups,)),
                pltpu.SemaphoreType.DMA((total,)),
                pltpu.SemaphoreType.DMA((total, PIECES)),
                pltpu.SemaphoreType.DMA((total, groups)),
            ],
        ),
        out_shape=[jax.ShapeDtypeStruct((height // count, chunk[2]), F32)
                   for chunk in chunks for _ in range(count)],
        cost_estimate=cost(),
        compiler_params=params(),
        name="second_halves" if received else "first_halves",
    )(place, limit, rows_live, parts_of_b, amplitudes, *received)


def place_kernel(side_ref, base, row_count, col_count, *refs):
    *parts, out_ref = refs
    side = side_ref[0]
    blocks = len(parts) // 2
    cols, rows = parts[0].shape
    col = base[0] + lax.broadcasted_iota(jnp.int32, (cols, rows), 0)
    row = base[1] + lax.broadcasted_iota(jnp.int32, (cols, rows), 1)
    for here in range(2):
        @pl.when(side == here)
        def _():
            order = parts[blocks:] + parts[:blocks] if here else parts
            kept = [
                jnp.where((col < col_count[h]) & (row < row_count[h]), part[...], F32(0.0))
                for h, part in enumerate(order)
            ]
            out_ref[...] = jnp.swapaxes(jnp.stack(kept), 0, 1)


def place_blocks(side, base, row_count, col_count, mine, other):
    cols, rows = mine[0].shape
    blocks = 2 * len(mine)
    vmem = pl.BlockSpec(memory_space=pltpu.VMEM)
    return pl.pallas_call(
        place_kernel,
        grid_spec=pltpu.PrefetchScalarGridSpec(
            num_scalar_prefetch=4, grid=(), in_specs=[vmem] * blocks, out_specs=vmem,
        ),
        out_shape=jax.ShapeDtypeStruct((cols, blocks, rows), F32),
        cost_estimate=cost(),
        compiler_params=params(),
        name="place_blocks",
    )(side, base, row_count, col_count, *mine, *other)


class Chain:
    def __init__(self):
        self.last = None

    def run(self, step, *args):
        if self.last is not None:
            args, _ = lax.optimization_barrier((args, self.last))
        result = step(*args)
        self.last = jax.tree.leaves(result)[0]
        return result


def local(inner, amplitudes, integrals, row_count, pair_count, col_count):
    blocks, depth, rows = amplitudes.shape
    all_cols = integrals.shape[0]
    tensor, rep = lax.axis_size("tensor"), lax.axis_size("rep")
    cols, row_local = all_cols // tensor, rows // rep
    me, side = lax.axis_index("tensor"), lax.axis_index("rep")
    z, x, core = me // (inner * CORES), me // CORES % inner, me % CORES
    place = jnp.stack([z, x, core]).astype(jnp.int32)

    pairs_here = lax.dynamic_slice_in_dim(pair_count, side * blocks, blocks) - me * depth
    rows_here = lax.dynamic_slice_in_dim(row_count, side * blocks, blocks)
    rows_here = jnp.where(pairs_here > 0, rows_here, 0)
    parts_of_b = integrals.reshape(all_cols, blocks, depth // LANES, LANES).transpose(0, 2, 1, 3)
    parts_of_b = parts_of_b.reshape(inner * OUTER, CORES, cols, blocks * depth // LANES, LANES)

    def index(z, x, core):
        return (z * inner + x) * CORES + core

    across = [(index(z, x, c), index(z, x, 1 - c))
              for z in range(OUTER) for x in range(inner) for c in range(CORES)]

    def along_inner(bit):
        return [(index(z, x, c), index(z, x ^ bit, c))
                for z in range(OUTER) for x in range(inner) for c in range(CORES)]

    def along_outer(bit):
        return [(index(z, x, c), index(z ^ bit, x, c))
                for z in range(OUTER) for x in range(inner) for c in range(CORES)]

    chain = Chain()
    received, totals, gens = {}, {}, {}

    def run_products(chunks, *got):
        return chain.run(
            lambda p, l, r, b, a, *g: products(p, l, r, b, a, chunks, inner, g),
            place, pairs_here, rows_here, parts_of_b, amplitudes, *got,
        )

    def first_halves(names):
        sent = run_products([(h, 0, rows, False) for h in names])
        for i, h in enumerate(names):
            received[h] = [lax.ppermute(part, "tensor", across)
                           for part in sent[i * PIECES:(i + 1) * PIECES]]

    def second_halves(names):
        got = [part for h in sorted({chunks[i][0] for i in names}) for part in received[h]]
        outs = run_products([chunks[i] for i in names], *got)
        for at, i in enumerate(names):
            gens[i] = work(*chunks[i], *outs[2 * at:2 * at + 2])

    def work(h, start, count, outer_first, keep, send):
        steps = [along_inner(1 << i) for i in range(inner.bit_length() - 1)]
        more = [along_outer(1 << i) for i in range(OUTER.bit_length() - 1)]
        for pairs in more + steps if outer_first else steps + more:
            got = lax.ppermute(send, "tensor", pairs)
            half = keep.shape[0] // 2
            if half < cols:
                totals[h, start] = chain.run(jnp.add, keep, got)
            else:
                keep, send = chain.run(
                    lambda a, b: (a[:half] + b[:half], a[half:] + b[half:]), keep, got
                )
            yield

    mine, other, arriving = {}, {}, []

    def exchange(group):
        if rep != 2:
            for h in group:
                mine[h] = totals[h, 0]
            return
        pairs = []
        for h in group:
            pairs.append([totals[at] for at in sorted(totals) if at[0] == h])

        def choose(parts):
            pairs = []
            for part in parts:
                if len(part) == 1 or part[0].shape[1] != row_local:
                    whole = jnp.concatenate(part, axis=1)
                    part = whole[:, :row_local], whole[:, row_local:]
                pairs.append(part)
            kept = [jnp.where(side == 0, a, b) for a, b in pairs]
            return kept, jnp.concatenate([jnp.where(side == 0, b, a) for a, b in pairs])

        kept, away = chain.run(choose, pairs)
        chain.last = away
        got = lax.ppermute(away, "rep", [(0, 1), (1, 0)])
        for i, h in enumerate(group):
            mine[h], other[h] = kept[i], got[i * cols:(i + 1) * cols]
        arriving.append(got)

    if inner == 2 and rep == 2 and blocks == 4:
        half = rows // 2
        chunks = [(0, 0, rows, False), (1, 0, rows, False), (2, 0, half, True),
                  (2, half, half, False), (3, 0, rows - TILE, False), (3, rows - TILE, TILE, False)]
        firsts = {"p": [0, 1], "q": [2, 3]}
        seconds = {"w": [0], "x": [1], "y": [2, 3], "z": [4, 5]}
        groups = {"a": [0, 1], "b": [2], "d": [3]}
        plan = "pwxq0yz012032141352a453Ab45Ad"
    else:
        chunks = [(h, 0, rows, False) for h in range(blocks)]
        firsts = {"p": list(range(blocks))}
        seconds = {"w": list(range(blocks))}
        groups = {"a": list(range(blocks))}
        steps = (inner * OUTER).bit_length() - 1
        plan = "pw" + "".join(str(h) * steps for h in range(blocks)) + "a"
    for move in plan:
        if move in firsts:
            first_halves(firsts[move])
        elif move in seconds:
            second_halves(seconds[move])
        elif move == "A":
            chain.last = chain.last, arriving[-1]
        elif move in groups:
            exchange(groups[move])
        else:
            next(gens[int(move)])

    if rep == 2:
        base = jnp.stack([me * cols, side * row_local]).astype(jnp.int32)
        return place_blocks(
            jnp.reshape(side, (1,)).astype(jnp.int32), base, row_count, col_count,
            [mine[h] for h in range(blocks)], [other[h] for h in range(blocks)],
        )
    arranged = lax.all_to_all(
        jnp.stack([mine[h] for h in range(blocks)], axis=1), "rep",
        split_axis=2, concat_axis=1, tiled=True,
    )
    col_index = me * cols + lax.broadcasted_iota(jnp.int32, (cols, 1, 1), 0)
    row_index = side * row_local + lax.broadcasted_iota(jnp.int32, (1, 1, row_local), 2)
    keep = (col_index < col_count[None, :, None]) & (row_index < row_count[None, :, None])
    return jnp.where(keep, arranged, F32(0.0))


def solution(mesh):
    inner = mesh.shape["tensor"] // (OUTER * CORES)
    in_specs = (P("rep", "tensor", None), P(None, "rep", "tensor"), P(), P(), P())
    out_specs = P("tensor", None, "rep")
    return jax.shard_map(
        functools.partial(local, inner), mesh=mesh, in_specs=in_specs, out_specs=out_specs,
        check_vma=False,
    )
```

```python
import functools

import jax
import jax.numpy as jnp
from jax import lax
from jax.experimental import pallas as pl
from jax.experimental.pallas import tpu as pltpu
from jax.sharding import PartitionSpec as P

OUTER = 4
CORES = 2
LANES = 128
TILE = 256
PIECES = 2
VMEM_BYTES = 44 * 1024 * 1024
F32 = jnp.float32
BF16 = jnp.bfloat16


def params():
    return pltpu.CompilerParams(vmem_limit_bytes=VMEM_BYTES)


def cost():
    return pl.CostEstimate(flops=1024, bytes_accessed=1024, transcendentals=0)


def split(value):
    high = value.astype(BF16)
    return high, (value - high.astype(F32)).astype(BF16)


def reversed_bits(value, count):
    result, bit = 0, 1
    while bit < count:
        result = 2 * result + (value // bit) % 2
        bit *= 2
    return result


def put_split(group, limit, first, b_ref, high_ref, low_ref, place):
    used = high_ref.shape[0]
    cols, depth = high_ref.shape[-2:]
    tiles = depth // LANES
    blocks = b_ref.shape[2] // tiles
    lane = lax.broadcasted_iota(jnp.int32, (1, LANES), 1)
    for h in range(used):
        rows = pl.ds(first + h, tiles, stride=blocks) if blocks > 1 else slice(None)
        turned = jnp.swapaxes(b_ref[group, :, rows, :], 0, 1)
        for t in range(tiles):
            value = jnp.where(lane < limit[first + h] - t * LANES, turned[t], F32(0.0))
            high, low = split(value)
            high_ref[(h, *place, slice(None), slice(t * LANES, (t + 1) * LANES))] = high
            low_ref[(h, *place, slice(None), slice(t * LANES, (t + 1) * LANES))] = low


def slot(group, place, inner):
    x = reversed_bits((group % inner) ^ place[1], inner)
    z = reversed_bits((group // inner) ^ place[0], OUTER)
    return x * OUTER + z


def dot3(left_high, left_low, a_ref):
    high, low = split(a_ref[...])
    dot = functools.partial(jnp.dot, preferred_element_type=F32)
    return dot(left_high, high) + (dot(left_high, low) + dot(left_low, high))


def products_kernel(first, inner, chunks, adds, place, limit, rows_live, b_hbm, a_hbm, *refs):
    received, (*outs, b_buf, a_buf, sums, high_ref, low_ref, b_sem, a_sem, in_sem, out_sem) = (
        refs[:adds], refs[adds:]
    )
    groups, cols, depth = high_ref.shape[1:]
    tile = a_buf.shape[2]
    height = groups * cols
    per_chunk = 2 if adds else PIECES
    side = lax.rem(place[2] + (0 if adds else 1), CORES)
    tiles = []
    at = 0
    for i, (h, start, count, outer_first) in enumerate(chunks):
        tiles.append((at, count // tile, h, start, outer_first, outs[i * per_chunk:(i + 1) * per_chunk]))
        at += count // tile

    def columns(n, start=0):
        return pl.ds(pl.multiple_of(start + n * tile, tile), tile)

    def load_b(g):
        return pltpu.make_async_copy(b_hbm.at[g, side], b_buf.at[g], b_sem.at[g])

    def load_a(at, n, h, start):
        return pltpu.make_async_copy(
            a_hbm.at[h, :, columns(n, start)], a_buf.at[at + n], a_sem.at[at + n]
        )

    def loads(at, n, h, start):
        part = height // PIECES
        return [pltpu.make_async_copy(
            received[(h - first) * PIECES + i].at[:, columns(n, start)],
            sums.at[at + n, pl.ds(i * part, part)], in_sem.at[at + n, i],
        ) for i in range(PIECES if adds else 0)]

    def stores(at, n, outer_first, out):
        copies = []
        part = height // len(out)
        pieces = groups if outer_first else len(out)
        for i in range(pieces):
            if outer_first:
                x, z = i // OUTER, i % OUTER
                to, row = divmod((z * inner + x) * cols, part)
            else:
                to, row = i, 0
            size = height // pieces
            copies.append(pltpu.make_async_copy(
                sums.at[at + n, pl.ds(i * size, size)],
                out[to].at[pl.ds(row, size), columns(n)], out_sem.at[at + n, i],
            ))
        return copies

    def live(n, h, start):
        return start + n * tile < rows_live[h]

    for g in range(groups):
        load_b(g).start()
    for at, count, h, start, _, _ in tiles:
        @pl.loop(0, count)
        def _(n):
            @pl.when(live(n, h, start))
            def _():
                load_a(at, n, h, start).start()
            for copy in loads(at, n, h, start):
                copy.start()

    @pl.loop(0, groups)
    def _(g):
        load_b(g).wait()
        put_split(g, limit, first, b_buf, high_ref, low_ref, (slot(g, place, inner),))

    for at, count, h, start, outer_first, out in tiles:
        @pl.loop(0, count)
        def _(n):
            for copy in loads(at, n, h, start):
                copy.wait()

            @pl.when(live(n, h, start))
            def _():
                load_a(at, n, h, start).wait()
                left = (r[h - first].reshape(height, depth) for r in (high_ref, low_ref))
                total = dot3(*left, a_buf.at[at + n])
                sums[at + n] = sums[at + n] + total if adds else total

            if not adds:
                @pl.when(jnp.logical_not(live(n, h, start)))
                def _():
                    sums[at + n] = jnp.zeros((height, tile), F32)

            for copy in stores(at, n, outer_first, out):
                copy.start()

    for at, count, _, _, outer_first, out in tiles:
        @pl.loop(0, count)
        def _(n):
            for copy in stores(at, n, outer_first, out):
                copy.wait()


def products(place, limit, rows_live, parts_of_b, amplitudes, chunks, inner, received):
    groups, _, cols, rows_b, _ = parts_of_b.shape
    blocks, depth, rows = amplitudes.shape
    tile = min(rows, TILE)
    first, last = chunks[0][0], chunks[-1][0]
    total = sum(chunk[2] for chunk in chunks) // tile
    height = groups * cols
    count = 2 if received else PIECES
    anywhere = pl.BlockSpec(memory_space=pl.ANY)
    part = pltpu.VMEM((last - first + 1, groups, cols, depth), BF16)
    return pl.pallas_call(
        functools.partial(products_kernel, first, inner, chunks, len(received)),
        grid_spec=pltpu.PrefetchScalarGridSpec(
            num_scalar_prefetch=3,
            grid=(),
            in_specs=[anywhere] * (2 + len(received)),
            out_specs=[anywhere] * (count * len(chunks)),
            scratch_shapes=[
                pltpu.VMEM((groups, cols, rows_b, LANES), F32),
                pltpu.VMEM((total, depth, tile), F32),
                pltpu.VMEM((total, height, tile), F32),
                part,
                part,
                pltpu.SemaphoreType.DMA((groups,)),
                pltpu.SemaphoreType.DMA((total,)),
                pltpu.SemaphoreType.DMA((total, PIECES)),
                pltpu.SemaphoreType.DMA((total, groups)),
            ],
        ),
        out_shape=[jax.ShapeDtypeStruct((height // count, chunk[2]), F32)
                   for chunk in chunks for _ in range(count)],
        cost_estimate=cost(),
        compiler_params=params(),
        name="second_halves" if received else "first_halves",
    )(place, limit, rows_live, parts_of_b, amplitudes, *received)


def place_kernel(side_ref, base, row_count, col_count, *refs):
    *parts, out_ref = refs
    side = side_ref[0]
    blocks = len(parts) // 2
    cols, rows = parts[0].shape
    col = base[0] + lax.broadcasted_iota(jnp.int32, (cols, rows), 0)
    row = base[1] + lax.broadcasted_iota(jnp.int32, (cols, rows), 1)
    for here in range(2):
        @pl.when(side == here)
        def _():
            order = parts[blocks:] + parts[:blocks] if here else parts
            kept = [
                jnp.where((col < col_count[h]) & (row < row_count[h]), part[...], F32(0.0))
                for h, part in enumerate(order)
            ]
            out_ref[...] = jnp.swapaxes(jnp.stack(kept), 0, 1)


def place_blocks(side, base, row_count, col_count, mine, other):
    cols, rows = mine[0].shape
    blocks = 2 * len(mine)
    vmem = pl.BlockSpec(memory_space=pltpu.VMEM)
    return pl.pallas_call(
        place_kernel,
        grid_spec=pltpu.PrefetchScalarGridSpec(
            num_scalar_prefetch=4, grid=(), in_specs=[vmem] * blocks, out_specs=vmem,
        ),
        out_shape=jax.ShapeDtypeStruct((cols, blocks, rows), F32),
        cost_estimate=cost(),
        compiler_params=params(),
        name="place_blocks",
    )(side, base, row_count, col_count, *mine, *other)


class Chain:
    def __init__(self):
        self.last = None

    def run(self, step, *args):
        if self.last is not None:
            args, _ = lax.optimization_barrier((args, self.last))
        result = step(*args)
        self.last = jax.tree.leaves(result)[0]
        return result


def local(inner, amplitudes, integrals, row_count, pair_count, col_count):
    blocks, depth, rows = amplitudes.shape
    all_cols = integrals.shape[0]
    tensor, rep = lax.axis_size("tensor"), lax.axis_size("rep")
    cols, row_local = all_cols // tensor, rows // rep
    me, side = lax.axis_index("tensor"), lax.axis_index("rep")
    z, x, core = me // (inner * CORES), me // CORES % inner, me % CORES
    place = jnp.stack([z, x, core]).astype(jnp.int32)

    pairs_here = lax.dynamic_slice_in_dim(pair_count, side * blocks, blocks) - me * depth
    rows_here = lax.dynamic_slice_in_dim(row_count, side * blocks, blocks)
    rows_here = jnp.where(pairs_here > 0, rows_here, 0)
    parts_of_b = integrals.reshape(all_cols, blocks, depth // LANES, LANES).transpose(0, 2, 1, 3)
    parts_of_b = parts_of_b.reshape(inner * OUTER, CORES, cols, blocks * depth // LANES, LANES)

    def index(z, x, core):
        return (z * inner + x) * CORES + core

    across = [(index(z, x, c), index(z, x, 1 - c))
              for z in range(OUTER) for x in range(inner) for c in range(CORES)]

    def along_inner(bit):
        return [(index(z, x, c), index(z, x ^ bit, c))
                for z in range(OUTER) for x in range(inner) for c in range(CORES)]

    def along_outer(bit):
        return [(index(z, x, c), index(z ^ bit, x, c))
                for z in range(OUTER) for x in range(inner) for c in range(CORES)]

    chain = Chain()
    received, totals, gens = {}, {}, {}

    def run_products(chunks, *got):
        return chain.run(
            lambda p, l, r, b, a, *g: products(p, l, r, b, a, chunks, inner, g),
            place, pairs_here, rows_here, parts_of_b, amplitudes, *got,
        )

    def first_halves(names):
        sent = run_products([(h, 0, rows, False) for h in names])
        for i, h in enumerate(names):
            received[h] = [lax.ppermute(part, "tensor", across)
                           for part in sent[i * PIECES:(i + 1) * PIECES]]

    def second_halves(names):
        got = [part for h in sorted({chunks[i][0] for i in names}) for part in received[h]]
        outs = run_products([chunks[i] for i in names], *got)
        for at, i in enumerate(names):
            gens[i] = work(*chunks[i], *outs[2 * at:2 * at + 2])

    def work(h, start, count, outer_first, keep, send):
        steps = [along_inner(1 << i) for i in range(inner.bit_length() - 1)]
        more = [along_outer(1 << i) for i in range(OUTER.bit_length() - 1)]
        for pairs in more + steps if outer_first else steps + more:
            got = lax.ppermute(send, "tensor", pairs)
            half = keep.shape[0] // 2
            if half < cols:
                totals[h, start] = chain.run(jnp.add, keep, got)
            else:
                keep, send = chain.run(
                    lambda a, b: (a[:half] + b[:half], a[half:] + b[half:]), keep, got
                )
            yield

    mine, other, arriving = {}, {}, []

    def exchange(group):
        if rep != 2:
            for h in group:
                mine[h] = totals[h, 0]
            return
        pairs = []
        for h in group:
            pairs.append([totals[at] for at in sorted(totals) if at[0] == h])

        def choose(parts):
            pairs = []
            for part in parts:
                if len(part) == 1 or part[0].shape[1] != row_local:
                    whole = jnp.concatenate(part, axis=1)
                    part = whole[:, :row_local], whole[:, row_local:]
                pairs.append(part)
            kept = [jnp.where(side == 0, a, b) for a, b in pairs]
            return kept, jnp.concatenate([jnp.where(side == 0, b, a) for a, b in pairs])

        kept, away = chain.run(choose, pairs)
        chain.last = away
        got = lax.ppermute(away, "rep", [(0, 1), (1, 0)])
        for i, h in enumerate(group):
            mine[h], other[h] = kept[i], got[i * cols:(i + 1) * cols]
        arriving.append(got)

    if inner == 2 and rep == 2 and blocks == 4:
        half = rows // 2
        chunks = [(0, 0, rows, False), (1, 0, rows, False), (2, 0, TILE, True),
                  (2, TILE, rows - TILE, False), (3, 0, half, False), (3, half, half, False)]
        firsts = {"p": [0, 1], "q": [2, 3]}
        seconds = {"w": [0], "x": [1], "y": [2, 3], "z": [4, 5]}
        groups = {"a": [0, 1], "b": [2], "d": [3]}
        plan = "pwxq0yz012032141352a453Ab45Ad"
    else:
        chunks = [(h, 0, rows, False) for h in range(blocks)]
        firsts = {"p": list(range(blocks))}
        seconds = {"w": list(range(blocks))}
        groups = {"a": list(range(blocks))}
        steps = (inner * OUTER).bit_length() - 1
        plan = "pw" + "".join(str(h) * steps for h in range(blocks)) + "a"
    for move in plan:
        if move in firsts:
            first_halves(firsts[move])
        elif move in seconds:
            second_halves(seconds[move])
        elif move == "A":
            chain.last = chain.last, arriving[-1]
        elif move in groups:
            exchange(groups[move])
        else:
            next(gens[int(move)])

    if rep == 2:
        base = jnp.stack([me * cols, side * row_local]).astype(jnp.int32)
        return place_blocks(
            jnp.reshape(side, (1,)).astype(jnp.int32), base, row_count, col_count,
            [mine[h] for h in range(blocks)], [other[h] for h in range(blocks)],
        )
    arranged = lax.all_to_all(
        jnp.stack([mine[h] for h in range(blocks)], axis=1), "rep",
        split_axis=2, concat_axis=1, tiled=True,
    )
    col_index = me * cols + lax.broadcasted_iota(jnp.int32, (cols, 1, 1), 0)
    row_index = side * row_local + lax.broadcasted_iota(jnp.int32, (1, 1, row_local), 2)
    keep = (col_index < col_count[None, :, None]) & (row_index < row_count[None, :, None])
    return jnp.where(keep, arranged, F32(0.0))


def solution(mesh):
    inner = mesh.shape["tensor"] // (OUTER * CORES)
    in_specs = (P("rep", "tensor", None), P(None, "rep", "tensor"), P(), P(), P())
    out_specs = P("tensor", None, "rep")
    return jax.shard_map(
        functools.partial(local, inner), mesh=mesh, in_specs=in_specs, out_specs=out_specs,
        check_vma=False,
    )
```
